32 devices in a mesh: dp: 8 (over z, x), mp: 4 (over y, core).
Axes of the slice: x: 2, y: 2, z: 4, core: 2. Of those that a mesh axis runs over, the one named last changes fastest.
Arguments:
- doc_tokens: bfloat16 [12288, 768], P('dp'), may hold values from -6 to 6
- query_tokens: bfloat16 [2048, 768], P('dp'), may hold values from -6 to 6
- w_query: bfloat16 [768, 768], P(None, 'mp'), may hold values from -0.02734375 to 0.02734375
- w_key: bfloat16 [768, 768], P(None, 'mp'), may hold values from -0.21875 to 0.21875
- w_value: bfloat16 [768, 768], P(None, 'mp'), may hold values from -0.21875 to 0.21875
- w_out: bfloat16 [768, 768], P('mp'), may hold values from -2 to 2
- w_gate: bfloat16 [768, 2048], P(None, 'mp'), may hold values from -0.21875 to 0.21875
- w_up: bfloat16 [768, 2048], P(None, 'mp'), may hold values from -0.21875 to 0.21875
- w_down: bfloat16 [2048, 768], P('mp'), may hold values from -0.125 to 0.125
- w_proj: bfloat16 [768, 128], replicated, may hold values from -0.21875 to 0.21875
- gain_attn: float32 [768], replicated, may hold values from 0.5 to 1.5
- gain_ffn: float32 [768], replicated, may hold values from 0.5 to 1.5
- gain_final: float32 [768], replicated, may hold values from 0.5 to 1.5
- bias_table: float32 [32, 12], P(None, 'mp'), may hold values from -4 to 4
- query_mask: int32 [64, 32], replicated, may hold values from 0 to 1, as said below
- retrieval_mask: int32 [64, 32, 24], P(None, None, 'dp'), may hold values 0 or 1
- positives: int32 [64], replicated, may hold values from 0 to 23
Outputs:
- mean_loss: float32 [], replicated
- retrieved_share: float32 [], replicated
- doc_embed: bfloat16 [12288, 128], P('dp')
- doc_tokens_grad: bfloat16 [12288, 768], P('dp')
- query_tokens_grad: bfloat16 [2048, 768], P('dp')
- grad_query: float32 [768, 768], P(None, 'mp')
- grad_key: float32 [768, 768], P(None, 'mp')
- grad_value: float32 [768, 768], P(None, 'mp')
- grad_out: float32 [768, 768], P('mp')
- grad_gate: float32 [768, 2048], P(None, 'mp')
- grad_up: float32 [768, 2048], P(None, 'mp')
- grad_down: float32 [2048, 768], P('mp')
- grad_proj: float32 [768, 128], replicated
- grad_gain_attn: float32 [768], replicated
- grad_gain_ffn: float32 [768], replicated
- grad_gain_final: float32 [768], replicated
- grad_bias: float32 [32, 12], P(None, 'mp')
The draws below stay inside these ranges and needn't reach their ends.
Inputs may be any that keep to these rules, and one draw needn't show every extreme that they name: `query_mask`: each row holds its ones first: between 8 and 32 real tokens of a query; some query has 32 and some has 8.
All inputs are finite; a program needn't handle non-finite values. No bound on the sum of `retrieval_mask` on one device may be relied on, other than what follows from the above.
Results may differ from the reference program's by a relative error of at most 0.0329.
Values may be sent and summed in bfloat16 or wider, within the bound.
No kernel may reach another device: no remote copies, remote signals or barrier semaphores. Data moves between devices by JAX's collectives and lax.ppermute only.
A program may use at most 192 MiB of HBM per device.

```python
import math
import jax
import jax.numpy as jnp
from jax import lax

D = 768
HEADS = 12
DH = 64
FF = 2048
E = 128
BUCKETS = 32
DOC_LEN = 512
QLEN = 32
DOCS = 24
QUERIES = 64
N_MP = 4


def draw_query_mask(key, part):
    key = jax.random.fold_in(key, 11)
    counts = jax.random.randint(key, (QUERIES,), 8, QLEN + 1)
    counts = counts.at[0].set(QLEN).at[1].set(8)
    position = jnp.arange(QLEN, dtype=jnp.int32)
    return (position[None, :] < counts[:, None]).astype(jnp.int32)


def plant(result, own_key, smallest, largest):
    place = [jax.random.randint(jax.random.fold_in(own_key, axis), (), 0, length) for axis, length in enumerate(result.shape)]
    longest = result.shape.index(max(result.shape))
    beside = place[:longest] + [(place[longest] + 1) % result.shape[longest]] + place[longest + 1:]
    return result.at[tuple(place)].set(smallest).at[tuple(beside)].set(largest)


def level_of(rng, extent, shards, smallest, largest):
    gain, own = 1.0, jax.random.fold_in(rng, 6)
    for axis_at, parts in shards:
        steps = jnp.exp(jax.random.uniform(jax.random.fold_in(own, axis_at), (parts,), jnp.float32, smallest / len(shards), largest / len(shards)))
        gain = gain * jnp.repeat(steps, extent[axis_at] // parts).reshape([-1 if axis == axis_at else 1 for axis in range(len(extent))])
    return gain


def centred(key, dims, scale, most, shards=(), held_as=jnp.bfloat16):
    gain = level_of(key, dims, shards, -0.22, 0.18) if shards else 1.0
    drawn = jax.random.normal(key, dims, jnp.float32) * scale * gain
    return jnp.minimum(jnp.maximum(drawn, -most), most).astype(held_as)


def setup_inputs(seed: int = 0) -> dict:
    key_of = jax.random.split(jax.random.key(seed), 18)
    doc_tokens = centred(key_of[0], (DOCS * DOC_LEN, D), 1.0, 6.0, ((0, 8),))
    query_tokens = centred(key_of[1], (QUERIES * QLEN, D), 1.0, 6.0, ((0, 8),))
    w_query = centred(key_of[2], (D, D), (D * DH) ** -0.5, 0.02734375, ((1, 4),))
    w_key = centred(key_of[3], (D, D), D ** -0.5, 0.21875, ((1, 4),))
    w_value = centred(key_of[4], (D, D), D ** -0.5, 0.21875, ((1, 4),))
    w_out = centred(key_of[5], (D, D), 8 ** -0.5, 2.0, ((0, 4),))
    w_gate = centred(key_of[6], (D, FF), D ** -0.5, 0.21875, ((1, 4),))
    w_up = centred(key_of[7], (D, FF), D ** -0.5, 0.21875, ((1, 4),))
    w_down = centred(key_of[8], (FF, D), FF ** -0.5, 0.125, ((0, 4),))
    w_proj = centred(key_of[9], (D, E), D ** -0.5, 0.21875)
    gain_attn = jnp.clip(1.0 + 0.1 * jax.random.normal(key_of[10], (D,), jnp.float32), 0.5, 1.5)
    gain_ffn = jnp.clip(1.0 + 0.1 * jax.random.normal(key_of[11], (D,), jnp.float32), 0.5, 1.5)
    gain_final = jnp.clip(1.0 + 0.1 * jax.random.normal(key_of[12], (D,), jnp.float32), 0.5, 1.5)
    bias_table = centred(key_of[13], (BUCKETS, HEADS), 1.0, 4.0, ((1, 4),), jnp.float32)
    query_mask = draw_query_mask(jax.random.fold_in(key_of[17], 71), 0)
    retrieval_mask = plant((jax.random.randint(key_of[15], (QUERIES, QLEN, DOCS), 0, 4) < 1).astype(jnp.int32), jax.random.fold_in(key_of[15], 1), 0, 1)
    positives = plant(jax.random.randint(key_of[16], (QUERIES,), 0, DOCS), jax.random.fold_in(key_of[16], 1), 0, DOCS - 1).astype(jnp.int32)
    return {"doc_tokens": doc_tokens, "query_tokens": query_tokens, "w_query": w_query, "w_key": w_key, "w_value": w_value, "w_out": w_out, "w_gate": w_gate, "w_up": w_up, "w_down": w_down, "w_proj": w_proj, "gain_attn": gain_attn, "gain_ffn": gain_ffn, "gain_final": gain_final, "bias_table": bias_table, "query_mask": query_mask, "retrieval_mask": retrieval_mask, "positives": positives}


@jax.custom_vjp
def low(v):
    return lax.optimization_barrier(v.astype(jnp.bfloat16)).astype(jnp.float32)

@jax.custom_vjp
def lowered_backward(v):
    return v

def low_keep(v):
    return (low(v), None)

def low_pass(kept, grad):
    return (grad,)

def back_keep(v):
    return (v, None)

def back_low(kept, grad):
    return (low(grad),)
low.defvjp(low_keep, low_pass)
lowered_backward.defvjp(back_keep, back_low)
epsilon = 1e-06
doc_temp = 32.0
bucket_edges = (12, 16, 23, 32, 46, 64, 91)
greatest_value = lax.Precision.HIGHEST

def both_ways(value):
    return lowered_backward(low(value))

def bucket_index(length):
    position = jnp.arange(length, dtype=jnp.int32)
    offset = position[None, :] - position[:, None]
    distance = jnp.abs(offset)
    far_bucket = 8 + sum(((distance >= edge).astype(jnp.int32) for edge in bucket_edges))
    return jnp.where(distance < 8, distance, far_bucket) + 16 * (offset > 0).astype(jnp.int32)

def rms_scale(value_entries, gain_vector):
    return value_entries * lax.rsqrt(lax.optimization_barrier(jnp.mean(value_entries * value_entries, axis=-1, keepdims=True)) + epsilon) * gain_vector

def project(value_entries, weight_matrix):
    return jnp.einsum('xvn,np->xvp', value_entries, weight_matrix, precision=greatest_value)

def encode(tokens, key_mask, weights):
    w_query, w_key, w_value, w_out, w_gate, w_up, w_down, w_proj, gain_attn, gain_ffn, gain_final, bias_table = weights
    seq_count, length, model_width = tokens.shape
    position_bias = jnp.transpose(bias_table[bucket_index(length)], (2, 0, 1))
    head_group = HEADS // N_MP
    head_cols = head_group * DH
    unit_group = FF // N_MP
    normed = low(rms_scale(tokens, gain_attn))
    attended = jnp.zeros_like(tokens)
    for group_number in range(N_MP):
        group_input = lowered_backward(normed)
        head_slice = slice(group_number * head_cols, (group_number + 1) * head_cols)

        def heads_of(weight_matrix):
            return both_ways(project(group_input, weight_matrix[:, head_slice])).reshape(seq_count, length, head_group, DH)
        query_heads = heads_of(w_query)
        key_heads = heads_of(w_key)
        value_heads = heads_of(w_value)
        logits = jnp.einsum('slhe,smhe->shlm', query_heads, key_heads, precision=greatest_value)
        group_bias = position_bias[group_number * head_group:(group_number + 1) * head_group]
        logits = lowered_backward(logits + group_bias[None])
        logits = jnp.where(key_mask[:, None, None, :], logits, -1000000000.0)
        probabilities = low(jax.nn.softmax(logits, axis=-1))
        context = jnp.einsum('shlm,smhe->slhe', probabilities, value_heads, precision=greatest_value)
        context = both_ways(context.reshape(seq_count, length, head_cols))
        attended = attended + low(project(context, w_out[head_slice, :]))
    middle = tokens + lowered_backward(attended)
    normed_ffn = low(rms_scale(middle, gain_ffn))
    feedforward = jnp.zeros_like(tokens)
    for group_number in range(N_MP):
        group_input = lowered_backward(normed_ffn)
        unit_slice = slice(group_number * unit_group, (group_number + 1) * unit_group)
        gate_value = lowered_backward(project(group_input, w_gate[:, unit_slice]))
        up_value = lowered_backward(project(group_input, w_up[:, unit_slice]))
        hidden = low(jax.nn.gelu(gate_value, approximate=True) * up_value)
        feedforward = feedforward + low(project(hidden, w_down[unit_slice, :]))
    output = middle + lowered_backward(feedforward)
    return both_ways(project(low(rms_scale(output, gain_final)), w_proj))

def doc_scores(query_emb, doc_emb, token_weights):
    scores = jnp.einsum('qie,dje->qidj', query_emb, doc_emb, precision=greatest_value)
    scores = lowered_backward(scores * query_emb.shape[-1] ** (-0.5))
    token_scores = jax.nn.logsumexp(scores, axis=-1) - math.log(doc_emb.shape[1])
    return lax.optimization_barrier(jnp.sum(token_weights * token_scores, axis=1))

def forward(doc_tokens, query_tokens, weights, query_keep, token_weights, positive_hot):
    query_count = query_keep.shape[0]
    query_group = math.gcd(query_count, max(1, 4096 // QLEN))
    doc_group = math.gcd(DOCS, max(1, 4096 // DOC_LEN))

    def query_encode(blocks):
        return encode(blocks[0], blocks[1], weights)
    query_emb = lax.map(jax.checkpoint(query_encode), (query_tokens.reshape(query_count // query_group, query_group, QLEN, D), query_keep.reshape(query_count // query_group, query_group, QLEN)))
    query_emb = query_emb.reshape(query_count, QLEN, E)
    full_keys = jnp.ones((doc_group, DOC_LEN), dtype=bool)

    def doc_block(blocks):
        doc_emb = encode(blocks[0], full_keys, weights)
        return (doc_emb, doc_scores(query_emb, doc_emb, blocks[1]))
    weight_blocks = jnp.moveaxis(token_weights.reshape(query_count, QLEN, DOCS // doc_group, doc_group), 2, 0)
    doc_emb, score_blocks = lax.map(jax.checkpoint(doc_block), (doc_tokens.reshape(DOCS // doc_group, doc_group, DOC_LEN, D), weight_blocks))
    doc_table = jnp.moveaxis(score_blocks, 0, 1).reshape(query_count, DOCS) * doc_temp
    losses = jax.nn.logsumexp(doc_table, axis=-1) - lax.optimization_barrier(jnp.sum(doc_table * positive_hot, axis=-1))
    return (jnp.mean(losses), doc_emb.reshape(DOCS * DOC_LEN, E))

def reference(doc_tokens, query_tokens, w_query, w_key, w_value, w_out, w_gate, w_up, w_down, w_proj, gain_attn, gain_ffn, gain_final, bias_table, query_mask, retrieval_mask, positives):
    weights = tuple((weight_arg.astype(jnp.float32) for weight_arg in (w_query, w_key, w_value, w_out, w_gate, w_up, w_down, w_proj, gain_attn, gain_ffn, gain_final, bias_table)))
    query_keep = query_mask > 0
    keep_float = query_mask.astype(jnp.float32)
    token_weights = keep_float[:, :, None] * retrieval_mask.astype(jnp.float32) / lax.optimization_barrier(jnp.sum(keep_float, axis=1))[:, None, None]
    positive_hot = (positives[:, None] == jnp.arange(DOCS, dtype=jnp.int32)[None, :]).astype(jnp.float32)
    share = jnp.mean(lax.optimization_barrier(jnp.sum(lax.optimization_barrier(jnp.sum(token_weights, axis=1)) * positive_hot, axis=-1)))

    def forward_pass(doc_input, query_input, weight_set):
        return forward(doc_input, query_input, weight_set, query_keep, token_weights, positive_hot)
    loss_value, backward, doc_embed = jax.vjp(forward_pass, doc_tokens.astype(jnp.float32), query_tokens.astype(jnp.float32), weights, has_aux=True)
    doc_grad, query_grad, weight_grads = backward(jnp.ones_like(loss_value))
    return (loss_value, share, doc_embed.astype(jnp.bfloat16), doc_grad.astype(jnp.bfloat16), query_grad.astype(jnp.bfloat16), weight_grads[0], weight_grads[1], weight_grads[2], weight_grads[3], weight_grads[4], weight_grads[5], weight_grads[6], weight_grads[7], weight_grads[8], weight_grads[9], weight_grads[10], weight_grads[11])
```

```python
import functools
import math

import jax
import jax.numpy as jnp
from jax import lax
from jax.experimental import pallas as pl
from jax.experimental.pallas import tpu as pltpu
from jax.sharding import PartitionSpec as P

DOC_LEN = 512
EPS = 1e-06
DOC_TEMP = 32.0
EDGES = (12, 16, 23, 32, 46, 64, 91)
HIGH = lax.Precision.HIGHEST
MASKED = -1000000000.0
BF = jnp.bfloat16
F32 = jnp.float32
WIDE = 2 * DOC_LEN
GELU_A = math.sqrt(2.0 / math.pi)
GELU_B = 0.044715


def nn(a, b):
    return jnp.dot(a, b, preferred_element_type=F32)


def nt(a, b):
    return lax.dot_general(a, b, (((1,), (1,)), ((), ())), preferred_element_type=F32)


def tn(a, b):
    return lax.dot_general(a, b, (((0,), (0,)), ((), ())), preferred_element_type=F32)


def rinv(v):
    return lax.rsqrt(jnp.mean(v * v, axis=-1, keepdims=True) + EPS)


def norm_back(v, r, gain, grad):
    scaled = grad * gain
    return r * scaled - v * (r * r * r * jnp.mean(scaled * v, axis=-1, keepdims=True))


def rowsum8(v):
    return jnp.broadcast_to(jnp.sum(v, axis=0, keepdims=True), (8, v.shape[1]))


def halves(place, half):
    mine = pl.multiple_of(place[1] * half, half)
    other = pl.multiple_of((1 - place[1]) * half, half)
    return (mine, other)


def vmem(shape=None, at=None):
    if shape is None:
        return pl.BlockSpec(memory_space=pltpu.VMEM)
    return pl.BlockSpec(shape, lambda i: at)


SMEM = pl.BlockSpec(memory_space=pltpu.SMEM)
ANYWHERE = pl.BlockSpec(memory_space=pl.ANY)


def call(body, name, out_shape, in_specs, out_specs, flops, bytes_moved, scratch=(), aliases=None):
    return pl.pallas_call(
        body,
        name=name,
        grid=(1,),
        out_shape=out_shape,
        in_specs=in_specs,
        out_specs=out_specs,
        scratch_shapes=list(scratch),
        input_output_aliases=aliases or {},
        compiler_params=pltpu.CompilerParams(vmem_limit_bytes=48 * 1024 * 1024),
        cost_estimate=pl.CostEstimate(flops=flops, bytes_accessed=bytes_moved, transcendentals=0),
    )


def sds(shape, dtype):
    return jax.ShapeDtypeStruct(shape, dtype)


def bias_body(table, out):
    lane = lax.broadcasted_iota(jnp.int32, (8, WIDE), 1)
    offset = jnp.where(lane < DOC_LEN, -lane, WIDE - lane)
    distance = jnp.abs(offset)
    far = jnp.full_like(distance, 8)
    for edge in EDGES:
        far = far + (distance >= edge).astype(jnp.int32)
    index = jnp.where(distance < 8, distance, far) + jnp.where(offset > 0, 16, 0)
    for head in range(out.shape[0]):
        row = jnp.zeros((8, WIDE), F32)
        for bucket in range(table.shape[0]):
            row = jnp.where(index == bucket, table[bucket, head], row)
        spread = jnp.broadcast_to(row[:1], (DOC_LEN, WIDE))
        rolled = pltpu.roll(spread, 0, 1, stride=1, stride_axis=0)
        out[head] = rolled[:, :DOC_LEN]


def make_bias(table):
    heads = table.shape[1]
    return call(
        bias_body,
        "rel_bias",
        sds((heads, DOC_LEN, DOC_LEN), F32),
        [SMEM],
        vmem(),
        10_000_000,
        3_000_000,
    )(table)


def attn_fwd_body(length, masked, heads, *refs):
    place, x, gain, wq, wk, wv, wo, bias = refs[:8]
    pos = 8
    keep_col = None
    if masked:
        keep_col = refs[8]
        pos = 9
    normed_o, q_o, k_o, v_o, lse_o, ctx_o, keep_o, send_o, part_s = refs[pos:]
    half = length // 2
    xf = x[...].astype(F32)
    normed = (xf * rinv(xf) * gain[...]).astype(BF)
    normed_o[...] = normed
    q = nn(normed, wq[...]).astype(BF)
    k = nn(normed, wk[...]).astype(BF)
    v = nn(normed, wv[...]).astype(BF)
    q_o[...] = q
    k_o[...] = k
    v_o[...] = v
    width = q.shape[1] // heads
    vt = v.T
    tile = min(length, 256)
    lse_o[...] = jnp.zeros_like(lse_o)
    for h in range(heads):
        cols = slice(h * width, (h + 1) * width)
        for start in range(0, length, tile):
            span = slice(start, start + tile)
            logits = nt(k[:, cols], q[span, cols]) + bias[h, :length, span]
            if masked:
                logits = jnp.where(query_mask_of(keep_col, length), logits, MASKED)
            top = jnp.max(logits, axis=0, keepdims=True)
            shifted = jnp.exp(logits - top)
            total = jnp.sum(shifted, axis=0, keepdims=True)
            probs = (shifted * (1.0 / total)).astype(BF)
            ctx_t = nn(vt[cols], probs)
            ctx_o[span, cols] = ctx_t.T.astype(BF)
            lse_o[h : h + 1, span] = top + jnp.log(total)
    part_s[...] = nn(ctx_o[...], wo[...]).astype(BF)
    mine, other = halves(place, half)
    keep_o[...] = part_s[pl.ds(mine, half)]
    send_o[...] = part_s[pl.ds(other, half)]


def query_mask_of(keep_col, length):
    key_row = lax.broadcasted_iota(jnp.int32, (length, length), 0)
    query_row = lax.broadcasted_iota(jnp.int32, (length, length), 1)
    return ((key_row // 32) == (query_row // 32)) & (keep_col[...] > 0)


def attn_fwd(chunk, place, tokens, gain, wq, wk, wv, wo, bias, keep_col):
    index, length, masked = chunk
    heads = bias.shape[0]
    cols = wq.shape[1]
    width = tokens.shape[1]
    specs = [SMEM, vmem((length, width), (index, 0))] + [vmem()] * 6
    operands = [place, tokens, gain, wq, wk, wv, wo, bias]
    if masked:
        specs.append(vmem())
        operands.append(keep_col)
    small = sds((length, cols), BF)
    part = sds((length // 2, width), BF)
    return call(
        functools.partial(attn_fwd_body, length, masked, heads),
        "attn_fwd",
        (sds((length, width), BF), small, small, small, sds((8, length), F32), small, part, part),
        specs,
        (vmem(),) * 8,
        4_000_000 * length,
        8_000 * length,
        [pltpu.VMEM((length, width), BF)],
    )(*operands)


def gelu_parts(gate):
    t = jnp.tanh(GELU_A * (gate + GELU_B * gate * gate * gate))
    return 0.5 * gate * (1.0 + t), t


def ffn_fwd_body(length, place, x, um, uo, gain, wg, wu, wd, normed_o, keep_o, send_o):
    half = length // 2
    bases = halves(place, half)
    for n, (u, out) in enumerate(((um, keep_o), (uo, send_o))):
        middle = x[pl.ds(bases[n], half)].astype(F32) + u[...].astype(F32)
        normed = (middle * rinv(middle) * gain[...]).astype(BF)
        normed_o[n * half : (n + 1) * half] = normed
        act, _ = gelu_parts(nn(normed, wg[...]))
        hidden = (act * nn(normed, wu[...])).astype(BF)
        out[...] = nn(hidden, wd[...]).astype(BF)


def ffn_fwd(chunk, place, tokens, um, uo, gain, wg, wu, wd):
    index, length, _ = chunk
    width = tokens.shape[1]
    part = sds((length // 2, width), BF)
    return call(
        functools.partial(ffn_fwd_body, length),
        "ffn_fwd",
        (sds((length, width), BF), part, part),
        [SMEM, vmem((length, width), (index, 0))] + [vmem()] * 6,
        (vmem(),) * 3,
        4_000_000 * length,
        8_000 * length,
    )(place, tokens, um, uo, gain, wg, wu, wd)


def embed_rows(length, place, x, us, fs, gain, wp, emb_s):
    half = length // 2
    bases = halves(place, half)
    for n in range(2):
        out = x[pl.ds(bases[n], half)].astype(F32) + us[n][...].astype(F32) + fs[n][...].astype(F32)
        normed = (out * rinv(out) * gain[...]).astype(BF)
        emb_s[pl.ds(bases[n], half)] = nn(normed, wp[...]).astype(BF)


def query_embed_body(length, lane, place, x, um, uo, fm, fo, gain, wp, lane_o, emb_s):
    embed_rows(length, place, x, (um, uo), (fm, fo), gain, wp, emb_s)
    lane_o[...] = emb_s[pl.ds(pl.multiple_of(place[0] * lane, lane), lane)]


def query_embed(chunk, place, tokens, um, uo, fm, fo, gain, wp, lane):
    index, length, _ = chunk
    width = tokens.shape[1]
    return call(
        functools.partial(query_embed_body, length, lane),
        "query_embed",
        sds((lane, wp.shape[1]), BF),
        [SMEM, vmem((length, width), (index, 0))] + [vmem()] * 6,
        vmem(),
        2_000_000 * length,
        8_000 * length,
        [pltpu.VMEM((length, wp.shape[1]), BF)],
    )(place, tokens, um, uo, fm, fo, gain, wp)


def lane_tile(tokens):
    return min(tokens, 512)


def doc_embed_body(length, aliased, *refs):
    refs = list(refs)
    if aliased:
        refs.pop(9)
    place, x, um, uo, fm, fo, gain, wp, queries, emb_o, lse_o = refs
    embed_rows(length, place, x, (um, uo), (fm, fo), gain, wp, emb_o)
    scale = wp.shape[1] ** (-0.5)
    tile = lane_tile(queries.shape[0])
    for start in range(0, queries.shape[0], tile):
        span = slice(start, start + tile)
        scores = nt(emb_o[...], queries[span]) * scale
        top = jnp.max(scores, axis=0, keepdims=True)
        total = jnp.sum(jnp.exp(scores - top), axis=0, keepdims=True)
        lse_o[:, span] = jnp.broadcast_to(top + jnp.log(total), (8, tile))


def doc_embed(chunk, place, tokens, um, uo, fm, fo, gain, wp, queries, so_far):
    index, length, _ = chunk
    width = tokens.shape[1]
    emb = wp.shape[1]
    specs = [SMEM, vmem((length, width), (index, 0))] + [vmem()] * 7
    operands = [place, tokens, um, uo, fm, fo, gain, wp, queries]
    aliases = None
    if so_far is not None:
        specs.append(ANYWHERE)
        operands.append(so_far)
        aliases = {9: 0}
    return call(
        functools.partial(doc_embed_body, length, so_far is not None),
        "doc_embed",
        (sds((tokens.shape[0], emb), BF), sds((8, queries.shape[0]), F32)),
        specs,
        (vmem((length, emb), (index, 0)), vmem()),
        4_000_000 * length,
        8_000 * length,
        aliases=aliases,
    )(*operands)


def segment(tokens, lanes):
    token = lax.broadcasted_iota(jnp.int32, (tokens, lanes), 0) // 32
    return (token == lax.broadcasted_iota(jnp.int32, (tokens, lanes), 1)).astype(F32)


def stats_body(docs, doc_len, *refs):
    lses = refs[:docs]
    weights, hot, out = refs[docs:]
    lanes = hot.shape[1]
    tokens = weights.shape[1]
    seg = segment(tokens, lanes)
    w = weights[...]
    rows = lax.broadcasted_iota(jnp.int32, (8, tokens), 0)
    scores = jnp.zeros((8, tokens), F32)
    for p in range(docs):
        scores = jnp.where(rows == p, lses[p][...], scores)
    scores = w * (scores - jnp.where(rows < docs, math.log(doc_len), 0.0))
    table = DOC_TEMP * jnp.dot(scores, seg, precision=HIGH, preferred_element_type=F32)
    share = jnp.dot(w, seg, precision=HIGH, preferred_element_type=F32)
    lane_rows = lax.broadcasted_iota(jnp.int32, (8, lanes), 0)
    positive = jnp.sum(table * hot[...], axis=0, keepdims=True)
    share = jnp.sum(share * hot[...], axis=0, keepdims=True)
    result = jnp.where(lane_rows < docs, table, 0.0)
    result = jnp.where(lane_rows == docs, positive, result)
    out[...] = jnp.where(lane_rows == docs + 1, share, result)


def stats(lses, weights, hot, doc_len):
    return call(
        functools.partial(stats_body, len(lses), doc_len),
        "doc_stats",
        sds(hot.shape, F32),
        [vmem()] * (len(lses) + 2),
        vmem(),
        1_000_000_000,
        100_000,
    )(*lses, weights, hot)


def score_back_body(docs, doc_len, lane_total, query_total, *refs):
    place, gathered, own, weights, hot, emb, queries = refs[:7]
    lses = refs[7 : 7 + docs]
    keep_o, send_o, query_o, scalars_o, doc_s, query_s = refs[7 + docs :]
    lanes = hot.shape[1]
    tokens = weights.shape[1]
    everything = gathered[...]
    rows = lax.broadcasted_iota(jnp.int32, everything.shape, 1)
    scores = jnp.where(rows < docs, everything, -jnp.inf)
    top = jnp.max(jnp.max(scores, axis=0), axis=0, keepdims=True)
    total = jnp.sum(jnp.sum(jnp.exp(scores - top[None]), axis=0), axis=0, keepdims=True)
    log_norm = top + jnp.log(total)
    summed = jnp.sum(everything, axis=0)
    valid = lax.broadcasted_iota(jnp.int32, (1, lanes), 1) < lane_total
    loss = jnp.where(valid, log_norm - summed[docs : docs + 1], 0.0)
    share = jnp.where(valid, summed[docs + 1 : docs + 2], 0.0)
    out_rows = lax.broadcasted_iota(jnp.int32, (8, 128), 0)
    loss = jnp.sum(loss, axis=1, keepdims=True) / query_total
    share = jnp.sum(share, axis=1, keepdims=True) / query_total
    scalars_o[...] = jnp.where(out_rows == 0, loss, share)
    own_rows = lax.broadcasted_iota(jnp.int32, own.shape, 0)
    grads = DOC_TEMP * (jnp.exp(own[...] - log_norm) - hot[...]) / query_total
    grads = jnp.where(own_rows < docs, grads, 0.0)
    seg = segment(tokens, lanes)
    spread = lax.dot_general(
        grads, seg, (((1,), (1,)), ((), ())), precision=HIGH, preferred_element_type=F32
    )
    token_grad = spread * weights[...]
    emb_width = queries.shape[1]
    scale = emb_width ** (-0.5)
    half = doc_len // 2
    bases = halves(place, half)
    tile = lane_tile(tokens)
    for start in range(0, tokens, tile):
        span = slice(start, start + tile)
        query = queries[span]
        query_grad = jnp.zeros((emb_width, tile), F32)
        for p in range(docs):
            doc = emb[p * doc_len : (p + 1) * doc_len]
            scores = nt(doc, query) * scale
            grad = (token_grad[p : p + 1, span] * jnp.exp(scores - lses[p][:1, span])).astype(BF)
            part = nn(grad, query) * scale
            if start == 0:
                doc_s[p * doc_len : (p + 1) * doc_len] = part
            else:
                doc_s[p * doc_len : (p + 1) * doc_len] += part
            query_grad = query_grad + nn(doc.T, grad)
        query_o[span] = (query_grad * scale).T.astype(BF)
    for p in range(docs):
        keep_o[p * half : (p + 1) * half] = doc_s[pl.ds(p * doc_len + bases[0], half)].astype(BF)
        send_o[p * half : (p + 1) * half] = doc_s[pl.ds(p * doc_len + bases[1], half)].astype(BF)


def score_back(place, gathered, own, weights, hot, emb, queries, lses, doc_len, lane_total, query_total):
    docs = len(lses)
    width = emb.shape[1]
    part = sds((docs * doc_len // 2, width), BF)
    return call(
        functools.partial(score_back_body, docs, doc_len, lane_total, query_total),
        "score_back",
        (part, part, sds(queries.shape, BF), sds((8, 128), F32)),
        [SMEM] + [vmem()] * (6 + docs),
        (vmem(),) * 4,
        6_000_000_000,
        2_000_000,
        [pltpu.VMEM((docs * doc_len, width), F32), pltpu.VMEM((8, 128), F32)],
    )(place, gathered, own, weights, hot, emb, queries, *lses)


def ffn_bwd_body(length, masked, *refs):
    place, x, um, uo, fm, fo = refs[:6]
    grads = refs[6:10] if masked else refs[6:8]
    pos = 10 if masked else 8
    normed, gain_ffn, gain_final, wp, wg, wu, wd = refs[pos : pos + 7]
    fgrad_o, hidden_o, ggrad_o, ugrad_o, proj_o, final_o, keep_o, send_o = refs[pos + 7 : pos + 15]
    half = length // 2
    bases = halves(place, half)
    if masked:
        emb_s = refs[pos + 15]
        lane = grads[0].shape[0]
        me = place[0]
        for step, grad in enumerate(grads):
            at = pl.multiple_of((me ^ step) * lane, lane)
            emb_s[pl.ds(at, lane)] = grad[...]
        egs = [emb_s[pl.ds(base, half)] for base in bases]
    else:
        egs = [grad[...] for grad in grads]
    final_sum = jnp.zeros((1, x.shape[1]), F32)
    proj = jnp.zeros(proj_o.shape, F32)
    for n, (u, f, out) in enumerate(((um, fm, keep_o), (uo, fo, send_o))):
        span = slice(n * half, (n + 1) * half)
        middle = x[pl.ds(bases[n], half)].astype(F32) + u[...].astype(F32)
        output = middle + f[...].astype(F32)
        r = rinv(output)
        dn = nt(egs[n], wp[...])
        unit = output * r
        final_sum = final_sum + jnp.sum(dn * unit, axis=0, keepdims=True)
        proj = proj + nn(egs[n].T, (unit * gain_final[...]).astype(BF))
        fgrad = norm_back(output, r, gain_final[...], dn).astype(BF)
        fgrad_o[span] = fgrad
        gate = nn(normed[span], wg[...])
        up = nn(normed[span], wu[...])
        act, t = gelu_parts(gate)
        hidden_o[span] = (act * up).astype(BF)
        hgrad = nt(fgrad, wd[...])
        slope = 0.5 * (1.0 + t) + 0.5 * gate * (1.0 - t * t) * (
            GELU_A * (1.0 + 3.0 * GELU_B * gate * gate)
        )
        ggrad = (hgrad * up * slope).astype(BF)
        ugrad = (hgrad * act).astype(BF)
        ggrad_o[span] = ggrad
        ugrad_o[span] = ugrad
        out[...] = (nt(ggrad, wg[...]) + nt(ugrad, wu[...])).astype(BF)
    proj_o[...] = proj
    final_o[...] = jnp.broadcast_to(final_sum, final_o.shape)


def ffn_bwd(chunk, place, tokens, us, fs, grads, normed, gain_ffn, gain_final, wp, wg, wu, wd):
    index, length, masked = chunk
    width = tokens.shape[1]
    emb = wp.shape[1]
    units = wg.shape[1]
    grad_specs = [vmem()] * 4 if masked else [vmem((length // 2, emb), (index, 0))] * 2
    part = sds((length // 2, width), BF)
    inner = sds((length, units), BF)
    return call(
        functools.partial(ffn_bwd_body, length, masked),
        "ffn_bwd",
        (
            sds((length, width), BF),
            inner,
            inner,
            inner,
            sds((emb, width), F32),
            sds((8, width), F32),
            part,
            part,
        ),
        [SMEM, vmem((length, width), (index, 0))] + [vmem()] * 4 + grad_specs + [vmem()] * 7,
        (vmem(),) * 8,
        8_000_000 * length,
        12_000 * length,
        [pltpu.VMEM((length, emb), BF)] if masked else [],
    )(place, tokens, *us, *fs, *grads, normed, gain_ffn, gain_final, wp, wg, wu, wd)


def ffn_wgrad_body(count, *refs):
    normed = refs[:count]
    fgrad = refs[count : 2 * count]
    hidden = refs[2 * count : 3 * count]
    ggrad = refs[3 * count : 4 * count]
    ugrad = refs[4 * count : 5 * count]
    out = refs[5 * count]
    width = normed[0].shape[1]
    for n, (left, right) in enumerate(((normed, ggrad), (normed, ugrad), (fgrad, hidden))):
        for start in range(0, width, 256):
            total = sum(tn(a[:, start : start + 256], b[...]) for a, b in zip(left, right))
            out[n * width + start : n * width + start + 256] = total.astype(BF)


def ffn_wgrad(normed, fgrad, hidden, ggrad, ugrad):
    count = len(normed)
    rows = 3 * normed[0].shape[1]
    return call(
        functools.partial(ffn_wgrad_body, count),
        "ffn_wgrad",
        sds((rows, hidden[0].shape[1]), BF),
        [vmem()] * (5 * count),
        vmem(),
        8_000_000_000,
        12_000_000,
    )(*normed, *fgrad, *hidden, *ggrad, *ugrad)


def diagonal_sums(block):
    length = block.shape[0]
    rows = length
    value = jnp.concatenate([block, jnp.zeros((rows, WIDE - length), F32)], axis=1)
    while rows > 8:
        rows //= 2
        value = value[:rows] + pltpu.roll(value[rows:], WIDE - rows, 1)
    total = value[0:1]
    for s in range(1, 8):
        total = total + pltpu.roll(jnp.broadcast_to(value[s : s + 1], (8, WIDE)), WIDE - s, 1)[:1]
    return total


def attn_bwd_body(length, masked, heads, *refs):
    place, x, um, uo, gm, go, fgrad, q, k, v, lse, bias, gain, wq, wk, wv, wo = refs[:17]
    pos = 17
    keep_col = None
    if masked:
        keep_col = refs[pos]
        pos += 1
    agrad_o, dq_o, dk_o, dv_o, diag_o, gain_o, keep_o, send_o, ctx_s, part_s = refs[pos:]
    half = length // 2
    bases = halves(place, half)
    gain_sum = jnp.zeros((1, x.shape[1]), F32)
    for n, (u, g) in enumerate(((um, gm), (uo, go))):
        rows = pl.ds(bases[n], half)
        middle = x[rows].astype(F32) + u[...].astype(F32)
        r = rinv(middle)
        dn = g[...].astype(F32)
        gain_sum = gain_sum + jnp.sum(dn * (middle * r), axis=0, keepdims=True)
        grad = fgrad[n * half : (n + 1) * half].astype(F32) + norm_back(middle, r, gain[...], dn)
        agrad = grad.astype(BF)
        agrad_o[rows] = agrad
        ctx_s[rows] = nt(agrad, wo[...]).astype(BF)
    gain_o[...] = jnp.broadcast_to(gain_sum, gain_o.shape)
    width = q.shape[1] // heads
    tile = min(length, 256)
    kt = k[...].T
    diag_o[...] = jnp.zeros_like(diag_o)
    for h in range(heads):
        cols = slice(h * width, (h + 1) * width)
        kh = k[:, cols]
        vh = v[:, cols]
        dk = jnp.zeros((length, width), F32)
        dv = jnp.zeros((length, width), F32)
        pieces = []
        for start in range(0, length, tile):
            span = slice(start, start + tile)
            qh = q[span, cols]
            ch = ctx_s[span, cols]
            logits = nt(kh, qh) + bias[h, :length, span]
            if masked:
                logits = jnp.where(query_mask_of(keep_col, length), logits, MASKED)
            probs = jnp.exp(logits - lse[h : h + 1, span])
            pgrad = nt(vh, ch)
            delta = jnp.sum(probs * pgrad, axis=0, keepdims=True)
            lgrad = (probs * (pgrad - delta)).astype(BF)
            dv = dv + nn(probs.astype(BF), ch)
            dk = dk + nn(lgrad, qh)
            dq_o[span, cols] = nn(kt[cols], lgrad).T.astype(BF)
            pieces.append(lgrad)
        dk_o[:, cols] = dk.astype(BF)
        dv_o[:, cols] = dv.astype(BF)
        lgrad = jnp.concatenate(pieces, axis=1) if len(pieces) > 1 else pieces[0]
        diag_o[h : h + 1] = diagonal_sums(lgrad.astype(F32))
    part_s[...] = (
        nt(dq_o[...], wq[...]) + nt(dk_o[...], wk[...]) + nt(dv_o[...], wv[...])
    ).astype(BF)
    keep_o[...] = part_s[pl.ds(bases[0], half)]
    send_o[...] = part_s[pl.ds(bases[1], half)]


def attn_bwd(chunk, place, tokens, us, gs, fgrad, kept, bias, gain, wq, wk, wv, wo, keep_col):
    index, length, masked = chunk
    q, k, v, lse = kept
    heads = bias.shape[0]
    cols = q.shape[1]
    width = tokens.shape[1]
    specs = [SMEM, vmem((length, width), (index, 0))] + [vmem()] * 15
    operands = [place, tokens, *us, *gs, fgrad, q, k, v, lse, bias, gain, wq, wk, wv, wo]
    if masked:
        specs.append(vmem())
        operands.append(keep_col)
    small = sds((length, cols), BF)
    part = sds((length // 2, width), BF)
    return call(
        functools.partial(attn_bwd_body, length, masked, heads),
        "attn_bwd",
        (
            sds((length, width), BF),
            small,
            small,
            small,
            sds((8, WIDE), F32),
            sds((8, width), F32),
            part,
            part,
        ),
        specs,
        (vmem(),) * 8,
        10_000_000 * length,
        12_000 * length,
        [pltpu.VMEM((length, cols), BF), pltpu.VMEM((length, width), BF)],
    )(*operands)


def attn_wgrad_body(count, *refs):
    normed, dq, dk, dv, agrad, ctx = (refs[i * count : (i + 1) * count] for i in range(6))
    out = refs[6 * count]
    width = normed[0].shape[1]
    cols = dq[0].shape[1]
    for n, (left, right) in enumerate(((normed, dq), (normed, dk), (normed, dv), (agrad, ctx))):
        total = sum(tn(a[...], b[...]) for a, b in zip(left, right))
        out[n * width : (n + 1) * width] = total.astype(BF)


def attn_wgrad(normed, dq, dk, dv, agrad, ctx):
    count = len(normed)
    width = normed[0].shape[1]
    return call(
        functools.partial(attn_wgrad_body, count),
        "attn_wgrad",
        sds((4 * width, dq[0].shape[1]), BF),
        [vmem()] * (6 * count),
        vmem(),
        4_000_000_000,
        8_000_000,
    )(*normed, *dq, *dk, *dv, *agrad, *ctx)


def tail_body(length, aliased, *refs):
    refs = list(refs)
    if aliased:
        refs.pop(6)
    place, x, agrad, nm, no, gain, out, gain_o = refs
    half = length // 2
    bases = halves(place, half)
    gain_sum = jnp.zeros((1, x.shape[1]), F32)
    for n, g in enumerate((nm, no)):
        rows = pl.ds(bases[n], half)
        xf = x[rows].astype(F32)
        r = rinv(xf)
        dn = g[...].astype(F32)
        gain_sum = gain_sum + jnp.sum(dn * (xf * r), axis=0, keepdims=True)
        out[rows] = (agrad[rows].astype(F32) + norm_back(xf, r, gain[...], dn)).astype(BF)
    gain_o[...] = jnp.broadcast_to(gain_sum, gain_o.shape)


def tail(chunk, place, tokens, agrad, ns, gain, so_far):
    index, length, _ = chunk
    width = tokens.shape[1]
    specs = [SMEM, vmem((length, width), (index, 0))] + [vmem()] * 4
    operands = [place, tokens, agrad, *ns, gain]
    aliases = None
    if so_far is not None:
        specs.append(ANYWHERE)
        operands.append(so_far)
        aliases = {6: 0}
    return call(
        functools.partial(tail_body, length, so_far is not None),
        "tokens_grad",
        (sds(tokens.shape, BF), sds((8, width), F32)),
        specs,
        (vmem((length, width), (index, 0)), vmem()),
        1_000_000 * length,
        8_000 * length,
        aliases=aliases,
    )(*operands)


def swap(block, axis, distance):
    count = lax.axis_size(axis)
    return lax.ppermute(block, axis, [(i, i ^ distance) for i in range(count)])


def added(a, b):
    return (a.astype(F32) + b.astype(F32)).astype(BF)


def mp_sum(keep, send):
    total = added(keep, swap(send, "mp", 1))
    total = added(total, swap(total, "mp", 2))
    return (total, swap(total, "mp", 1))


def dp_gather(block):
    count = lax.axis_size("dp")
    spread = jnp.broadcast_to(block[None], (count,) + block.shape)
    return lax.all_to_all(spread, "dp", 0, 0, tiled=True)


def on_device(
    doc_tokens,
    query_tokens,
    w_query,
    w_key,
    w_value,
    w_out,
    w_gate,
    w_up,
    w_down,
    w_proj,
    gain_attn,
    gain_ffn,
    gain_final,
    bias_table,
    query_mask,
    retrieval_mask,
    positives,
):
    dp_count = lax.axis_size("dp")
    mp_count = lax.axis_size("mp")
    dp_index = lax.axis_index("dp")
    mp_index = lax.axis_index("mp")
    query_len = query_mask.shape[1]
    docs_here = doc_tokens.shape[0] // DOC_LEN
    queries_here = query_tokens.shape[0] // query_len
    query_total = dp_count * queries_here
    width = doc_tokens.shape[1]
    emb_width = w_proj.shape[1]
    units = w_gate.shape[1]
    lane_count = queries_here // mp_count
    lane_total = lane_count * dp_count
    lane_tokens = lane_total * query_len
    lane_pad = -(-lane_total // 128) * 128
    place = jnp.stack([mp_index, mp_index % 2]).astype(jnp.int32)
    gain_attn = gain_attn.reshape(1, width)
    gain_ffn = gain_ffn.reshape(1, width)
    gain_final = gain_final.reshape(1, width)
    home_keep = lax.dynamic_slice_in_dim(query_mask, dp_index * queries_here, queries_here, 0)
    keep_col = home_keep.astype(F32).reshape(-1, 1)

    def lane_view(whole):
        grouped = whole.reshape((dp_count, queries_here) + whole.shape[1:])
        picked = lax.dynamic_slice_in_dim(grouped, mp_index * lane_count, lane_count, 1)
        return picked.reshape((lane_total,) + whole.shape[1:])

    lane_keep = lane_view(query_mask).astype(F32)
    lane_hits = lane_view(retrieval_mask).astype(F32)
    token_weights = lane_keep[:, :, None] * lane_hits / jnp.sum(lane_keep, axis=1)[:, None, None]
    token_weights = token_weights.reshape(lane_tokens, docs_here).T
    token_weights = jnp.pad(token_weights, ((0, 8 - docs_here), (0, 0)))
    doc_ids = dp_index * docs_here + jnp.arange(8, dtype=jnp.int32)
    doc_ids = jnp.where(jnp.arange(8) < docs_here, doc_ids, -1)
    lane_positive = jnp.pad(lane_view(positives), (0, lane_pad - lane_total), constant_values=-2)
    hot = (lane_positive[None, :] == doc_ids[:, None]).astype(F32)

    chunks = [(0, query_tokens.shape[0], True)] + [(p, DOC_LEN, False) for p in range(docs_here)]
    sources = [query_tokens] + [doc_tokens] * docs_here
    bias = make_bias(bias_table)

    attn = [
        attn_fwd(c, place, t, gain_attn, w_query, w_key, w_value, w_out, bias, keep_col)
        for c, t in zip(chunks, sources)
    ]
    attended = [mp_sum(a[6], a[7]) for a in attn]
    ffn = [
        ffn_fwd(c, place, t, *u, gain_ffn, w_gate, w_up, w_down)
        for c, t, u in zip(chunks, sources, attended)
    ]
    forwarded = [mp_sum(f[1], f[2]) for f in ffn]

    lane_block = query_embed(
        chunks[0], place, query_tokens, *attended[0], *forwarded[0], gain_final, w_proj,
        lane_count * query_len,
    )
    queries = dp_gather(lane_block).reshape(lane_tokens, emb_width)
    emb = None
    lses = []
    for c, u, f in zip(chunks[1:], attended[1:], forwarded[1:]):
        emb, lse = doc_embed(c, place, doc_tokens, *u, *f, gain_final, w_proj, queries, emb)
        lses.append(lse)
    own = stats(lses, token_weights, hot, DOC_LEN)
    gathered = dp_gather(own)
    keep, send, query_part, scalars = score_back(
        place, gathered, own, token_weights, hot, emb, queries, lses, DOC_LEN, lane_total, query_total
    )
    doc_grads = mp_sum(keep, send)
    query_part = query_part.reshape(dp_count, lane_count * query_len, emb_width)
    query_part = lax.all_to_all(query_part, "dp", 0, 0, tiled=True)
    query_here = jnp.sum(query_part.astype(F32), axis=0).astype(BF)
    query_far = swap(query_here, "mp", 2)
    query_grads = [query_here, swap(query_here, "mp", 1), query_far, swap(query_far, "mp", 1)]
    scalars = scalars + swap(scalars, "mp", 1)
    scalars = scalars + swap(scalars, "mp", 2)

    order = list(range(1, docs_here + 1)) + [0]
    back = {}
    for n in order:
        back[n] = ffn_bwd(
            chunks[n],
            place,
            sources[n],
            attended[n],
            forwarded[n],
            query_grads if n == 0 else doc_grads,
            ffn[n][0],
            gain_ffn,
            gain_final,
            w_proj,
            w_gate,
            w_up,
            w_down,
        )
    middle_back = {n: mp_sum(back[n][6], back[n][7]) for n in order}
    ffn_pack = ffn_wgrad(
        [ffn[n][0] for n in order], *[[back[n][i] for n in order] for i in range(4)]
    )
    attn_back = {}
    for n in order:
        attn_back[n] = attn_bwd(
            chunks[n],
            place,
            sources[n],
            attended[n],
            middle_back[n],
            back[n][0],
            (attn[n][1], attn[n][2], attn[n][3], attn[n][4]),
            bias,
            gain_ffn,
            w_query,
            w_key,
            w_value,
            w_out,
            keep_col,
        )
    inputs_back = {n: mp_sum(attn_back[n][6], attn_back[n][7]) for n in order}
    attn_pack = attn_wgrad(
        [attn[n][0] for n in order],
        [attn_back[n][1] for n in order],
        [attn_back[n][2] for n in order],
        [attn_back[n][3] for n in order],
        [attn_back[n][0] for n in order],
        [attn[n][5] for n in order],
    )
    tokens_grad = None
    gains = []
    for n in order[:-1]:
        tokens_grad, gain = tail(
            chunks[n], place, doc_tokens, attn_back[n][0], inputs_back[n], gain_attn, tokens_grad
        )
        gains.append(gain)
    query_tokens_grad, gain = tail(
        chunks[0], place, query_tokens, attn_back[0][0], inputs_back[0], gain_attn, None
    )
    gains.append(gain)

    proj = sum(back[n][4] for n in order)
    diag = sum(attn_back[n][4] for n in order)
    small = jnp.concatenate(
        [
            sum(gains)[:1],
            sum(attn_back[n][5] for n in order)[:1],
            sum(back[n][5] for n in order)[:1],
        ],
        axis=0,
    )
    ffn_pack, proj = lax.psum((ffn_pack, proj.astype(BF)), "dp")
    attn_pack = lax.psum(attn_pack, "dp")
    small, diag = lax.psum((small, diag), "dp")

    lane = jnp.arange(WIDE, dtype=jnp.int32)
    offset = jnp.where(lane < DOC_LEN, -lane, WIDE - lane)
    distance = jnp.abs(offset)
    far = 8 + sum(((distance >= edge).astype(jnp.int32) for edge in EDGES))
    index = jnp.where(distance < 8, distance, far) + 16 * (offset > 0).astype(jnp.int32)
    onehot = (jnp.arange(bias_table.shape[0], dtype=jnp.int32)[:, None] == index[None]).astype(F32)
    grad_bias = lax.dot_general(
        onehot, diag[: bias_table.shape[1]], (((1,), (1,)), ((), ())), precision=HIGH
    )
    ffn_pack = ffn_pack.astype(F32)
    attn_pack = attn_pack.astype(F32)
    return (
        scalars[0, 0],
        scalars[1, 0],
        emb,
        tokens_grad,
        query_tokens_grad,
        attn_pack[:width],
        attn_pack[width : 2 * width],
        attn_pack[2 * width : 3 * width],
        attn_pack[3 * width :].T,
        ffn_pack[:width],
        ffn_pack[width : 2 * width],
        ffn_pack[2 * width :].T,
        proj.astype(F32).T,
        small[0],
        small[1],
        small[2],
        grad_bias,
    )


def solution(mesh):
    placed = (
        P("dp", None),
        P("dp", None),
        P(None, "mp"),
        P(None, "mp"),
        P(None, "mp"),
        P("mp", None),
        P(None, "mp"),
        P(None, "mp"),
        P("mp", None),
        P(),
        P(),
        P(),
        P(),
        P(None, "mp"),
        P(),
        P(None, None, "dp"),
        P(),
    )
    return jax.shard_map(
        on_device,
        mesh=mesh,
        in_specs=placed,
        out_specs=(
            P(),
            P(),
            P("dp", None),
            P("dp", None),
            P("dp", None),
            P(None, "mp"),
            P(None, "mp"),
            P(None, "mp"),
            P("mp", None),
            P(None, "mp"),
            P(None, "mp"),
            P("mp", None),
            P(),
            P(),
            P(),
            P(),
            P(None, "mp"),
        ),
        check_vma=False,
    )
```

```python
import functools
import math

import jax
import jax.numpy as jnp
from jax import lax
from jax.experimental import pallas as pl
from jax.experimental.pallas import tpu as pltpu
from jax.sharding import PartitionSpec as P

DOC_LEN = 512
EPS = 1e-06
DOC_TEMP = 32.0
EDGES = (12, 16, 23, 32, 46, 64, 91)
HIGH = lax.Precision.HIGHEST
MASKED = -1000000000.0
BF = jnp.bfloat16
F32 = jnp.float32
WIDE = 2 * DOC_LEN
GELU_A = math.sqrt(2.0 / math.pi)
GELU_B = 0.044715


def nn(a, b):
    return jnp.dot(a, b, preferred_element_type=F32)


def nt(a, b):
    return lax.dot_general(a, b, (((1,), (1,)), ((), ())), preferred_element_type=F32)


def tn(a, b):
    return lax.dot_general(a, b, (((0,), (0,)), ((), ())), preferred_element_type=F32)


def rinv(v):
    return lax.rsqrt(jnp.mean(v * v, axis=-1, keepdims=True) + EPS)


def norm_back(v, r, gain, grad):
    scaled = grad * gain
    return r * scaled - v * (r * r * r * jnp.mean(scaled * v, axis=-1, keepdims=True))


def rowsum8(v):
    return jnp.broadcast_to(jnp.sum(v, axis=0, keepdims=True), (8, v.shape[1]))


def halves(place, half):
    mine = pl.multiple_of(place[1] * half, half)
    other = pl.multiple_of((1 - place[1]) * half, half)
    return (mine, other)


class Load:
    def __init__(self, start=0, rows=None, pinned=True):
        self.start = start
        self.rows = rows
        self.pinned = pinned

    def shape(self, operand):
        return operand.shape if self.rows is None else (self.rows,) + operand.shape[1:]

    def of(self, ref):
        return ref if self.rows is None else ref.at[pl.ds(self.start, self.rows)]


class Held:
    def __init__(self, ref, copy):
        self.ref = ref
        self.copy = copy
        self.begun = False

    @property
    def shape(self):
        return self.ref.shape

    @property
    def dtype(self):
        return self.ref.dtype


class Operand(Held):
    def ready(self):
        if not self.begun:
            self.begun = True
            self.copy.wait()
        return self.ref

    def __getitem__(self, at):
        return self.ready()[at]


class Result(Held):
    def __getitem__(self, at):
        return self.ref[at]

    def __setitem__(self, at, value):
        self.ref[at] = value

    def done(self):
        if not self.begun:
            self.begun = True
            self.copy.start()


LOAD = Load()
PASS = Load(pinned=False)
SMEM = pl.BlockSpec(memory_space=pltpu.SMEM)
FAR = pl.BlockSpec(memory_space=pltpu.HBM)


def sds(shape, dtype):
    return jax.ShapeDtypeStruct(shape, dtype)


class Kept:
    def __init__(self, shape, dtype):
        self.shape = shape
        self.dtype = dtype


def kept(shape, dtype):
    return Kept(shape, dtype)


def call(body, name, outs, in_specs, micros, scratch=(), into=None, after=(), order=()):
    count = len(outs)
    stores = [LOAD] * count
    out_shape = list(outs)
    if into is not None:
        out_shape[0], start, into_so_far = into
        stores[0] = Load(start, outs[0].shape[0])
        if into_so_far is not None:
            after = (into_so_far,) + tuple(after)

    def run(*operands):
        pinned = [
            pltpu.with_memory_space_constraint(operand, pltpu.HBM) if isinstance(spec, Load) and spec.pinned else operand
            for spec, operand in zip(in_specs, operands)
        ]
        loads = [n for n, spec in enumerate(in_specs) if isinstance(spec, Load)]
        total = len(loads)
        given = len(operands)
        buffers = [
            pltpu.VMEM(in_specs[n].shape(operands[n]), operands[n].dtype) for n in loads
        ] + [pltpu.VMEM(out.shape, out.dtype) for out in outs]

        def kernel(*refs):
            ins = list(refs[:given])
            results = refs[given + len(after) : given + len(after) + count]
            rest = refs[given + len(after) + count :]
            own, held, sems = rest[: len(scratch)], rest[len(scratch) : -1], rest[-1]
            for n in sorted(loads, key=lambda n: order.index(n) if n in order else given + n):
                k = loads.index(n)
                copy = pltpu.make_async_copy(in_specs[n].of(ins[n]), held[k], sems.at[k])
                copy.start()
                ins[n] = Operand(held[k], copy)
            made = []
            for k, result in enumerate(results):
                buffer = held[total + k]
                copy = pltpu.make_async_copy(buffer, stores[k].of(result), sems.at[total + k])
                made.append(Result(buffer, copy))
            body(*ins, *made, *own)
            for n in loads:
                ins[n].ready()
            for result in made:
                result.done()
            for result in made:
                result.copy.wait()

        return pl.pallas_call(
            kernel,
            name=name,
            out_shape=tuple(
                pltpu.HBM(out.shape, out.dtype) if isinstance(out, Kept) else out for out in out_shape
            ),
            in_specs=[FAR if isinstance(spec, Load) else spec for spec in in_specs]
            + [FAR] * len(after),
            out_specs=(FAR,) * count,
            scratch_shapes=list(scratch) + buffers + [pltpu.SemaphoreType.DMA((total + count,))],
            input_output_aliases={given: 0} if into is not None and into[2] is not None else {},
            compiler_params=pltpu.CompilerParams(vmem_limit_bytes=48 * 1024 * 1024),
            cost_estimate=pl.CostEstimate(
                flops=int(micros * 1.15e9), bytes_accessed=int(micros * 1e6), transcendentals=0
            ),
        )(*pinned, *after)

    return run


def bias_into(table, out):
    lane = lax.broadcasted_iota(jnp.int32, (8, WIDE), 1)
    offset = jnp.where(lane < DOC_LEN, -lane, WIDE - lane)
    distance = jnp.abs(offset)
    far = jnp.full_like(distance, 8)
    for edge in EDGES:
        far = far + (distance >= edge).astype(jnp.int32)
    index = jnp.where(distance < 8, distance, far) + jnp.where(offset > 0, 16, 0)
    for head in range(out.shape[0]):
        row = jnp.zeros((8, WIDE), F32)
        for bucket in range(table.shape[1]):
            row = jnp.where(index == bucket, table[head, bucket], row)
        spread = jnp.broadcast_to(row[:1], (DOC_LEN, WIDE))
        rolled = pltpu.roll(spread, 0, 1, stride=1, stride_axis=0)
        out[head] = rolled[:, :DOC_LEN]


def make_bias(table):
    return call(
        bias_into,
        "rel_bias",
        (kept((table.shape[0], DOC_LEN, DOC_LEN), F32),),
        [SMEM],
        2.0,
    )(table)[0]


def attn_fwd_body(length, masked, heads, *refs):
    place, x, gain, wq, wk, wv, wo, bias = refs[:8]
    pos = 8
    keep_col = None
    if masked:
        keep_col = refs[8]
        pos = 9
    normed_o, q_o, k_o, v_o, lse_o, ctx_o, keep_o, send_o, part_s = refs[pos:]
    half = length // 2
    xf = x[...].astype(F32)
    normed = (xf * rinv(xf) * gain[...]).astype(BF)
    normed_o[...] = normed
    normed_o.done()
    q = nt(normed, wq[...]).astype(BF)
    k = nt(normed, wk[...]).astype(BF)
    v = nt(normed, wv[...]).astype(BF)
    q_o[...] = q
    k_o[...] = k
    v_o[...] = v
    for result in (q_o, k_o, v_o):
        result.done()
    width = q.shape[1] // heads
    vt = v.T
    tile = min(length, 256)
    lse_o[...] = jnp.zeros(lse_o.shape, F32)
    for h in range(heads):
        cols = slice(h * width, (h + 1) * width)
        for start in range(0, length, tile):
            span = slice(start, start + tile)
            logits = nt(k[:, cols], q[span, cols]) + bias[h, :length, span]
            if masked:
                logits = jnp.where(query_mask_of(keep_col, length), logits, MASKED)
            top = jnp.max(logits, axis=0, keepdims=True)
            shifted = jnp.exp(logits - top)
            total = jnp.sum(shifted, axis=0, keepdims=True)
            probs = (shifted * (1.0 / total)).astype(BF)
            ctx_t = nn(vt[cols], probs)
            ctx_o[span, cols] = ctx_t.T.astype(BF)
            lse_o[h : h + 1, span] = top + jnp.log(total)
    ctx_o.done()
    lse_o.done()
    part_s[...] = nn(ctx_o[...], wo[...]).astype(BF)
    mine, other = halves(place, half)
    keep_o[...] = part_s[pl.ds(mine, half)]
    send_o[...] = part_s[pl.ds(other, half)]


def query_mask_of(keep_col, length):
    key_row = lax.broadcasted_iota(jnp.int32, (length, length), 0)
    query_row = lax.broadcasted_iota(jnp.int32, (length, length), 1)
    return ((key_row // 32) == (query_row // 32)) & (keep_col[...] > 0)


def attn_fwd(chunk, place, tokens, gain, wq, wk, wv, wo, bias, keep_col, after):
    index, length, masked = chunk
    heads = bias.shape[0]
    cols = wq.shape[0]
    width = tokens.shape[1]
    specs = [SMEM, Load(index * length, length), PASS] + [LOAD] * 5
    operands = [place, tokens, gain, wq, wk, wv, wo, bias]
    if masked:
        specs.append(PASS)
        operands.append(keep_col)
    small = kept((length, cols), BF)
    part = sds((length // 2, width), BF)
    return call(
        functools.partial(attn_fwd_body, length, masked, heads),
        "attn_fwd",
        (kept((length, width), BF), small, small, small, kept((8, length), F32), small, part, part),
        specs,
        0.012 * length,
        [pltpu.VMEM((length, width), BF)],
        after=after,
    )(*operands)


def gelu_parts(gate):
    t = jnp.tanh(GELU_A * (gate + GELU_B * gate * gate * gate))
    return 0.5 * gate * (1.0 + t), t


def ffn_fwd_body(length, place, x, um, uo, gain, wg, wu, wd, middle_o, normed_o, keep_o, send_o):
    half = length // 2
    bases = halves(place, half)
    for n, (u, out) in enumerate(((um, keep_o), (uo, send_o))):
        middle = x[pl.ds(bases[n], half)].astype(F32) + u[...].astype(F32)
        middle_o[n * half : (n + 1) * half] = middle
        normed = (middle * rinv(middle) * gain[...]).astype(BF)
        normed_o[n * half : (n + 1) * half] = normed
        if n == 1:
            middle_o.done()
            normed_o.done()
        act, _ = gelu_parts(nn(normed, wg[...]))
        hidden = (act * nn(normed, wu[...])).astype(BF)
        out[...] = nn(hidden, wd[...]).astype(BF)


def ffn_fwd(chunk, place, tokens, um, uo, gain, wg, wu, wd, after):
    index, length, _ = chunk
    width = tokens.shape[1]
    part = sds((length // 2, width), BF)
    return call(
        functools.partial(ffn_fwd_body, length),
        "ffn_fwd",
        (kept((length, width), F32), kept((length, width), BF), part, part),
        [SMEM, Load(index * length, length)] + [PASS] * 3 + [LOAD] * 3,
        0.01 * length,
        after=after,
        order=(4, 2, 1, 5, 6, 7, 3),
    )(place, tokens, um, uo, gain, wg, wu, wd)


def embed_rows(length, place, middle, fs, gain, wp, emb_s, out_o):
    half = length // 2
    bases = halves(place, half)
    for n in range(2):
        span = slice(n * half, (n + 1) * half)
        out = middle[span] + fs[n][...].astype(F32)
        out_o[span] = out
        if n == 1:
            out_o.done()
        normed = (out * rinv(out) * gain[...]).astype(BF)
        emb_s[pl.ds(bases[n], half)] = nn(normed, wp[...]).astype(BF)


def query_embed_body(length, lane, place, middle, fm, fo, gain, wp, lane_o, out_o, emb_s):
    embed_rows(length, place, middle, (fm, fo), gain, wp, emb_s, out_o)
    lane_o[...] = emb_s[pl.ds(pl.multiple_of(place[0] * lane, lane), lane)]


def query_embed(place, middle, fm, fo, gain, wp, lane):
    length = middle.shape[0]
    emb = wp.shape[1]
    return call(
        functools.partial(query_embed_body, length, lane),
        "query_embed",
        (sds((lane, emb), BF), kept(middle.shape, F32)),
        [SMEM, LOAD] + [PASS] * 3 + [LOAD],
        0.004 * length,
        [pltpu.VMEM((length, emb), BF)],
    )(place, middle, fm, fo, gain, wp)


def lane_tile(tokens):
    return min(tokens, 512)


def doc_embed_body(length, place, middle, fm, fo, gain, wp, queries, emb_o, lse_o, out_o):
    embed_rows(length, place, middle, (fm, fo), gain, wp, emb_o, out_o)
    emb_o.done()
    scale = wp.shape[1] ** (-0.5)
    tile = lane_tile(queries.shape[0])
    for start in range(0, queries.shape[0], tile):
        span = slice(start, start + tile)
        scores = nt(emb_o[...], queries[span]) * scale
        top = jnp.max(scores, axis=0, keepdims=True)
        total = jnp.sum(jnp.exp(scores - top), axis=0, keepdims=True)
        lse_o[:, span] = jnp.broadcast_to(top + jnp.log(total), (8, tile))


def doc_embed(index, place, middle, fm, fo, gain, wp, queries, so_far, docs):
    length = middle.shape[0]
    emb = wp.shape[1]
    return call(
        functools.partial(doc_embed_body, length),
        "doc_embed",
        (kept((length, emb), BF), sds((8, queries.shape[0]), F32), kept(middle.shape, F32)),
        [SMEM, LOAD] + [PASS] * 3 + [LOAD, PASS],
        0.005 * length,
        into=(kept((docs * length, emb), BF), index * length, so_far),
        order=(4, 2, 1, 5, 6, 3),
    )(place, middle, fm, fo, gain, wp, queries)


def segment(tokens, lanes):
    token = lax.broadcasted_iota(jnp.int32, (tokens, lanes), 0) // 32
    return (token == lax.broadcasted_iota(jnp.int32, (tokens, lanes), 1)).astype(F32)


def stats_body(docs, doc_len, *refs):
    lses = refs[:docs]
    weights, hot, out = refs[docs:]
    lanes = hot.shape[1]
    tokens = weights.shape[1]
    seg = segment(tokens, lanes)
    w = weights[...]
    rows = lax.broadcasted_iota(jnp.int32, (8, tokens), 0)
    scores = jnp.zeros((8, tokens), F32)
    for p in range(docs):
        scores = jnp.where(rows == p, lses[p][...], scores)
    scores = w * (scores - jnp.where(rows < docs, math.log(doc_len), 0.0))
    table = DOC_TEMP * jnp.dot(scores, seg, precision=HIGH, preferred_element_type=F32)
    share = jnp.dot(w, seg, precision=HIGH, preferred_element_type=F32)
    lane_rows = lax.broadcasted_iota(jnp.int32, (8, lanes), 0)
    positive = jnp.sum(table * hot[...], axis=0, keepdims=True)
    share = jnp.sum(share * hot[...], axis=0, keepdims=True)
    result = jnp.where(lane_rows < docs, table, 0.0)
    result = jnp.where(lane_rows == docs, positive, result)
    out[...] = jnp.where(lane_rows == docs + 1, share, result)


def stats(lses, weights, hot, doc_len):
    return call(
        functools.partial(stats_body, len(lses), doc_len),
        "doc_stats",
        (sds(hot.shape, F32),),
        [PASS] * (len(lses) + 2),
        0.5,
    )(*lses, weights, hot)[0]


def score_back_body(docs, doc_len, lane_total, query_total, *refs):
    place, gathered, own, weights, hot, emb, queries = refs[:7]
    lses = refs[7 : 7 + docs]
    keep_o, send_o, query_o, scalars_o, doc_s, query_s = refs[7 + docs :]
    lanes = hot.shape[1]
    tokens = weights.shape[1]
    everything = gathered[...]
    rows = lax.broadcasted_iota(jnp.int32, everything.shape, 1)
    scores = jnp.where(rows < docs, everything, -jnp.inf)
    top = jnp.max(jnp.max(scores, axis=0), axis=0, keepdims=True)
    total = jnp.sum(jnp.sum(jnp.exp(scores - top[None]), axis=0), axis=0, keepdims=True)
    log_norm = top + jnp.log(total)
    summed = jnp.sum(everything, axis=0)
    valid = lax.broadcasted_iota(jnp.int32, (1, lanes), 1) < lane_total
    loss = jnp.where(valid, log_norm - summed[docs : docs + 1], 0.0)
    share = jnp.where(valid, summed[docs + 1 : docs + 2], 0.0)
    out_rows = lax.broadcasted_iota(jnp.int32, (8, 128), 0)
    loss = jnp.sum(loss, axis=1, keepdims=True) / query_total
    share = jnp.sum(share, axis=1, keepdims=True) / query_total
    scalars_o[...] = jnp.where(out_rows == 0, loss, share)
    own_rows = lax.broadcasted_iota(jnp.int32, own.shape, 0)
    grads = DOC_TEMP * (jnp.exp(own[...] - log_norm) - hot[...]) / query_total
    grads = jnp.where(own_rows < docs, grads, 0.0)
    seg = segment(tokens, lanes)
    spread = lax.dot_general(
        grads, seg, (((1,), (1,)), ((), ())), precision=HIGH, preferred_element_type=F32
    )
    token_grad = spread * weights[...]
    emb_width = queries.shape[1]
    scale = emb_width ** (-0.5)
    half = doc_len // 2
    bases = halves(place, half)
    tile = lane_tile(tokens)
    for start in range(0, tokens, tile):
        span = slice(start, start + tile)
        query = queries[span]
        query_grad = jnp.zeros((emb_width, tile), F32)
        for p in range(docs):
            doc = emb[p * doc_len : (p + 1) * doc_len]
            scores = nt(doc, query) * scale
            grad = (token_grad[p : p + 1, span] * jnp.exp(scores - lses[p][:1, span])).astype(BF)
            part = nn(grad, query) * scale
            if start == 0:
                doc_s[p * doc_len : (p + 1) * doc_len] = part
            else:
                doc_s[p * doc_len : (p + 1) * doc_len] += part
            query_grad = query_grad + nn(doc.T, grad)
        query_o[span] = (query_grad * scale).T.astype(BF)
    for p in range(docs):
        keep_o[p * half : (p + 1) * half] = doc_s[pl.ds(p * doc_len + bases[0], half)].astype(BF)
        send_o[p * half : (p + 1) * half] = doc_s[pl.ds(p * doc_len + bases[1], half)].astype(BF)


def score_back(place, gathered, own, weights, hot, emb, queries, lses, doc_len, lane_total, query_total):
    docs = len(lses)
    width = emb.shape[1]
    part = sds((docs * doc_len // 2, width), BF)
    return call(
        functools.partial(score_back_body, docs, doc_len, lane_total, query_total),
        "score_back",
        (part, part, sds(queries.shape, BF), sds((8, 128), F32)),
        [SMEM] + [PASS] * 4 + [LOAD] + [PASS] * (1 + docs),
        3.0,
        [pltpu.VMEM((docs * doc_len, width), F32), pltpu.VMEM((8, 128), F32)],
    )(place, gathered, own, weights, hot, emb, queries, *lses)


def query_sum_body(parts, out):
    out[...] = jnp.sum(parts[...].astype(F32), axis=0).astype(BF)


def query_sum(parts, after):
    return call(
        query_sum_body, "query_sum", (sds(parts.shape[1:], BF),), [PASS], 1.5, after=after
    )(parts)[0]


def ffn_bwd_body(length, masked, *refs):
    place, final = refs[:2]
    grads = refs[2:6] if masked else refs[2:4]
    pos = 6 if masked else 4
    normed, gain_final, wp, wg, wu, wd = refs[pos : pos + 6]
    fgrad_o, hidden_o, ggrad_o, ugrad_o, proj_o, final_o, keep_o, send_o = refs[pos + 6 : pos + 14]
    half = length // 2
    bases = halves(place, half)
    if masked:
        emb_s = refs[pos + 14]
        lane = grads[0].shape[0]
        me = place[0]
        for step, grad in enumerate(grads):
            at = pl.multiple_of((me ^ step) * lane, lane)
            emb_s[pl.ds(at, lane)] = grad[...]
        egs = [emb_s[pl.ds(base, half)] for base in bases]
    else:
        egs = [grad[...] for grad in grads]
    final_sum = jnp.zeros((1, final.shape[1]), F32)
    proj = jnp.zeros(proj_o.shape, F32)
    for n, out in enumerate((keep_o, send_o)):
        span = slice(n * half, (n + 1) * half)
        output = final[span]
        r = rinv(output)
        dn = nt(egs[n], wp[...])
        unit = output * r
        final_sum = final_sum + jnp.sum(dn * unit, axis=0, keepdims=True)
        proj = proj + nn(egs[n].T, (unit * gain_final[...]).astype(BF))
        fgrad = norm_back(output, r, gain_final[...], dn).astype(BF)
        fgrad_o[span] = fgrad
        if n == 1:
            fgrad_o.done()
        gate = nn(normed[span], wg[...])
        up = nn(normed[span], wu[...])
        act, t = gelu_parts(gate)
        hidden_o[span] = (act * up).astype(BF)
        hgrad = nt(fgrad, wd[...])
        slope = 0.5 * (1.0 + t) + 0.5 * gate * (1.0 - t * t) * (
            GELU_A * (1.0 + 3.0 * GELU_B * gate * gate)
        )
        ggrad = (hgrad * up * slope).astype(BF)
        ugrad = (hgrad * act).astype(BF)
        ggrad_o[span] = ggrad
        ugrad_o[span] = ugrad
        if n == 1:
            for result in (hidden_o, ggrad_o, ugrad_o):
                result.done()
        out[...] = (nt(ggrad, wg[...]) + nt(ugrad, wu[...])).astype(BF)
    proj_o[...] = proj
    final_o[...] = jnp.broadcast_to(final_sum, final_o.shape)


def ffn_bwd(chunk, place, final, grads, normed, gain_final, wp, wg, wu, wd, after):
    index, length, masked = chunk
    width = final.shape[1]
    emb = wp.shape[1]
    units = wg.shape[1]
    half = length // 2
    grad_specs = [PASS] * 4 if masked else [Load(index * half, half, pinned=False)] * 2
    part = sds((half, width), BF)
    inner = kept((length, units), BF)
    return call(
        functools.partial(ffn_bwd_body, length, masked),
        "ffn_bwd",
        (
            kept((length, width), BF),
            inner,
            inner,
            inner,
            kept((emb, width), F32),
            sds((8, width), F32),
            part,
            part,
        ),
        [SMEM, LOAD] + grad_specs + [LOAD, PASS] + [LOAD] * 4,
        0.013 * length,
        [pltpu.VMEM((length, emb), BF)] if masked else [],
        after=after,
        order=(7, 2, 3, 4, 5, 8, 1, 6, 9, 10, 11) if masked else (5, 2, 3, 6, 1, 4, 7, 8, 9),
    )(place, final, *grads, normed, gain_final, wp, wg, wu, wd)


def relative_store(out, value, place, pieces, rows, first, lanes):
    for n in range(value.shape[0] // rows):
        slot = reversed_bits(first + n, pieces) ^ place[2]
        out[pl.ds(pl.multiple_of(slot * rows, rows), rows), lanes] = value[n * rows : (n + 1) * rows]


def reversed_bits(number, count):
    result = 0
    while count > 1:
        result = result * 2 + number % 2
        number //= 2
        count //= 2
    return result


def split_out(out, keep_o, send_o):
    half = out.shape[0] // 2
    keep_o[...] = out[:half]
    send_o[...] = out[half:]


def ffn_wgrad_body(count, pieces, *refs):
    place = refs[0]
    normed, fgrad, hidden, ggrad, ugrad, proj = (
        refs[1 + i * count : 1 + (i + 1) * count] for i in range(6)
    )
    wide_keep, wide_send, down_keep, down_send, wide_s, down_s = refs[1 + 6 * count :]
    width = normed[0].shape[1]
    units = hidden[0].shape[1]
    rows = width // pieces
    for start in range(0, width, 2 * rows):
        span = slice(start, start + 2 * rows)
        gate = sum(tn(a[:, span], b[...]) for a, b in zip(normed, ggrad)).astype(BF)
        relative_store(wide_s, gate, place, pieces, rows, start // rows, slice(0, units))
    for start in range(0, width, 2 * rows):
        span = slice(start, start + 2 * rows)
        up = sum(tn(a[:, span], b[...]) for a, b in zip(normed, ugrad)).astype(BF)
        relative_store(wide_s, up, place, pieces, rows, start // rows, slice(units, 2 * units))
    total = sum(p[...] for p in proj).T.astype(BF)
    relative_store(wide_s, total, place, pieces, rows, 0, slice(2 * units, wide_s.shape[1]))
    split_out(wide_s, wide_keep, wide_send)
    wide_send.done()
    wide_keep.done()
    rows = units // pieces
    for start in range(0, units, 2 * rows):
        span = slice(start, start + 2 * rows)
        down = sum(tn(a[:, span], b[...]) for a, b in zip(hidden, fgrad)).astype(BF)
        relative_store(down_s, down, place, pieces, rows, start // rows, slice(0, width))
    split_out(down_s, down_keep, down_send)


def ffn_wgrad(place, pieces, normed, fgrad, hidden, ggrad, ugrad, proj, after):
    count = len(normed)
    width = normed[0].shape[1]
    units = hidden[0].shape[1]
    lanes = 2 * units + proj[0].shape[0]
    wide = sds((width // 2, lanes), BF)
    down = sds((units // 2, width), BF)
    return call(
        functools.partial(ffn_wgrad_body, count, pieces),
        "ffn_wgrad",
        (wide, wide, down, down),
        [SMEM] + [LOAD] * (6 * count),
        10.0,
        after=after,
        order=[1 + i * count + n for i in (0, 3, 4, 5, 2, 1) for n in range(count)],
        scratch=[pltpu.VMEM((width, lanes), BF), pltpu.VMEM((units, width), BF)],
    )(place, *normed, *fgrad, *hidden, *ggrad, *ugrad, *proj)


def unpack_body(pieces, rows, count, cut, *refs):
    place = refs[0]
    parts = [part.ready() for part in refs[1 : 1 + count]]
    outs = refs[1 + count :]
    for number in range(pieces):
        slot = reversed_bits(number, pieces) ^ place[2]
        for part, base in zip(parts, (0, pieces // 2)):

            @pl.when((slot >= base) & (slot < base + part.shape[0] // rows))
            def _(part=part, base=base):
                start = pl.multiple_of((slot - base) * rows, rows)
                value = part[pl.ds(start, rows)].astype(F32)
                cut(outs, number * rows, rows, value)


def cut_lanes(outs, at, rows, value):
    lane = 0
    for out in outs:
        out[at : at + rows] = value[:, lane : lane + out.shape[1]]
        lane += out.shape[1]


def cut_rows(outs, at, rows, value):
    n, at = divmod(at, outs[0].shape[0])
    outs[n][at : at + rows] = value


def unpack(place, pieces, parts, cut, shapes):
    rows = sum(part.shape[0] for part in parts) // pieces
    return call(
        functools.partial(unpack_body, pieces, rows, len(parts), cut),
        "unpack",
        tuple(kept(shape, F32) for shape in shapes),
        [SMEM] + [PASS] * len(parts),
        2.0,
    )(place, *parts)


def diagonal_sums(block):
    length = block.shape[0]
    rows = length
    value = jnp.concatenate([block, jnp.zeros((rows, WIDE - length), F32)], axis=1)
    while rows > 8:
        rows //= 2
        value = value[:rows] + pltpu.roll(value[rows:], WIDE - rows, 1)
    total = value[0:1]
    for s in range(1, 8):
        total = total + pltpu.roll(jnp.broadcast_to(value[s : s + 1], (8, WIDE)), WIDE - s, 1)[:1]
    return total


def attn_bwd_body(length, masked, heads, *refs):
    place, x, mid, gm, go, fgrad, q, k, v, lse, bias, gain, wq, wk, wv, wo = refs[:16]
    pos = 16
    keep_col = None
    if masked:
        keep_col = refs[pos]
        pos += 1
    agrad_o, dq_o, dk_o, dv_o, diag_o, gain_o, keep_o, send_o, ctx_s, part_s = refs[pos:]
    half = length // 2
    bases = halves(place, half)
    gain_sum = jnp.zeros((1, x.shape[1]), F32)
    for n, g in enumerate((gm, go)):
        rows = pl.ds(bases[n], half)
        middle = mid[n * half : (n + 1) * half]
        r = rinv(middle)
        dn = g[...].astype(F32)
        gain_sum = gain_sum + jnp.sum(dn * (middle * r), axis=0, keepdims=True)
        grad = fgrad[n * half : (n + 1) * half].astype(F32) + norm_back(middle, r, gain[...], dn)
        agrad = grad.astype(BF)
        agrad_o[rows] = agrad
        ctx_s[rows] = nt(agrad, wo[...]).astype(BF)
    agrad_o.done()
    width = q.shape[1] // heads
    tile = min(length, 256)
    kt = k[...].T
    diag_o[...] = jnp.zeros(diag_o.shape, F32)
    for h in range(heads):
        cols = slice(h * width, (h + 1) * width)
        kh = k[:, cols]
        vh = v[:, cols]
        dk = jnp.zeros((length, width), F32)
        dv = jnp.zeros((length, width), F32)
        pieces = []
        for start in range(0, length, tile):
            span = slice(start, start + tile)
            qh = q[span, cols]
            ch = ctx_s[span, cols]
            logits = nt(kh, qh) + bias[h, :length, span]
            if masked:
                logits = jnp.where(query_mask_of(keep_col, length), logits, MASKED)
            probs = jnp.exp(logits - lse[h : h + 1, span])
            pgrad = nt(vh, ch)
            delta = jnp.sum(probs * pgrad, axis=0, keepdims=True)
            lgrad = (probs * (pgrad - delta)).astype(BF)
            dv = dv + nn(probs.astype(BF), ch)
            dk = dk + nn(lgrad, qh)
            dq_o[span, cols] = nn(kt[cols], lgrad).T.astype(BF)
            pieces.append(lgrad)
        dk_o[:, cols] = dk.astype(BF)
        dv_o[:, cols] = dv.astype(BF)
        lgrad = jnp.concatenate(pieces, axis=1) if len(pieces) > 1 else pieces[0]
        diag_o[h : h + 1] = diagonal_sums(lgrad.astype(F32))
    for result in (dq_o, dk_o, dv_o, diag_o):
        result.done()
    part = nn(dq_o[...], wq[...]) + nn(dk_o[...], wk[...]) + nn(dv_o[...], wv[...])
    part_s[...] = part.astype(BF)
    xf = x[...].astype(F32)
    own_sum = jnp.sum(part * (xf * rinv(xf)), axis=0, keepdims=True)
    row = lax.broadcasted_iota(jnp.int32, gain_o.shape, 0)
    gain_o[...] = jnp.where(row == 0, own_sum, gain_sum)
    keep_o[...] = part_s[pl.ds(bases[0], half)]
    send_o[...] = part_s[pl.ds(bases[1], half)]


def attn_bwd(
    chunk, place, tokens, middle, gs, fgrad, heads_kept, bias, gain, wq, wk, wv, wo, keep_col, after
):
    index, length, masked = chunk
    q, k, v, lse = heads_kept
    heads = bias.shape[0]
    cols = q.shape[1]
    width = tokens.shape[1]
    specs = [SMEM, Load(index * length, length), LOAD, PASS, PASS] + [LOAD] * 6 + [PASS] + [LOAD] * 4
    operands = [place, tokens, middle, *gs, fgrad, q, k, v, lse, bias, gain, wq, wk, wv, wo]
    if masked:
        specs.append(PASS)
        operands.append(keep_col)
    small = kept((length, cols), BF)
    part = sds((length // 2, width), BF)
    return call(
        functools.partial(attn_bwd_body, length, masked, heads),
        "attn_bwd",
        (
            kept((length, width), BF),
            small,
            small,
            small,
            sds((8, WIDE), F32),
            sds((8, width), F32),
            part,
            part,
        ),
        specs,
        0.02 * length,
        [pltpu.VMEM((length, cols), BF), pltpu.VMEM((length, width), BF)],
        after=after,
        order=(11, 2, 3, 4, 5, 15, 7, 6, 8, 9, 16, 10, 12, 13, 14, 1),
    )(*operands)


def attn_wgrad_body(count, pieces, *refs):
    place = refs[0]
    normed, dq, dk, dv, agrad, ctx = (refs[1 + i * count : 1 + (i + 1) * count] for i in range(6))
    keep_o, send_o, out = refs[1 + 6 * count :]
    cols = dq[0].shape[1]
    for n, (left, right) in enumerate(((dq, normed), (dk, normed), (dv, normed), (ctx, agrad))):
        total = sum(tn(a[...], b[...]) for a, b in zip(left, right)).astype(BF)
        rows = out.shape[0] // pieces
        relative_store(out, total, place, pieces, rows, n * cols // rows, slice(0, out.shape[1]))
    split_out(out, keep_o, send_o)


def attn_wgrad(place, pieces, normed, dq, dk, dv, agrad, ctx, after):
    count = len(normed)
    width = normed[0].shape[1]
    rows = 4 * dq[0].shape[1]
    part = sds((rows // 2, width), BF)
    return call(
        functools.partial(attn_wgrad_body, count, pieces),
        "attn_wgrad",
        (part, part),
        [SMEM] + [LOAD] * (6 * count),
        6.0,
        [pltpu.VMEM((rows, width), BF)],
        after=after,
    )(place, *normed, *dq, *dk, *dv, *agrad, *ctx)


def tail_body(length, *refs):
    place, x, agrad, nm, no, gain, out = refs
    half = length // 2
    bases = halves(place, half)
    for n, g in enumerate((nm, no)):
        rows = pl.ds(bases[n], half)
        xf = x[rows].astype(F32)
        r = rinv(xf)
        dn = g[...].astype(F32)
        out[rows] = (agrad[rows].astype(F32) + norm_back(xf, r, gain[...], dn)).astype(BF)


def tail(chunk, place, tokens, agrad, ns, gain, so_far, rows, after):
    index, length, _ = chunk
    width = tokens.shape[1]
    specs = [SMEM, Load(index * length, length), LOAD] + [PASS] * 3
    operands = [place, tokens, agrad, *ns, gain]
    return call(
        functools.partial(tail_body, length),
        "tokens_grad",
        (kept((length, width), BF),),
        specs,
        0.005 * length,
        into=(kept((rows, width), BF), index * length, so_far),
        after=after,
        order=(5, 3, 1, 2, 4),
    )(*operands)[0]


def swap(block, axis, distance):
    count = lax.axis_size(axis)
    return lax.ppermute(block, axis, [(i, i ^ distance) for i in range(count)])


def added(a, b):
    return (a.astype(F32) + b.astype(F32)).astype(BF)


def dp_sum(keep, send):
    count = lax.axis_size("dp")
    sizes = []
    distance = 1
    while True:
        total = added(keep, swap(send, "dp", distance))
        distance *= 2
        if distance == count:
            break
        half = total.shape[0] // 2
        keep, send = total[:half], total[half:]
    while distance > 2:
        distance //= 2
        total = jnp.concatenate([total, swap(total, "dp", distance)], axis=0)
    return (total, swap(total, "dp", 1))


def dp_gather(block):
    count = lax.axis_size("dp")
    spread = jnp.broadcast_to(block[None], (count,) + block.shape)
    return lax.all_to_all(spread, "dp", 0, 0, tiled=True)


def on_device(
    doc_tokens,
    query_tokens,
    w_query,
    w_key,
    w_value,
    w_out,
    w_gate,
    w_up,
    w_down,
    w_proj,
    gain_attn,
    gain_ffn,
    gain_final,
    bias_table,
    query_mask,
    retrieval_mask,
    positives,
):
    dp_count = lax.axis_size("dp")
    mp_count = lax.axis_size("mp")
    dp_index = lax.axis_index("dp")
    mp_index = lax.axis_index("mp")
    query_len = query_mask.shape[1]
    docs_here = doc_tokens.shape[0] // DOC_LEN
    queries_here = query_tokens.shape[0] // query_len
    query_total = dp_count * queries_here
    width = doc_tokens.shape[1]
    emb_width = w_proj.shape[1]
    units = w_gate.shape[1]
    lane_count = queries_here // mp_count
    lane_total = lane_count * dp_count
    lane_tokens = lane_total * query_len
    lane_pad = -(-lane_total // 128) * 128
    pieces = 8
    order_here = sum(((dp_index >> bit) & 1) << (2 - bit) for bit in range(3))
    if dp_count != pieces:
        order_here = jnp.zeros_like(dp_index)
    place = jnp.stack([mp_index, mp_index % 2, order_here]).astype(jnp.int32)
    w_query = w_query.T
    w_key = w_key.T
    w_value = w_value.T
    gain_attn = gain_attn.reshape(1, width)
    gain_ffn = gain_ffn.reshape(1, width)
    gain_final = gain_final.reshape(1, width)
    home_keep = lax.dynamic_slice_in_dim(query_mask, dp_index * queries_here, queries_here, 0)
    keep_col = home_keep.astype(F32).reshape(-1, 1)

    def lane_view(whole):
        grouped = whole.reshape((dp_count, queries_here) + whole.shape[1:])
        picked = lax.dynamic_slice_in_dim(grouped, mp_index * lane_count, lane_count, 1)
        return picked.reshape((lane_total,) + whole.shape[1:])

    lane_keep = lane_view(query_mask).astype(F32)
    lane_hits = lane_view(retrieval_mask).astype(F32)
    token_weights = lane_keep[:, :, None] * lane_hits / jnp.sum(lane_keep, axis=1)[:, None, None]
    token_weights = token_weights.reshape(lane_tokens, docs_here).T
    token_weights = jnp.pad(token_weights, ((0, 8 - docs_here), (0, 0)))
    doc_ids = dp_index * docs_here + jnp.arange(8, dtype=jnp.int32)
    doc_ids = jnp.where(jnp.arange(8) < docs_here, doc_ids, -1)
    lane_positive = jnp.pad(lane_view(positives), (0, lane_pad - lane_total), constant_values=-2)
    hot = (lane_positive[None, :] == doc_ids[:, None]).astype(F32)

    chunks = [(0, query_tokens.shape[0], True)] + [(p, DOC_LEN, False) for p in range(docs_here)]
    bias = make_bias(bias_table.T)
    sources = [query_tokens] + [doc_tokens] * docs_here
    line = []
    chain = []

    def grads_sum(keep, send):
        if dp_count == pieces:
            return dp_sum(keep, send)
        return lax.psum((keep, send), "dp")

    def mp_sum(keep, send):
        total = added(keep, swap(send, "mp", 1))
        line.append(total)
        total = added(total, swap(total, "mp", 2))
        return (total, swap(total, "mp", 1))

    def turn():
        return line[-2:-1] + chain[-1:]

    attn = []
    attended = []
    for c, t in zip(chunks, sources):
        a = attn_fwd(
            c, place, t, gain_attn, w_query, w_key, w_value, w_out, bias, keep_col, turn()
        )
        attn.append(a)
        chain.append(a[6])
        attended.append(mp_sum(a[6], a[7]))
    ffn = []
    forwarded = []
    for c, t, u in zip(chunks, sources, attended):
        f = ffn_fwd(c, place, t, *u, gain_ffn, w_gate, w_up, w_down, turn())
        ffn.append(f)
        chain.append(f[2])
        forwarded.append(mp_sum(f[2], f[3]))

    lane_block, output = query_embed(
        place, ffn[0][0], *forwarded[0], gain_final, w_proj, lane_count * query_len
    )
    outputs = [output]
    queries = dp_gather(lane_block).reshape(lane_tokens, emb_width)
    emb = None
    lses = []
    for p in range(docs_here):
        emb, lse, output = doc_embed(
            p, place, ffn[p + 1][0], *forwarded[p + 1], gain_final, w_proj, queries, emb, docs_here
        )
        lses.append(lse)
        outputs.append(output)
    own = stats(lses, token_weights, hot, DOC_LEN)
    gathered = dp_gather(own)
    keep, send, query_part, scalars = score_back(
        place, gathered, own, token_weights, hot, emb, queries, lses, DOC_LEN, lane_total, query_total
    )
    doc_grads = mp_sum(keep, send)
    query_part = query_part.reshape(dp_count, lane_count * query_len, emb_width)
    query_part = lax.all_to_all(query_part, "dp", 0, 0, tiled=True)
    scalars = scalars + swap(scalars, "mp", 1)
    scalars = scalars + swap(scalars, "mp", 2)

    order = list(range(1, docs_here + 1)) + [0]
    back = {}
    middle_back = {}
    line.clear()
    chain.clear()
    for n in order:
        if n == order[1]:
            query_here = query_sum(query_part, chain[-1:])
            query_far = swap(query_here, "mp", 2)
            query_grads = [
                query_here,
                swap(query_here, "mp", 1),
                query_far,
                swap(query_far, "mp", 1),
            ]
        back[n] = ffn_bwd(
            chunks[n],
            place,
            outputs[n],
            query_grads if n == 0 else doc_grads,
            ffn[n][1],
            gain_final,
            w_proj,
            w_gate,
            w_up,
            w_down,
            turn(),
        )
        chain.append(back[n][6])
        middle_back[n] = mp_sum(back[n][6], back[n][7])
    ffn_pack = ffn_wgrad(
        place,
        pieces,
        [ffn[n][1] for n in order],
        *[[back[n][i] for n in order] for i in range(5)],
        turn(),
    )
    chain.append(ffn_pack[0])
    wide_pack = grads_sum(*ffn_pack[:2])
    down_pack = grads_sum(*ffn_pack[2:])
    attn_back = {}
    inputs_back = {}
    for n in order:
        attn_back[n] = attn_bwd(
            chunks[n],
            place,
            sources[n],
            ffn[n][0],
            middle_back[n],
            back[n][0],
            (attn[n][1], attn[n][2], attn[n][3], attn[n][4]),
            bias,
            gain_ffn,
            w_query,
            w_key,
            w_value,
            w_out,
            keep_col,
            turn(),
        )
        chain.append(attn_back[n][6])
        inputs_back[n] = mp_sum(attn_back[n][6], attn_back[n][7])
    attn_pack = attn_wgrad(
        place,
        pieces,
        [attn[n][0] for n in order],
        [attn_back[n][1] for n in order],
        [attn_back[n][2] for n in order],
        [attn_back[n][3] for n in order],
        [attn_back[n][0] for n in order],
        [attn[n][5] for n in order],
        turn(),
    )
    chain.append(attn_pack[0])
    tokens_grad = None
    for n in order[:-1]:
        tokens_grad = tail(
            chunks[n],
            place,
            sources[n],
            attn_back[n][0],
            inputs_back[n],
            gain_attn,
            tokens_grad,
            doc_tokens.shape[0],
            turn(),
        )
    query_tokens_grad = tail(
        chunks[0],
        place,
        sources[0],
        attn_back[0][0],
        inputs_back[0],
        gain_attn,
        None,
        query_tokens.shape[0],
        turn(),
    )

    own_gain = sum(attn_back[n][5] for n in order)[:1]
    own_gain = own_gain + swap(own_gain, "mp", 1)
    own_gain = own_gain + swap(own_gain, "mp", 2)
    small = jnp.concatenate(
        [
            own_gain,
            sum(attn_back[n][5] for n in order)[1:2],
            sum(back[n][5] for n in order)[:1],
        ],
        axis=0,
    )
    diag = sum(attn_back[n][4] for n in order)
    small = jnp.concatenate([small, jnp.zeros((5, width), F32)], axis=0)
    small = jnp.concatenate([small, diag], axis=1)
    distance = 1
    while distance < dp_count:
        small = small + swap(small, "dp", distance)
        distance *= 2
    diag = small[:, width:]
    attn_pack = grads_sum(*attn_pack)
    cols = w_query.shape[0]
    ffn_grads = unpack(
        place, pieces, wide_pack, cut_lanes, [(width, units), (width, units), (width, emb_width)]
    )
    down_grad = unpack(place, pieces, down_pack, cut_lanes, [(units, width)])
    attn_grads = unpack(place, pieces, attn_pack, cut_rows, [(cols, width)] * 4)

    lane = jnp.arange(WIDE, dtype=jnp.int32)
    offset = jnp.where(lane < DOC_LEN, -lane, WIDE - lane)
    distance = jnp.abs(offset)
    far = 8 + sum(((distance >= edge).astype(jnp.int32) for edge in EDGES))
    index = jnp.where(distance < 8, distance, far) + 16 * (offset > 0).astype(jnp.int32)
    onehot = (jnp.arange(bias_table.shape[0], dtype=jnp.int32)[:, None] == index[None]).astype(F32)
    grad_bias = lax.dot_general(
        onehot, diag[: bias_table.shape[1]], (((1,), (1,)), ((), ())), precision=HIGH
    )
    return (
        scalars[0, 0],
        scalars[1, 0],
        emb,
        tokens_grad,
        query_tokens_grad,
        attn_grads[0].T,
        attn_grads[1].T,
        attn_grads[2].T,
        attn_grads[3],
        ffn_grads[0],
        ffn_grads[1],
        down_grad[0],
        ffn_grads[2],
        small[0, :width],
        small[1, :width],
        small[2, :width],
        grad_bias,
    )


def solution(mesh):
    placed = (
        P("dp", None),
        P("dp", None),
        P(None, "mp"),
        P(None, "mp"),
        P(None, "mp"),
        P("mp", None),
        P(None, "mp"),
        P(None, "mp"),
        P("mp", None),
        P(),
        P(),
        P(),
        P(),
        P(None, "mp"),
        P(),
        P(None, None, "dp"),
        P(),
    )
    return jax.shard_map(
        on_device,
        mesh=mesh,
        in_specs=placed,
        out_specs=(
            P(),
            P(),
            P("dp", None),
            P("dp", None),
            P("dp", None),
            P(None, "mp"),
            P(None, "mp"),
            P(None, "mp"),
            P("mp", None),
            P(None, "mp"),
            P(None, "mp"),
            P("mp", None),
            P(),
            P(),
            P(),
            P(),
            P(None, "mp"),
        ),
        check_vma=False,
    )
```

```python
import functools
import math

import jax
import jax.numpy as jnp
from jax import lax
from jax.experimental import pallas as pl
from jax.experimental.pallas import tpu as pltpu
from jax.sharding import PartitionSpec as P

DOC_LEN = 512
EPS = 1e-06
DOC_TEMP = 32.0
EDGES = (12, 16, 23, 32, 46, 64, 91)
HIGH = lax.Precision.HIGHEST
MASKED = -1000000000.0
BF = jnp.bfloat16
F32 = jnp.float32
WIDE = 2 * DOC_LEN
GELU_A = math.sqrt(2.0 / math.pi)
GELU_B = 0.044715


def nn(a, b):
    return jnp.dot(a, b, preferred_element_type=F32)


def nt(a, b):
    return lax.dot_general(a, b, (((1,), (1,)), ((), ())), preferred_element_type=F32)


def tn(a, b):
    return lax.dot_general(a, b, (((0,), (0,)), ((), ())), preferred_element_type=F32)


def rinv(v):
    return lax.rsqrt(jnp.mean(v * v, axis=-1, keepdims=True) + EPS)


def norm_back(v, r, gain, grad):
    scaled = grad * gain
    return r * scaled - v * (r * r * r * jnp.mean(scaled * v, axis=-1, keepdims=True))


def rowsum8(v):
    return jnp.broadcast_to(jnp.sum(v, axis=0, keepdims=True), (8, v.shape[1]))


def halves(place, half):
    mine = pl.multiple_of(place[1] * half, half)
    other = pl.multiple_of((1 - place[1]) * half, half)
    return (mine, other)


class Load:
    def __init__(self, start=0, rows=None, pinned=True):
        self.start = start
        self.rows = rows
        self.pinned = pinned

    def shape(self, operand):
        return operand.shape if self.rows is None else (self.rows,) + operand.shape[1:]

    def of(self, ref):
        return ref if self.rows is None else ref.at[pl.ds(self.start, self.rows)]


class Held:
    def __init__(self, ref, copy):
        self.ref = ref
        self.copy = copy
        self.begun = False

    @property
    def shape(self):
        return self.ref.shape

    @property
    def dtype(self):
        return self.ref.dtype


class Operand(Held):
    def ready(self):
        if not self.begun:
            self.begun = True
            self.copy.wait()
        return self.ref

    def __getitem__(self, at):
        return self.ready()[at]


class Result(Held):
    def __getitem__(self, at):
        return self.ref[at]

    def __setitem__(self, at, value):
        self.ref[at] = value

    def done(self):
        if not self.begun:
            self.begun = True
            self.copy.start()


LOAD = Load()
PASS = Load(pinned=False)
SMEM = pl.BlockSpec(memory_space=pltpu.SMEM)
FAR = pl.BlockSpec(memory_space=pltpu.HBM)


def sds(shape, dtype):
    return jax.ShapeDtypeStruct(shape, dtype)


class Kept:
    def __init__(self, shape, dtype):
        self.shape = shape
        self.dtype = dtype


def kept(shape, dtype):
    return Kept(shape, dtype)


def call(body, name, outs, in_specs, micros, scratch=(), into=None, after=(), order=()):
    count = len(outs)
    stores = [LOAD] * count
    out_shape = list(outs)
    begun = []
    for k, (whole, start, so_far) in (into or {}).items():
        out_shape[k] = whole
        stores[k] = Load(start, outs[k].shape[0])
        if so_far is not None:
            begun.append((k, so_far))
    after = [so_far for _, so_far in begun] + list(after)

    def run(*operands):
        pinned = [
            pltpu.with_memory_space_constraint(operand, pltpu.HBM) if isinstance(spec, Load) and spec.pinned else operand
            for spec, operand in zip(in_specs, operands)
        ]
        loads = [n for n, spec in enumerate(in_specs) if isinstance(spec, Load)]
        total = len(loads)
        given = len(operands)
        buffers = [
            pltpu.VMEM(in_specs[n].shape(operands[n]), operands[n].dtype) for n in loads
        ] + [pltpu.VMEM(out.shape, out.dtype) for out in outs]

        def kernel(*refs):
            ins = list(refs[:given])
            results = refs[given + len(after) : given + len(after) + count]
            rest = refs[given + len(after) + count :]
            own, held, sems = rest[: len(scratch)], rest[len(scratch) : -1], rest[-1]
            for n in sorted(loads, key=lambda n: order.index(n) if n in order else given + n):
                k = loads.index(n)
                copy = pltpu.make_async_copy(in_specs[n].of(ins[n]), held[k], sems.at[k])
                copy.start()
                ins[n] = Operand(held[k], copy)
            made = []
            for k, result in enumerate(results):
                buffer = held[total + k]
                copy = pltpu.make_async_copy(buffer, stores[k].of(result), sems.at[total + k])
                made.append(Result(buffer, copy))
            body(*ins, *made, *own)
            for n in loads:
                ins[n].ready()
            for result in made:
                result.done()
            for result in made:
                result.copy.wait()

        return pl.pallas_call(
            kernel,
            name=name,
            out_shape=tuple(
                pltpu.HBM(out.shape, out.dtype) if isinstance(out, Kept) else out for out in out_shape
            ),
            in_specs=[FAR if isinstance(spec, Load) else spec for spec in in_specs]
            + [FAR] * len(after),
            out_specs=(FAR,) * count,
            scratch_shapes=list(scratch) + buffers + [pltpu.SemaphoreType.DMA((total + count,))],
            input_output_aliases={given + n: k for n, (k, _) in enumerate(begun)},
            compiler_params=pltpu.CompilerParams(vmem_limit_bytes=48 * 1024 * 1024),
            cost_estimate=pl.CostEstimate(
                flops=int(micros * 2e8), bytes_accessed=int(micros * 1e5), transcendentals=0
            ),
        )(*pinned, *after)

    return run


def bias_into(table, out):
    lane = lax.broadcasted_iota(jnp.int32, (8, WIDE), 1)
    offset = jnp.where(lane < DOC_LEN, -lane, WIDE - lane)
    distance = jnp.abs(offset)
    far = jnp.full_like(distance, 8)
    for edge in EDGES:
        far = far + (distance >= edge).astype(jnp.int32)
    index = jnp.where(distance < 8, distance, far) + jnp.where(offset > 0, 16, 0)
    for head in range(out.shape[0]):
        row = jnp.zeros((8, WIDE), F32)
        for bucket in range(table.shape[1]):
            row = jnp.where(index == bucket, table[head, bucket], row)
        spread = jnp.broadcast_to(row[:1], (DOC_LEN, WIDE))
        rolled = pltpu.roll(spread, 0, 1, stride=1, stride_axis=0)
        out[head] = rolled[:, :DOC_LEN]


def make_bias(table):
    return call(
        bias_into,
        "rel_bias",
        (kept((table.shape[0], DOC_LEN, DOC_LEN), F32),),
        [SMEM],
        2.0,
    )(table)[0]


def attn_fwd_body(length, masked, heads, *refs):
    place, x, gain, wq, wk, wv, wo, bias = refs[:8]
    pos = 8
    keep_col = None
    if masked:
        keep_col = refs[8]
        pos = 9
    normed_o, q_o, k_o, v_o, lse_o, ctx_o, keep_o, send_o, part_s = refs[pos:]
    half = length // 2
    xf = x[...].astype(F32)
    normed = (xf * rinv(xf) * gain[...]).astype(BF)
    normed_o[...] = normed
    normed_o.done()
    q = nt(normed, wq[...]).astype(BF)
    k = nt(normed, wk[...]).astype(BF)
    v = nt(normed, wv[...]).astype(BF)
    q_o[...] = q
    k_o[...] = k
    v_o[...] = v
    for result in (q_o, k_o, v_o):
        result.done()
    width = q.shape[1] // heads
    vt = v.T
    tile = min(length, 256)
    lse_o[...] = jnp.zeros(lse_o.shape, F32)
    for h in range(heads):
        cols = slice(h * width, (h + 1) * width)
        for start in range(0, length, tile):
            span = slice(start, start + tile)
            logits = nt(k[:, cols], q[span, cols]) + bias[h, :length, span]
            if masked:
                logits = jnp.where(query_mask_of(keep_col, length), logits, MASKED)
            top = jnp.max(logits, axis=0, keepdims=True)
            shifted = jnp.exp(logits - top)
            total = jnp.sum(shifted, axis=0, keepdims=True)
            probs = (shifted * (1.0 / total)).astype(BF)
            ctx_t = nn(vt[cols], probs)
            ctx_o[span, cols] = ctx_t.T.astype(BF)
            lse_o[h : h + 1, span] = top + jnp.log(total)
    ctx_o.done()
    lse_o.done()
    part_s[...] = nn(ctx_o[...], wo[...]).astype(BF)
    mine, other = halves(place, half)
    keep_o[...] = part_s[pl.ds(mine, half)]
    send_o[...] = part_s[pl.ds(other, half)]


def query_mask_of(keep_col, length):
    key_row = lax.broadcasted_iota(jnp.int32, (length, length), 0)
    query_row = lax.broadcasted_iota(jnp.int32, (length, length), 1)
    return ((key_row // 32) == (query_row // 32)) & (keep_col[...] > 0)


def attn_fwd(chunk, place, tokens, gain, wq, wk, wv, wo, bias, keep_col, after):
    index, length, masked = chunk
    heads = bias.shape[0]
    cols = wq.shape[0]
    width = tokens.shape[1]
    specs = [SMEM, Load(index * length, length), PASS] + [LOAD] * 5
    operands = [place, tokens, gain, wq, wk, wv, wo, bias]
    if masked:
        specs.append(PASS)
        operands.append(keep_col)
    small = kept((length, cols), BF)
    part = sds((length // 2, width), BF)
    return call(
        functools.partial(attn_fwd_body, length, masked, heads),
        "attn_fwd",
        (kept((length, width), BF), small, small, small, kept((8, length), F32), small, part, part),
        specs,
        0.012 * length,
        [pltpu.VMEM((length, width), BF)],
        after=after,
    )(*operands)


def gelu_parts(gate):
    t = jnp.tanh(GELU_A * (gate + GELU_B * gate * gate * gate))
    return 0.5 * gate * (1.0 + t), t


def ffn_fwd_body(length, place, x, um, uo, gain, wg, wu, wd, middle_o, normed_o, keep_o, send_o):
    half = length // 2
    bases = halves(place, half)
    for n, (u, out) in enumerate(((um, keep_o), (uo, send_o))):
        middle = x[pl.ds(bases[n], half)].astype(F32) + u[...].astype(F32)
        middle_o[n * half : (n + 1) * half] = middle
        normed = (middle * rinv(middle) * gain[...]).astype(BF)
        normed_o[n * half : (n + 1) * half] = normed
        if n == 1:
            middle_o.done()
            normed_o.done()
        act, _ = gelu_parts(nn(normed, wg[...]))
        hidden = (act * nn(normed, wu[...])).astype(BF)
        out[...] = nn(hidden, wd[...]).astype(BF)


def ffn_fwd(chunk, place, tokens, um, uo, gain, wg, wu, wd, after):
    index, length, _ = chunk
    width = tokens.shape[1]
    part = sds((length // 2, width), BF)
    return call(
        functools.partial(ffn_fwd_body, length),
        "ffn_fwd",
        (kept((length, width), F32), kept((length, width), BF), part, part),
        [SMEM, Load(index * length, length)] + [PASS] * 3 + [LOAD] * 3,
        0.01 * length,
        after=after,
        order=(4, 2, 1, 5, 6, 7, 3),
    )(place, tokens, um, uo, gain, wg, wu, wd)


def embed_rows(length, place, middle, fs, gain, wp, emb_s, out_o):
    half = length // 2
    bases = halves(place, half)
    for n in range(2):
        span = slice(n * half, (n + 1) * half)
        out = middle[span] + fs[n][...].astype(F32)
        out_o[span] = out
        if n == 1:
            out_o.done()
        normed = (out * rinv(out) * gain[...]).astype(BF)
        emb_s[pl.ds(bases[n], half)] = nn(normed, wp[...]).astype(BF)


def query_embed_body(length, lane, place, middle, fm, fo, gain, wp, lane_o, out_o, emb_s):
    embed_rows(length, place, middle, (fm, fo), gain, wp, emb_s, out_o)
    lane_o[...] = emb_s[pl.ds(pl.multiple_of(place[0] * lane, lane), lane)]


def query_embed(place, middle, fm, fo, gain, wp, lane, after):
    length = middle.shape[0]
    emb = wp.shape[1]
    return call(
        functools.partial(query_embed_body, length, lane),
        "query_embed",
        (sds((lane, emb), BF), kept(middle.shape, F32)),
        [SMEM, LOAD] + [PASS] * 3 + [LOAD],
        0.004 * length,
        [pltpu.VMEM((length, emb), BF)],
        after=after,
    )(place, middle, fm, fo, gain, wp)


def lane_tile(tokens):
    return min(tokens, 512)


def doc_embed_body(length, place, middle, fm, fo, gain, wp, queries, emb_o, lse_o, out_o):
    embed_rows(length, place, middle, (fm, fo), gain, wp, emb_o, out_o)
    emb_o.done()
    scale = wp.shape[1] ** (-0.5)
    tile = lane_tile(queries.shape[0])
    for start in range(0, queries.shape[0], tile):
        span = slice(start, start + tile)
        scores = nt(emb_o[...], queries[span]) * scale
        top = jnp.max(scores, axis=0, keepdims=True)
        total = jnp.sum(jnp.exp(scores - top), axis=0, keepdims=True)
        lse_o[:, span] = jnp.broadcast_to(top + jnp.log(total), (8, tile))


def doc_embed(index, place, middle, fm, fo, gain, wp, queries, so_far, docs):
    length = middle.shape[0]
    emb = wp.shape[1]
    return call(
        functools.partial(doc_embed_body, length),
        "doc_embed",
        (kept((length, emb), BF), sds((8, queries.shape[0]), F32), kept(middle.shape, F32)),
        [SMEM, LOAD] + [PASS] * 3 + [LOAD, PASS],
        0.005 * length,
        into={0: (kept((docs * length, emb), BF), index * length, so_far)},
        order=(4, 2, 1, 5, 6, 3),
    )(place, middle, fm, fo, gain, wp, queries)


def segment(tokens, lanes):
    token = lax.broadcasted_iota(jnp.int32, (tokens, lanes), 0) // 32
    return (token == lax.broadcasted_iota(jnp.int32, (tokens, lanes), 1)).astype(F32)


def stats_body(docs, doc_len, *refs):
    lses = refs[:docs]
    weights, hot, out = refs[docs:]
    lanes = hot.shape[1]
    tokens = weights.shape[1]
    seg = segment(tokens, lanes)
    w = weights[...]
    rows = lax.broadcasted_iota(jnp.int32, (8, tokens), 0)
    scores = jnp.zeros((8, tokens), F32)
    for p in range(docs):
        scores = jnp.where(rows == p, lses[p][...], scores)
    scores = w * (scores - jnp.where(rows < docs, math.log(doc_len), 0.0))
    table = DOC_TEMP * jnp.dot(scores, seg, precision=HIGH, preferred_element_type=F32)
    share = jnp.dot(w, seg, precision=HIGH, preferred_element_type=F32)
    lane_rows = lax.broadcasted_iota(jnp.int32, (8, lanes), 0)
    positive = jnp.sum(table * hot[...], axis=0, keepdims=True)
    share = jnp.sum(share * hot[...], axis=0, keepdims=True)
    result = jnp.where(lane_rows < docs, table, 0.0)
    result = jnp.where(lane_rows == docs, positive, result)
    out[...] = jnp.where(lane_rows == docs + 1, share, result)


def stats(lses, weights, hot, doc_len):
    return call(
        functools.partial(stats_body, len(lses), doc_len),
        "doc_stats",
        (sds(hot.shape, F32),),
        [PASS] * (len(lses) + 2),
        0.5,
    )(*lses, weights, hot)[0]


def score_back_body(docs, doc_len, lane_total, query_total, *refs):
    place, gathered, own, weights, hot, emb, queries = refs[:7]
    lses = refs[7 : 7 + docs]
    keep_o, send_o, query_o, scalars_o, doc_s, query_s = refs[7 + docs :]
    lanes = hot.shape[1]
    tokens = weights.shape[1]
    everything = gathered[...]
    rows = lax.broadcasted_iota(jnp.int32, everything.shape, 1)
    scores = jnp.where(rows < docs, everything, -jnp.inf)
    top = jnp.max(jnp.max(scores, axis=0), axis=0, keepdims=True)
    total = jnp.sum(jnp.sum(jnp.exp(scores - top[None]), axis=0), axis=0, keepdims=True)
    log_norm = top + jnp.log(total)
    summed = jnp.sum(everything, axis=0)
    valid = lax.broadcasted_iota(jnp.int32, (1, lanes), 1) < lane_total
    loss = jnp.where(valid, log_norm - summed[docs : docs + 1], 0.0)
    share = jnp.where(valid, summed[docs + 1 : docs + 2], 0.0)
    out_rows = lax.broadcasted_iota(jnp.int32, (8, 128), 0)
    loss = jnp.sum(loss, axis=1, keepdims=True) / query_total
    share = jnp.sum(share, axis=1, keepdims=True) / query_total
    scalars_o[...] = jnp.where(out_rows == 0, loss, share)
    own_rows = lax.broadcasted_iota(jnp.int32, own.shape, 0)
    grads = DOC_TEMP * (jnp.exp(own[...] - log_norm) - hot[...]) / query_total
    grads = jnp.where(own_rows < docs, grads, 0.0)
    seg = segment(tokens, lanes)
    spread = lax.dot_general(
        grads, seg, (((1,), (1,)), ((), ())), precision=HIGH, preferred_element_type=F32
    )
    token_grad = spread * weights[...]
    emb_width = queries.shape[1]
    scale = emb_width ** (-0.5)
    half = doc_len // 2
    bases = halves(place, half)
    tile = lane_tile(tokens)
    for start in range(0, tokens, tile):
        span = slice(start, start + tile)
        query = queries[span]
        query_grad = jnp.zeros((emb_width, tile), F32)
        for p in range(docs):
            doc = emb[p * doc_len : (p + 1) * doc_len]
            scores = nt(doc, query) * scale
            grad = (token_grad[p : p + 1, span] * jnp.exp(scores - lses[p][:1, span])).astype(BF)
            part = nn(grad, query) * scale
            if start == 0:
                doc_s[p * doc_len : (p + 1) * doc_len] = part
            else:
                doc_s[p * doc_len : (p + 1) * doc_len] += part
            query_grad = query_grad + nn(doc.T, grad)
        query_o[span] = (query_grad * scale).T.astype(BF)
    for p in range(docs):
        keep_o[p * half : (p + 1) * half] = doc_s[pl.ds(p * doc_len + bases[0], half)].astype(BF)
        send_o[p * half : (p + 1) * half] = doc_s[pl.ds(p * doc_len + bases[1], half)].astype(BF)


def score_back(place, gathered, own, weights, hot, emb, queries, lses, doc_len, lane_total, query_total):
    docs = len(lses)
    width = emb.shape[1]
    part = sds((docs * doc_len // 2, width), BF)
    return call(
        functools.partial(score_back_body, docs, doc_len, lane_total, query_total),
        "score_back",
        (part, part, sds(queries.shape, BF), sds((8, 128), F32)),
        [SMEM] + [PASS] * 4 + [LOAD] + [PASS] * (1 + docs),
        3.0,
        [pltpu.VMEM((docs * doc_len, width), F32), pltpu.VMEM((8, 128), F32)],
    )(place, gathered, own, weights, hot, emb, queries, *lses)


def query_sum_body(parts, out):
    out[...] = jnp.sum(parts[...].astype(F32), axis=0).astype(BF)


def query_sum(parts, after):
    return call(
        query_sum_body, "query_sum", (sds(parts.shape[1:], BF),), [PASS], 1.5, after=after
    )(parts)[0]


def ffn_bwd_body(lengths, pieces, *refs):
    refs = list(refs)
    count = len(lengths)

    def take(number):
        taken = refs[:number]
        del refs[:number]
        return taken

    (place,) = take(1)
    finals, normeds = take(count), take(count)
    doc_mine, doc_other = take(2)
    query_grads = take(4)
    gain_final, wp, wg, wu, wd = take(5)
    fgrads = take(count)
    keeps, sends = take(2), take(2)
    gain_o, wide_keep, wide_send, down_keep, down_send = take(5)
    emb_s, hidden, ggrad, ugrad, wide_s, down_s = refs
    width = finals[0].shape[1]
    units = hidden.shape[1]
    gain_sum = jnp.zeros((1, width), F32)
    proj = jnp.zeros((wp.shape[1], width), F32)
    at = 0
    part_at = [0, 0]
    for c, length in enumerate(lengths):
        half = length // 2
        bases = halves(place, half)
        if c == count - 1:
            lane = query_grads[0].shape[0]
            for step, grad in enumerate(query_grads):
                emb_s[pl.ds(pl.multiple_of((place[0] ^ step) * lane, lane), lane)] = grad[...]
            egs = [emb_s[pl.ds(base, half)] for base in bases]
        else:
            egs = [grad[c * half : (c + 1) * half] for grad in (doc_mine, doc_other)]
        group = 0 if c < 2 else 1
        for n, out in enumerate((keeps[group], sends[group])):
            span = slice(n * half, (n + 1) * half)
            rows = slice(at + n * half, at + (n + 1) * half)
            output = finals[c][span]
            r = rinv(output)
            dn = nt(egs[n], wp[...])
            unit = output * r
            gain_sum = gain_sum + jnp.sum(dn * unit, axis=0, keepdims=True)
            proj = proj + nn(egs[n].T, (unit * gain_final[...]).astype(BF))
            fgrad = norm_back(output, r, gain_final[...], dn).astype(BF)
            fgrads[c][span] = fgrad
            if n == 1:
                fgrads[c].done()
            gate = nn(normeds[c][span], wg[...])
            up = nn(normeds[c][span], wu[...])
            act, t = gelu_parts(gate)
            hidden[rows] = (act * up).astype(BF)
            hgrad = nt(fgrad, wd[...])
            slope = 0.5 * (1.0 + t) + 0.5 * gate * (1.0 - t * t) * (
                GELU_A * (1.0 + 3.0 * GELU_B * gate * gate)
            )
            gg = (hgrad * up * slope).astype(BF)
            ug = (hgrad * act).astype(BF)
            ggrad[rows] = gg
            ugrad[rows] = ug
            out[part_at[group] : part_at[group] + half] = (
                nt(gg, wg[...]) + nt(ug, wu[...])
            ).astype(BF)
        at += length
        part_at[group] += half
        if c == 1 or c == count - 1:
            sends[group].done()
            keeps[group].done()
    gain_o[...] = jnp.broadcast_to(gain_sum, gain_o.shape)
    starts = [sum(lengths[:c]) for c in range(count)]

    def total(left, right, span):
        return sum(
            tn(a[:, span], right[starts[c] : starts[c] + lengths[c]]) for c, a in enumerate(left)
        ).astype(BF)

    rows = width // pieces
    for lanes, grads in ((slice(0, units), ggrad), (slice(units, 2 * units), ugrad)):
        for start in range(0, width, 4 * rows):
            value = total(normeds, grads, slice(start, start + 4 * rows))
            relative_store(wide_s, value, place, pieces, rows, start // rows, lanes)
    lanes = slice(2 * units, wide_s.shape[1])
    relative_store(wide_s, proj.T.astype(BF), place, pieces, rows, 0, lanes)
    split_out(wide_s, wide_keep, wide_send)
    wide_send.done()
    wide_keep.done()
    rows = units // pieces
    for start in range(0, units, 4 * rows):
        span = slice(start, start + 4 * rows)
        value = sum(
            tn(hidden[starts[c] : starts[c] + lengths[c], span], fgrads[c][...])
            for c in range(count)
        ).astype(BF)
        relative_store(down_s, value, place, pieces, rows, start // rows, slice(0, width))
    split_out(down_s, down_keep, down_send)


def ffn_bwd(lengths, pieces, place, finals, normeds, doc_grads, query_grads, gain, wp, wg, wu, wd):
    count = len(lengths)
    width = finals[0].shape[1]
    emb = wp.shape[1]
    units = wg.shape[1]
    rows = sum(lengths)
    first = sds((sum(lengths[:2]) // 2, width), BF)
    rest = sds((sum(lengths[2:]) // 2, width), BF)
    wide = sds((width // 2, 2 * units + emb), BF)
    down = sds((units // 2, width), BF)
    inner = pltpu.VMEM((rows, units), BF)
    gates = 1 + 2 * count
    order = [gates + 6, gates, gates + 1, gates + 7, 1, 1 + count, gates + 8, gates + 9, gates + 10]
    return call(
        functools.partial(ffn_bwd_body, lengths, pieces),
        "ffn_bwd",
        tuple(kept((length, width), BF) for length in lengths)
        + (first, rest, first, rest, sds((8, width), F32), wide, wide, down, down),
        [SMEM] + [LOAD] * (2 * count) + [PASS] * 7 + [LOAD] * 4,
        30.0,
        [
            pltpu.VMEM((lengths[-1], emb), BF),
            inner,
            inner,
            inner,
            pltpu.VMEM((width, 2 * units + emb), BF),
            pltpu.VMEM((units, width), BF),
        ],
        order=order,
    )(place, *finals, *normeds, *doc_grads, *query_grads, gain, wp, wg, wu, wd)


def relative_store(out, value, place, pieces, rows, first, lanes):
    for n in range(value.shape[0] // rows):
        slot = reversed_bits(first + n, pieces) ^ place[2]
        out[pl.ds(pl.multiple_of(slot * rows, rows), rows), lanes] = value[n * rows : (n + 1) * rows]


def reversed_bits(number, count):
    result = 0
    while count > 1:
        result = result * 2 + number % 2
        number //= 2
        count //= 2
    return result


def split_out(out, keep_o, send_o):
    half = out.shape[0] // 2
    keep_o[...] = out[:half]
    send_o[...] = out[half:]


def unpack_body(pieces, rows, count, cut, *refs):
    place = refs[0]
    parts = [part.ready() for part in refs[1 : 1 + count]]
    outs = refs[1 + count :]
    for number in range(pieces):
        slot = reversed_bits(number, pieces) ^ place[2]
        for part, base in zip(parts, (0, pieces // 2)):

            @pl.when((slot >= base) & (slot < base + part.shape[0] // rows))
            def _(part=part, base=base):
                start = pl.multiple_of((slot - base) * rows, rows)
                value = part[pl.ds(start, rows)].astype(F32)
                cut(outs, number * rows, rows, value)


def cut_lanes(outs, at, rows, value):
    lane = 0
    for out in outs:
        out[at : at + rows] = value[:, lane : lane + out.shape[1]]
        lane += out.shape[1]


def cut_rows(outs, at, rows, value):
    n, at = divmod(at, outs[0].shape[0])
    outs[n][at : at + rows] = value


def unpack(place, pieces, parts, cut, shapes):
    rows = sum(part.shape[0] for part in parts) // pieces
    return call(
        functools.partial(unpack_body, pieces, rows, len(parts), cut),
        "unpack",
        tuple(kept(shape, F32) for shape in shapes),
        [SMEM] + [PASS] * len(parts),
        2.0,
    )(place, *parts)


def diagonal_sums(block):
    length = block.shape[0]
    rows = length
    value = jnp.concatenate([block, jnp.zeros((rows, WIDE - length), F32)], axis=1)
    while rows > 8:
        rows //= 2
        value = value[:rows] + pltpu.roll(value[rows:], WIDE - rows, 1)
    total = value[0:1]
    for s in range(1, 8):
        total = total + pltpu.roll(jnp.broadcast_to(value[s : s + 1], (8, WIDE)), WIDE - s, 1)[:1]
    return total


def attn_bwd_chunk(place, length, masked, heads, ins, shared, outs, sums, base, ctx_s):
    x, mid, gm, go, g_at, fgrad, q, k, v, lse = ins
    bias, gain, wq, wk, wv, wo, keep_col = shared
    agrad_o, dq_o, dk_o, dv_o, keep_o, send_o = outs
    half = length // 2
    bases = halves(place, half)
    for n, g in enumerate((gm, go)):
        rows = pl.ds(bases[n], half)
        middle = mid[n * half : (n + 1) * half]
        r = rinv(middle)
        dn = g[g_at : g_at + half].astype(F32)
        sums["ffn"] = sums["ffn"] + jnp.sum(dn * (middle * r), axis=0, keepdims=True)
        grad = fgrad[n * half : (n + 1) * half].astype(F32) + norm_back(middle, r, gain[...], dn)
        agrad = grad.astype(BF)
        agrad_o[rows] = agrad
        ctx_s[rows] = nt(agrad, wo[...]).astype(BF)
    agrad_o.done()
    width = q.shape[1] // heads
    tile = min(length, 256)
    kt = k[...].T
    for h in range(heads):
        cols = slice(h * width, (h + 1) * width)
        kh = k[:, cols]
        vh = v[:, cols]
        dk = jnp.zeros((length, width), F32)
        dv = jnp.zeros((length, width), F32)
        pieces = []
        for start in range(0, length, tile):
            span = slice(start, start + tile)
            qh = q[span, cols]
            ch = ctx_s[span, cols]
            logits = nt(kh, qh) + bias[h, :length, span]
            if masked:
                logits = jnp.where(query_mask_of(keep_col, length), logits, MASKED)
            probs = jnp.exp(logits - lse[h : h + 1, span])
            pgrad = nt(vh, ch)
            delta = jnp.sum(probs * pgrad, axis=0, keepdims=True)
            lgrad = (probs * (pgrad - delta)).astype(BF)
            dv = dv + nn(probs.astype(BF), ch)
            dk = dk + nn(lgrad, qh)
            dq_o[span, cols] = nn(kt[cols], lgrad).T.astype(BF)
            pieces.append(lgrad)
        dk_o[:, cols] = dk.astype(BF)
        dv_o[:, cols] = dv.astype(BF)
        lgrad = jnp.concatenate(pieces, axis=1) if len(pieces) > 1 else pieces[0]
        sums["diag"][h] = sums["diag"][h] + diagonal_sums(lgrad.astype(F32))
    for result in (dq_o, dk_o, dv_o):
        result.done()
    part = nn(dq_o[...], wq[...]) + nn(dk_o[...], wk[...]) + nn(dv_o[...], wv[...])
    xf = x[...].astype(F32)
    sums["attn"] = sums["attn"] + jnp.sum(part * (xf * rinv(xf)), axis=0, keepdims=True)
    return part.astype(BF)


def attn_bwd_body(group, heads, pieces, weights, *refs):
    refs = list(refs)
    size = len(group)
    others = weights - size if weights else 0

    def take(number):
        taken = refs[:number]
        del refs[:number]
        return taken

    (place,) = take(1)
    x, mid, fgrad, q, k, v, lse = (take(size) for _ in range(7))
    gm, go, bias, gain, wq, wk, wv, wo, keep_col = take(9)
    earlier = [take(others) for _ in range(4)]
    normed, ctx = take(weights), take(weights)
    agrad, dq, dk, dv = (take(size) for _ in range(4))
    keep_o, send_o, diag_o, gain_o = take(4)
    packs = take(2) if weights else None
    ctx_s, part_s = take(2)
    width = x[0].shape[1]
    sums = {
        "ffn": jnp.zeros((1, width), F32),
        "attn": jnp.zeros((1, width), F32),
        "diag": [jnp.zeros((1, WIDE), F32)] * heads,
    }
    at = 0
    for c, (length, masked) in enumerate(group):
        half = length // 2
        part = attn_bwd_chunk(
            place,
            length,
            masked,
            heads,
            (x[c], mid[c], gm, go, at, fgrad[c], q[c], k[c], v[c], lse[c]),
            (bias, gain, wq, wk, wv, wo, keep_col),
            (agrad[c], dq[c], dk[c], dv[c], keep_o, send_o),
            sums,
            at,
            ctx_s,
        )
        part_s[:length] = part
        bases = halves(place, half)
        keep_o[at : at + half] = part_s[pl.ds(bases[0], half)]
        send_o[at : at + half] = part_s[pl.ds(bases[1], half)]
        at += half
    send_o.done()
    keep_o.done()
    diag_o[...] = jnp.zeros(diag_o.shape, F32)
    for h in range(heads):
        diag_o[h : h + 1] = sums["diag"][h]
    row = lax.broadcasted_iota(jnp.int32, gain_o.shape, 0)
    gain_o[...] = jnp.where(row == 0, sums["attn"], sums["ffn"])
    if weights:
        pack_s = refs[0]
        cols = q[0].shape[1]
        rows = pack_s.shape[0] // pieces
        every = [old + new for old, new in zip(earlier, (dq, dk, dv, agrad))]
        pairs = ((every[0], normed), (every[1], normed), (every[2], normed), (ctx, every[3]))
        for n, (left, right) in enumerate(pairs):
            total = sum(tn(a[...], b[...]) for a, b in zip(left, right)).astype(BF)
            relative_store(pack_s, total, place, pieces, rows, n * cols // rows, slice(0, width))
        split_out(pack_s, *packs)


def attn_bwd(
    group, place, xs, mids, fgrads, heads_kept, gs, bias, gain, wq, wk, wv, wo, keep_col,
    pieces=0, earlier=None, normed=(), ctx=(), after=(), start=0, rows=0, so_far=(None, None),
):
    heads = bias.shape[0]
    size = len(group)
    cols = wq.shape[0]
    width = wq.shape[1]
    weights = len(normed)
    others = weights - size if weights else 0
    longest = max(length for _, length, _ in group)
    part = sds((sum(length for _, length, _ in group) // 2, width), BF)
    outs = tuple(kept((length, width), BF) for _, length, _ in group)
    outs += tuple(kept((length, cols), BF) for _, length, _ in group) * 3
    outs += (part, part, sds((8, WIDE), F32), sds((8, width), F32))
    scratch = [pltpu.VMEM((longest, cols), BF), pltpu.VMEM((longest, width), BF)]
    if weights:
        outs += (sds((2 * cols, width), BF),) * 2
        scratch.append(pltpu.VMEM((4 * cols, width), BF))
    specs = [SMEM] + [Load(index * length, length) for index, length, _ in group]
    sums = Load(start, part.shape[0], pinned=False)
    specs += [LOAD] * (6 * size) + [sums] * 2 + [LOAD, PASS] + [LOAD] * 4 + [PASS]
    specs += [LOAD] * (4 * others + 2 * weights)
    operands = [place, *xs, *mids, *fgrads]
    operands += [kept_heads[i] for i in range(4) for kept_heads in heads_kept]
    operands += [*gs, bias, gain, wq, wk, wv, wo, keep_col]
    operands += [array for arrays in (earlier or ()) for array in arrays]
    operands += [*normed, *ctx]
    g = 1 + 7 * size
    order = [g + 3, 1 + size, g, g + 1, 1 + 2 * size, g + 7]
    order += [1 + 4 * size, 1 + 3 * size, 1 + 5 * size, 1 + 6 * size, g + 2, g + 4, g + 5, g + 6, 1]
    return call(
        functools.partial(
            attn_bwd_body, [(length, masked) for _, length, masked in group], heads, pieces, weights
        ),
        "attn_bwd",
        outs,
        specs,
        9.0 * size,
        scratch,
        after=after,
        order=order,
        into={
            4 * size + n: (sds((rows, width), BF), start, so_far[n]) for n in range(2)
        },
    )(*operands)


def tail_body(group, *refs):
    refs = list(refs)
    size = len(group)

    def take(number):
        taken = refs[:number]
        del refs[:number]
        return taken

    (place, x_doc, x_query), agrad, grads = take(3), take(size), take(4)
    gain, doc_o, query_o = refs
    at = [0, 0]
    for c, (length, masked) in enumerate(group):
        half = length // 2
        bases = halves(place, half)
        pair = 0 if c < 2 else 1
        x, out, base = (x_query, query_o, 0) if masked else (x_doc, doc_o, c * length)
        for n in range(2):
            rows = pl.ds(base + bases[n], half)
            xf = x[rows].astype(F32)
            dn = grads[2 * pair + n][at[pair] : at[pair] + half].astype(F32)
            own = agrad[c][pl.ds(bases[n], half)].astype(F32)
            out[rows] = (own + norm_back(xf, rinv(xf), gain[...], dn)).astype(BF)
        at[pair] += half


def tail(group, place, doc_tokens, query_tokens, agrads, first, rest, gain, after):
    return call(
        functools.partial(tail_body, group),
        "tokens_grad",
        (kept(doc_tokens.shape, BF), kept(query_tokens.shape, BF)),
        [SMEM] + [LOAD] * (2 + len(group)) + [PASS] * 5,
        8.0,
        after=after,
    )(place, doc_tokens, query_tokens, *agrads, *first, *rest, gain)


def swap(block, axis, distance):
    count = lax.axis_size(axis)
    return lax.ppermute(block, axis, [(i, i ^ distance) for i in range(count)])


def added(a, b):
    return (a.astype(F32) + b.astype(F32)).astype(BF)


def once(value, earlier):
    if not earlier:
        return value
    return lax.optimization_barrier((value, *earlier))[0]


class DpSum:
    def __init__(self, keep, send):
        self.keep = keep
        self.send = send
        self.distance = 1
        self.count = lax.axis_size("dp")
        self.total = None

    def start(self, holds=()):
        if self.distance < self.count:
            self.arrived = swap(once(self.send, holds), "dp", self.distance)
        else:
            self.back //= 2
            self.arrived = swap(once(self.total, holds), "dp", self.back)

    def add(self, holds=()):
        if self.distance < self.count:
            self.total = added(self.keep, once(self.arrived, holds))
            self.distance *= 2
            self.back = self.count
            if self.distance < self.count:
                half = self.total.shape[0] // 2
                self.keep, self.send = self.total[:half], self.total[half:]
        else:
            self.total = jnp.concatenate([self.total, once(self.arrived, holds)], axis=0)
        return self.total


class DpWhole:
    def __init__(self, keep, send):
        self.total, self.arrived = lax.psum((keep, send), "dp")

    def start(self, holds=()):
        self.distance, self.count, self.back = 1, 1, 1

    def add(self, holds=()):
        return self.total


def dp_gather(block):
    count = lax.axis_size("dp")
    spread = jnp.broadcast_to(block[None], (count,) + block.shape)
    return lax.all_to_all(spread, "dp", 0, 0, tiled=True)


def on_device(
    doc_tokens,
    query_tokens,
    w_query,
    w_key,
    w_value,
    w_out,
    w_gate,
    w_up,
    w_down,
    w_proj,
    gain_attn,
    gain_ffn,
    gain_final,
    bias_table,
    query_mask,
    retrieval_mask,
    positives,
):
    dp_count = lax.axis_size("dp")
    mp_count = lax.axis_size("mp")
    dp_index = lax.axis_index("dp")
    mp_index = lax.axis_index("mp")
    query_len = query_mask.shape[1]
    docs_here = doc_tokens.shape[0] // DOC_LEN
    queries_here = query_tokens.shape[0] // query_len
    query_total = dp_count * queries_here
    width = doc_tokens.shape[1]
    emb_width = w_proj.shape[1]
    units = w_gate.shape[1]
    lane_count = queries_here // mp_count
    lane_total = lane_count * dp_count
    lane_tokens = lane_total * query_len
    lane_pad = -(-lane_total // 128) * 128
    pieces = 8
    order_here = sum(((dp_index >> bit) & 1) << (2 - bit) for bit in range(3))
    if dp_count != pieces:
        order_here = jnp.zeros_like(dp_index)
    place = jnp.stack([mp_index, mp_index % 2, order_here]).astype(jnp.int32)
    w_query = w_query.T
    w_key = w_key.T
    w_value = w_value.T
    gain_attn = gain_attn.reshape(1, width)
    gain_ffn = gain_ffn.reshape(1, width)
    gain_final = gain_final.reshape(1, width)
    home_keep = lax.dynamic_slice_in_dim(query_mask, dp_index * queries_here, queries_here, 0)
    keep_col = home_keep.astype(F32).reshape(-1, 1)

    def lane_view(whole):
        grouped = whole.reshape((dp_count, queries_here) + whole.shape[1:])
        picked = lax.dynamic_slice_in_dim(grouped, mp_index * lane_count, lane_count, 1)
        return picked.reshape((lane_total,) + whole.shape[1:])

    lane_keep = lane_view(query_mask).astype(F32)
    lane_hits = lane_view(retrieval_mask).astype(F32)
    token_weights = lane_keep[:, :, None] * lane_hits / jnp.sum(lane_keep, axis=1)[:, None, None]
    token_weights = token_weights.reshape(lane_tokens, docs_here).T
    token_weights = jnp.pad(token_weights, ((0, 8 - docs_here), (0, 0)))
    doc_ids = dp_index * docs_here + jnp.arange(8, dtype=jnp.int32)
    doc_ids = jnp.where(jnp.arange(8) < docs_here, doc_ids, -1)
    lane_positive = jnp.pad(lane_view(positives), (0, lane_pad - lane_total), constant_values=-2)
    hot = (lane_positive[None, :] == doc_ids[:, None]).astype(F32)

    chunks = [(0, query_tokens.shape[0], True)] + [(p, DOC_LEN, False) for p in range(docs_here)]
    bias = make_bias(bias_table.T)
    sources = [query_tokens] + [doc_tokens] * docs_here
    dp_sum = DpSum if dp_count == pieces else DpWhole

    class MpSum:
        def __init__(self, keep, send):
            self.keep = keep
            self.arrived = swap(send, "mp", 1)

        def near(self, holds=()):
            self.sum = added(self.keep, once(self.arrived, holds))
            self.arrived = swap(self.sum, "mp", 2)
            return self.sum

        def far(self, holds=()):
            total = added(self.sum, once(self.arrived, holds))
            return (total, swap(total, "mp", 1))

    last = len(chunks) - 1
    attn, ffn, attn_sums, ffn_sums, attended = [], [], [], [], []
    for n, (c, t) in enumerate(zip(chunks, sources)):
        after = [a[6] for a in attn[-1:]] + [m.sum for m in attn_sums[-2:-1]]
        a = attn_fwd(
            c, place, t, gain_attn, w_query, w_key, w_value, w_out, bias, keep_col, after
        )
        attn.append(a)
        attn_sums.append(MpSum(a[6], a[7]))
        if n >= 1:
            attn_sums[n - 1].near([a[6]])
        if n >= 2:
            attended.append(attn_sums[n - 2].far([a[6]]))
    done, summed = attn[-1][6], attn_sums[-2].sum
    for n, (c, t) in enumerate(zip(chunks, sources)):
        f = ffn_fwd(
            c, place, t, *attended[n], gain_ffn, w_gate, w_up, w_down, [done, summed]
        )
        done = f[2]
        ffn.append(f)
        ffn_sums.append(MpSum(f[2], f[3]))
        summed = (attn_sums[last] if n == 0 else ffn_sums[n - 1]).near([done])
        if len(attended) <= last and n >= 1:
            attended.append(attn_sums[len(attended)].far([done]))
    ffn_sums[last].near()

    lane_block, output = query_embed(
        place,
        ffn[0][0],
        *ffn_sums[0].far([done]),
        gain_final,
        w_proj,
        lane_count * query_len,
        [ffn_sums[last].sum],
    )
    outputs = [output]
    queries = dp_gather(lane_block).reshape(lane_tokens, emb_width)
    emb = None
    lses = []
    done = queries
    for p in range(docs_here):
        emb, lse, output = doc_embed(
            p,
            place,
            ffn[p + 1][0],
            *ffn_sums[p + 1].far([done]),
            gain_final,
            w_proj,
            queries,
            emb,
            docs_here,
        )
        done = lse
        lses.append(lse)
        outputs.append(output)
    own = stats(lses, token_weights, hot, DOC_LEN)
    gathered = dp_gather(own)
    keep, send, query_part, scalars = score_back(
        place, gathered, own, token_weights, hot, emb, queries, lses, DOC_LEN, lane_total, query_total
    )
    doc_sum = MpSum(keep, send)
    doc_sum.near()
    doc_grads = doc_sum.far()
    query_part = query_part.reshape(dp_count, lane_count * query_len, emb_width)
    query_part = lax.all_to_all(query_part, "dp", 0, 0, tiled=True)

    query_here = query_sum(query_part, ())
    query_far = swap(query_here, "mp", 2)
    query_grads = [query_here, swap(query_here, "mp", 1), query_far, swap(query_far, "mp", 1)]
    order = list(range(1, docs_here + 1)) + [0]
    count = len(order)
    lengths = [chunks[n][1] for n in order]
    back = ffn_bwd(
        lengths,
        pieces,
        place,
        [outputs[n] for n in order],
        [ffn[n][1] for n in order],
        doc_grads,
        query_grads,
        gain_final,
        w_proj,
        w_gate,
        w_up,
        w_down,
    )
    fgrads = back[:count]
    keep_first, keep_rest, send_first, send_rest, final_gain = back[count : count + 5]
    wide = dp_sum(*back[count + 5 : count + 7])
    down = dp_sum(*back[count + 7 :])

    def attn_chunk(i, grads, position, so_far=(None, None), **more):
        n = order[i]
        return attn_bwd(
            [chunks[n]],
            place,
            [sources[n]],
            [ffn[n][0]],
            [fgrads[i]],
            [attn[n][1:5]],
            grads,
            bias,
            gain_ffn,
            w_query,
            w_key,
            w_value,
            w_out,
            keep_col,
            start=position,
            rows=(keep_first if i < 2 else keep_rest).shape[0],
            so_far=so_far,
            **more,
        )

    half = DOC_LEN // 2
    near_first = added(keep_first, swap(send_first, "mp", 1))
    near_rest = added(keep_rest, swap(send_rest, "mp", 1))
    wide.start()
    sum_first = added(near_first, swap(near_first, "mp", 2))
    grads_first = (sum_first, swap(sum_first, "mp", 1))
    near_rest = once(near_rest, [sum_first])
    far_rest = swap(near_rest, "mp", 2)
    wide.add([sum_first])
    wide.start()
    down.start([wide.total])
    back0 = attn_chunk(0, grads_first, 0, after=[wide.total, near_rest])
    wide.add([back0[6]])
    wide.start()
    back1 = attn_chunk(
        1, grads_first, half, back0[4:6], after=[wide.total, back0[6]]
    )
    sum_rest = added(near_rest, once(far_rest, [back1[6]]))
    grads_rest = (sum_rest, swap(sum_rest, "mp", 1))
    down.add([back1[6]])
    down.start()
    near_first = added(back1[4], swap(back1[5], "mp", 1))
    back2 = attn_chunk(2, grads_rest, 0, after=[down.total, back1[6]])
    near_first = once(near_first, [back2[6]])
    far_first = swap(near_first, "mp", 2)
    wide.add([back2[6]])
    wide.start()
    down.add([back2[6]])
    down.start()
    back3 = attn_chunk(
        3,
        grads_rest,
        half,
        back2[4:6],
        after=[wide.total, down.total, near_first, back2[6]],
        pieces=pieces,
        earlier=[[b[n] for b in (back0, back1, back2)] for n in (1, 2, 3, 0)],
        normed=[attn[n][0] for n in order],
        ctx=[attn[n][5] for n in order],
    )
    ends = [back3[6]]
    gain_rows = back0[7] + back1[7] + back2[7] + back3[7]
    diag = back0[6] + back1[6] + back2[6] + back3[6]
    small = jnp.concatenate([gain_rows[:2], final_gain[:1], jnp.zeros((5, width), F32)], axis=0)
    small = jnp.concatenate([small, diag], axis=1)
    heads_sum = dp_sum(*back3[8:10])
    heads_sum.start()
    wide.add(ends)
    wide.start()
    near_rest = added(back3[4], swap(back3[5], "mp", 1))
    down.add(ends)
    down.start()
    far_rest = swap(near_rest, "mp", 2)
    step = [heads_sum.add([near_rest])]
    heads_sum.start()
    wide.add(step)
    wide.start()
    sum_first = added(near_first, once(far_first, step))
    input_first = (sum_first, swap(sum_first, "mp", 1))
    distance = 1
    arrived = swap(small, "dp", distance)
    step = [heads_sum.add()]
    heads_sum.start()
    down.add(step)
    down.start()
    sum_rest = added(near_rest, once(far_rest, step))
    input_rest = (sum_rest, swap(sum_rest, "mp", 1))
    while distance < dp_count:
        small = small + once(arrived, step)
        distance *= 2
        if distance < dp_count:
            arrived = swap(small, "dp", distance)
        if heads_sum.distance < heads_sum.count or heads_sum.back > 1:
            step = [heads_sum.add()]
            heads_sum.start()
            if heads_sum.back == 2:
                down.add(step)
                down.start()
    tokens_grad, query_tokens_grad = tail(
        [chunks[n][1:] for n in order],
        place,
        doc_tokens,
        query_tokens,
        [b[0] for b in (back0, back1, back2, back3)],
        input_first,
        input_rest,
        gain_attn,
        step,
    )
    own_gain = small[:1, :width]
    own_gain = own_gain + swap(own_gain, "mp", 1)
    own_gain = own_gain + swap(own_gain, "mp", 2)
    scalars = once(scalars, [back1[6]])
    scalars = scalars + swap(scalars, "mp", 1)
    scalars = scalars + swap(scalars, "mp", 2)
    diag = small[:, width:]
    wide_pack, down_pack, attn_pack = ((d.total, d.arrived) for d in (wide, down, heads_sum))
    cols = w_query.shape[0]
    ffn_grads = unpack(
        place, pieces, wide_pack, cut_lanes, [(width, units), (width, units), (width, emb_width)]
    )
    down_grad = unpack(place, pieces, down_pack, cut_lanes, [(units, width)])
    attn_grads = unpack(place, pieces, attn_pack, cut_rows, [(cols, width)] * 4)

    lane = jnp.arange(WIDE, dtype=jnp.int32)
    offset = jnp.where(lane < DOC_LEN, -lane, WIDE - lane)
    distance = jnp.abs(offset)
    far = 8 + sum(((distance >= edge).astype(jnp.int32) for edge in EDGES))
    index = jnp.where(distance < 8, distance, far) + 16 * (offset > 0).astype(jnp.int32)
    onehot = (jnp.arange(bias_table.shape[0], dtype=jnp.int32)[:, None] == index[None]).astype(F32)
    grad_bias = lax.dot_general(
        onehot, diag[: bias_table.shape[1]], (((1,), (1,)), ((), ())), precision=HIGH
    )
    return (
        scalars[0, 0],
        scalars[1, 0],
        emb,
        tokens_grad,
        query_tokens_grad,
        attn_grads[0].T,
        attn_grads[1].T,
        attn_grads[2].T,
        attn_grads[3],
        ffn_grads[0],
        ffn_grads[1],
        down_grad[0],
        ffn_grads[2],
        own_gain[0],
        small[1, :width],
        small[2, :width],
        grad_bias,
    )


def solution(mesh):
    placed = (
        P("dp", None),
        P("dp", None),
        P(None, "mp"),
        P(None, "mp"),
        P(None, "mp"),
        P("mp", None),
        P(None, "mp"),
        P(None, "mp"),
        P("mp", None),
        P(),
        P(),
        P(),
        P(),
        P(None, "mp"),
        P(),
        P(None, None, "dp"),
        P(),
    )
    return jax.shard_map(
        on_device,
        mesh=mesh,
        in_specs=placed,
        out_specs=(
            P(),
            P(),
            P("dp", None),
            P("dp", None),
            P("dp", None),
            P(None, "mp"),
            P(None, "mp"),
            P(None, "mp"),
            P("mp", None),
            P(None, "mp"),
            P(None, "mp"),
            P("mp", None),
            P(),
            P(),
            P(),
            P(),
            P(None, "mp"),
        ),
        check_vma=False,
    )
```

```python
import functools
import math

import jax
import jax.numpy as jnp
from jax import lax
from jax.experimental import pallas as pl
from jax.experimental.pallas import tpu as pltpu
from jax.sharding import PartitionSpec as P

DOC_LEN = 512
EPS = 1e-06
DOC_TEMP = 32.0
EDGES = (12, 16, 23, 32, 46, 64, 91)
HIGH = lax.Precision.HIGHEST
MASKED = -1000000000.0
BF = jnp.bfloat16
F32 = jnp.float32
WIDE = 2 * DOC_LEN
GELU_A = math.sqrt(2.0 / math.pi)
GELU_B = 0.044715


def nn(a, b):
    return jnp.dot(a, b, preferred_element_type=F32)


def nt(a, b):
    return lax.dot_general(a, b, (((1,), (1,)), ((), ())), preferred_element_type=F32)


def tn(a, b):
    return lax.dot_general(a, b, (((0,), (0,)), ((), ())), preferred_element_type=F32)


def rinv(v):
    return lax.rsqrt(jnp.mean(v * v, axis=-1, keepdims=True) + EPS)


def norm_back(v, r, gain, grad):
    scaled = grad * gain
    return r * scaled - v * (r * r * r * jnp.mean(scaled * v, axis=-1, keepdims=True))


def rowsum8(v):
    return jnp.broadcast_to(jnp.sum(v, axis=0, keepdims=True), (8, v.shape[1]))


def halves(place, half):
    mine = pl.multiple_of(place[1] * half, half)
    other = pl.multiple_of((1 - place[1]) * half, half)
    return (mine, other)


class Load:
    def __init__(self, start=0, rows=None, pinned=True):
        self.start = start
        self.rows = rows
        self.pinned = pinned

    def shape(self, operand):
        return operand.shape if self.rows is None else (self.rows,) + operand.shape[1:]

    def of(self, ref):
        return ref if self.rows is None else ref.at[pl.ds(self.start, self.rows)]


class Held:
    def __init__(self, ref, copy):
        self.ref = ref
        self.copy = copy
        self.begun = False

    @property
    def shape(self):
        return self.ref.shape

    @property
    def dtype(self):
        return self.ref.dtype


class Operand(Held):
    def ready(self):
        if not self.begun:
            self.begun = True
            self.copy.wait()
        return self.ref

    def __getitem__(self, at):
        return self.ready()[at]


class Result(Held):
    def __getitem__(self, at):
        return self.ref[at]

    def __setitem__(self, at, value):
        self.ref[at] = value

    def done(self):
        if not self.begun:
            self.begun = True
            self.copy.start()


LOAD = Load()
PASS = Load(pinned=False)
SMEM = pl.BlockSpec(memory_space=pltpu.SMEM)
FAR = pl.BlockSpec(memory_space=pltpu.HBM)


def sds(shape, dtype):
    return jax.ShapeDtypeStruct(shape, dtype)


class Kept:
    def __init__(self, shape, dtype):
        self.shape = shape
        self.dtype = dtype


def kept(shape, dtype):
    return Kept(shape, dtype)


def call(body, name, outs, in_specs, micros, scratch=(), into=None, after=(), order=()):
    count = len(outs)
    stores = [LOAD] * count
    out_shape = list(outs)
    begun = []
    for k, (whole, start, so_far) in (into or {}).items():
        out_shape[k] = whole
        stores[k] = Load(start, outs[k].shape[0])
        if so_far is not None:
            begun.append((k, so_far))
    after = [so_far for _, so_far in begun] + list(after)

    def run(*operands):
        pinned = [
            pltpu.with_memory_space_constraint(operand, pltpu.HBM) if isinstance(spec, Load) and spec.pinned else operand
            for spec, operand in zip(in_specs, operands)
        ]
        loads = [n for n, spec in enumerate(in_specs) if isinstance(spec, Load)]
        total = len(loads)
        given = len(operands)
        buffers = [
            pltpu.VMEM(in_specs[n].shape(operands[n]), operands[n].dtype) for n in loads
        ] + [pltpu.VMEM(out.shape, out.dtype) for out in outs]

        def kernel(*refs):
            ins = list(refs[:given])
            results = refs[given + len(after) : given + len(after) + count]
            rest = refs[given + len(after) + count :]
            own, held, sems = rest[: len(scratch)], rest[len(scratch) : -1], rest[-1]
            for n in sorted(loads, key=lambda n: order.index(n) if n in order else given + n):
                k = loads.index(n)
                copy = pltpu.make_async_copy(in_specs[n].of(ins[n]), held[k], sems.at[k])
                copy.start()
                ins[n] = Operand(held[k], copy)
            made = []
            for k, result in enumerate(results):
                buffer = held[total + k]
                copy = pltpu.make_async_copy(buffer, stores[k].of(result), sems.at[total + k])
                made.append(Result(buffer, copy))
            body(*ins, *made, *own)
            for n in loads:
                ins[n].ready()
            for result in made:
                result.done()
            for result in made:
                result.copy.wait()

        return pl.pallas_call(
            kernel,
            name=name,
            out_shape=tuple(
                pltpu.HBM(out.shape, out.dtype) if isinstance(out, Kept) else out for out in out_shape
            ),
            in_specs=[FAR if isinstance(spec, Load) else spec for spec in in_specs]
            + [FAR] * len(after),
            out_specs=(FAR,) * count,
            scratch_shapes=list(scratch) + buffers + [pltpu.SemaphoreType.DMA((total + count,))],
            input_output_aliases={given + n: k for n, (k, _) in enumerate(begun)},
            compiler_params=pltpu.CompilerParams(vmem_limit_bytes=48 * 1024 * 1024),
            cost_estimate=pl.CostEstimate(
                flops=int(micros * 2e8), bytes_accessed=int(micros * 1e5), transcendentals=0
            ),
        )(*pinned, *after)

    return run


def bias_into(table, out):
    lane = lax.broadcasted_iota(jnp.int32, (8, WIDE), 1)
    offset = jnp.where(lane < DOC_LEN, -lane, WIDE - lane)
    distance = jnp.abs(offset)
    far = jnp.full_like(distance, 8)
    for edge in EDGES:
        far = far + (distance >= edge).astype(jnp.int32)
    index = jnp.where(distance < 8, distance, far) + jnp.where(offset > 0, 16, 0)
    for head in range(out.shape[0]):
        row = jnp.zeros((8, WIDE), F32)
        for bucket in range(table.shape[1]):
            row = jnp.where(index == bucket, table[head, bucket], row)
        spread = jnp.broadcast_to(row[:1], (DOC_LEN, WIDE))
        rolled = pltpu.roll(spread, 0, 1, stride=1, stride_axis=0)
        out[head] = rolled[:, :DOC_LEN]


def make_bias(table):
    return call(
        bias_into,
        "rel_bias",
        (kept((table.shape[0], DOC_LEN, DOC_LEN), F32),),
        [SMEM],
        2.0,
    )(table)[0]


def attn_fwd_body(length, masked, heads, *refs):
    place, x, gain, wq, wk, wv, wo, bias = refs[:8]
    pos = 8
    keep_col = None
    if masked:
        keep_col = refs[8]
        pos = 9
    normed_o, q_o, k_o, v_o, lse_o, ctx_o, keep_o, send_o, part_s = refs[pos:]
    half = length // 2
    xf = x[...].astype(F32)
    normed = (xf * rinv(xf) * gain[...]).astype(BF)
    normed_o[...] = normed
    normed_o.done()
    q = nt(normed, wq[...]).astype(BF)
    k = nt(normed, wk[...]).astype(BF)
    v = nt(normed, wv[...]).astype(BF)
    q_o[...] = q
    k_o[...] = k
    v_o[...] = v
    for result in (q_o, k_o, v_o):
        result.done()
    width = q.shape[1] // heads
    vt = v.T
    tile = min(length, 256)
    lse_o[...] = jnp.zeros(lse_o.shape, F32)
    for h in range(heads):
        cols = slice(h * width, (h + 1) * width)
        for start in range(0, length, tile):
            span = slice(start, start + tile)
            logits = nt(k[:, cols], q[span, cols]) + bias[h, :length, span]
            if masked:
                logits = jnp.where(query_mask_of(keep_col, length), logits, MASKED)
            top = jnp.max(logits, axis=0, keepdims=True)
            shifted = jnp.exp(logits - top)
            total = jnp.sum(shifted, axis=0, keepdims=True)
            probs = (shifted * (1.0 / total)).astype(BF)
            ctx_t = nn(vt[cols], probs)
            ctx_o[span, cols] = ctx_t.T.astype(BF)
            lse_o[h : h + 1, span] = top + jnp.log(total)
    ctx_o.done()
    lse_o.done()
    part_s[...] = nn(ctx_o[...], wo[...]).astype(BF)
    mine, other = halves(place, half)
    keep_o[...] = part_s[pl.ds(mine, half)]
    send_o[...] = part_s[pl.ds(other, half)]


def query_mask_of(keep_col, length):
    key_row = lax.broadcasted_iota(jnp.int32, (length, length), 0)
    query_row = lax.broadcasted_iota(jnp.int32, (length, length), 1)
    return ((key_row // 32) == (query_row // 32)) & (keep_col[...] > 0)


def attn_fwd(chunk, place, tokens, gain, wq, wk, wv, wo, bias, keep_col, after):
    index, length, masked = chunk
    heads = bias.shape[0]
    cols = wq.shape[0]
    width = tokens.shape[1]
    specs = [SMEM, Load(index * length, length), PASS] + [LOAD] * 5
    operands = [place, tokens, gain, wq, wk, wv, wo, bias]
    if masked:
        specs.append(PASS)
        operands.append(keep_col)
    small = kept((length, cols), BF)
    part = sds((length // 2, width), BF)
    return call(
        functools.partial(attn_fwd_body, length, masked, heads),
        "attn_fwd",
        (kept((length, width), BF), small, small, small, kept((8, length), F32), small, part, part),
        specs,
        0.012 * length,
        [pltpu.VMEM((length, width), BF)],
        after=after,
    )(*operands)


def gelu_parts(gate):
    t = jnp.tanh(GELU_A * (gate + GELU_B * gate * gate * gate))
    return 0.5 * gate * (1.0 + t), t


def ffn_fwd_body(length, place, x, um, uo, gain, wg, wu, wd, middle_o, normed_o, keep_o, send_o):
    half = length // 2
    bases = halves(place, half)
    for n, (u, out) in enumerate(((um, keep_o), (uo, send_o))):
        middle = x[pl.ds(bases[n], half)].astype(F32) + u[...].astype(F32)
        middle_o[n * half : (n + 1) * half] = middle
        normed = (middle * rinv(middle) * gain[...]).astype(BF)
        normed_o[n * half : (n + 1) * half] = normed
        if n == 1:
            middle_o.done()
            normed_o.done()
        act, _ = gelu_parts(nn(normed, wg[...]))
        hidden = (act * nn(normed, wu[...])).astype(BF)
        out[...] = nn(hidden, wd[...]).astype(BF)


def ffn_fwd(chunk, place, tokens, um, uo, gain, wg, wu, wd, after):
    index, length, _ = chunk
    width = tokens.shape[1]
    part = sds((length // 2, width), BF)
    return call(
        functools.partial(ffn_fwd_body, length),
        "ffn_fwd",
        (kept((length, width), F32), kept((length, width), BF), part, part),
        [SMEM, Load(index * length, length)] + [PASS] * 3 + [LOAD] * 3,
        0.01 * length,
        after=after,
        order=(4, 2, 1, 5, 6, 7, 3),
    )(place, tokens, um, uo, gain, wg, wu, wd)


def embed_rows(length, place, middle, fs, gain, wp, emb_s, out_o):
    half = length // 2
    bases = halves(place, half)
    for n in range(2):
        span = slice(n * half, (n + 1) * half)
        out = middle[span] + fs[n][...].astype(F32)
        out_o[span] = out
        if n == 1:
            out_o.done()
        normed = (out * rinv(out) * gain[...]).astype(BF)
        emb_s[pl.ds(bases[n], half)] = nn(normed, wp[...]).astype(BF)


def query_embed_body(length, lane, place, middle, fm, fo, gain, wp, lane_o, out_o, emb_s):
    embed_rows(length, place, middle, (fm, fo), gain, wp, emb_s, out_o)
    lane_o[...] = emb_s[pl.ds(pl.multiple_of(place[0] * lane, lane), lane)]


def query_embed(place, middle, fm, fo, gain, wp, lane, after):
    length = middle.shape[0]
    emb = wp.shape[1]
    return call(
        functools.partial(query_embed_body, length, lane),
        "query_embed",
        (sds((lane, emb), BF), kept(middle.shape, F32)),
        [SMEM, LOAD] + [PASS] * 3 + [LOAD],
        0.004 * length,
        [pltpu.VMEM((length, emb), BF)],
        after=after,
    )(place, middle, fm, fo, gain, wp)


def lane_tile(tokens):
    return min(tokens, 512)


def doc_embed_body(length, place, middle, fm, fo, gain, wp, queries, emb_o, lse_o, out_o):
    embed_rows(length, place, middle, (fm, fo), gain, wp, emb_o, out_o)
    emb_o.done()
    scale = wp.shape[1] ** (-0.5)
    tile = lane_tile(queries.shape[0])
    for start in range(0, queries.shape[0], tile):
        span = slice(start, start + tile)
        scores = nt(emb_o[...], queries[span]) * scale
        top = jnp.max(scores, axis=0, keepdims=True)
        total = jnp.sum(jnp.exp(scores - top), axis=0, keepdims=True)
        lse_o[:, span] = jnp.broadcast_to(top + jnp.log(total), (8, tile))


def doc_embed(index, place, middle, fm, fo, gain, wp, queries, so_far, docs, after):
    length = middle.shape[0]
    emb = wp.shape[1]
    return call(
        functools.partial(doc_embed_body, length),
        "doc_embed",
        (kept((length, emb), BF), sds((8, queries.shape[0]), F32), kept(middle.shape, F32)),
        [SMEM, LOAD] + [PASS] * 3 + [LOAD, PASS],
        0.005 * length,
        into={0: (kept((docs * length, emb), BF), index * length, so_far)},
        order=(4, 2, 1, 5, 6, 3),
        after=after,
    )(place, middle, fm, fo, gain, wp, queries)


def segment(tokens, lanes):
    token = lax.broadcasted_iota(jnp.int32, (tokens, lanes), 0) // 32
    return (token == lax.broadcasted_iota(jnp.int32, (tokens, lanes), 1)).astype(F32)


def stats_body(docs, doc_len, *refs):
    lses = refs[:docs]
    weights, hot, out = refs[docs:]
    lanes = hot.shape[1]
    tokens = weights.shape[1]
    seg = segment(tokens, lanes)
    w = weights[...]
    rows = lax.broadcasted_iota(jnp.int32, (8, tokens), 0)
    scores = jnp.zeros((8, tokens), F32)
    for p in range(docs):
        scores = jnp.where(rows == p, lses[p][...], scores)
    scores = w * (scores - jnp.where(rows < docs, math.log(doc_len), 0.0))
    table = DOC_TEMP * jnp.dot(scores, seg, precision=HIGH, preferred_element_type=F32)
    share = jnp.dot(w, seg, precision=HIGH, preferred_element_type=F32)
    lane_rows = lax.broadcasted_iota(jnp.int32, (8, lanes), 0)
    positive = jnp.sum(table * hot[...], axis=0, keepdims=True)
    share = jnp.sum(share * hot[...], axis=0, keepdims=True)
    result = jnp.where(lane_rows < docs, table, 0.0)
    result = jnp.where(lane_rows == docs, positive, result)
    out[...] = jnp.where(lane_rows == docs + 1, share, result)


def stats(lses, weights, hot, doc_len):
    return call(
        functools.partial(stats_body, len(lses), doc_len),
        "doc_stats",
        (sds(hot.shape, F32),),
        [PASS] * (len(lses) + 2),
        0.5,
    )(*lses, weights, hot)[0]


def score_back_body(docs, doc_len, lane_total, query_total, *refs):
    place, gathered, own, weights, hot, emb, queries = refs[:7]
    lses = refs[7 : 7 + docs]
    keep_o, send_o, query_o, scalars_o, doc_s, query_s = refs[7 + docs :]
    lanes = hot.shape[1]
    tokens = weights.shape[1]
    everything = gathered[...]
    rows = lax.broadcasted_iota(jnp.int32, everything.shape, 1)
    scores = jnp.where(rows < docs, everything, -jnp.inf)
    top = jnp.max(jnp.max(scores, axis=0), axis=0, keepdims=True)
    total = jnp.sum(jnp.sum(jnp.exp(scores - top[None]), axis=0), axis=0, keepdims=True)
    log_norm = top + jnp.log(total)
    summed = jnp.sum(everything, axis=0)
    valid = lax.broadcasted_iota(jnp.int32, (1, lanes), 1) < lane_total
    loss = jnp.where(valid, log_norm - summed[docs : docs + 1], 0.0)
    share = jnp.where(valid, summed[docs + 1 : docs + 2], 0.0)
    out_rows = lax.broadcasted_iota(jnp.int32, (8, 128), 0)
    loss = jnp.sum(loss, axis=1, keepdims=True) / query_total
    share = jnp.sum(share, axis=1, keepdims=True) / query_total
    scalars_o[...] = jnp.where(out_rows == 0, loss, share)
    own_rows = lax.broadcasted_iota(jnp.int32, own.shape, 0)
    grads = DOC_TEMP * (jnp.exp(own[...] - log_norm) - hot[...]) / query_total
    grads = jnp.where(own_rows < docs, grads, 0.0)
    seg = segment(tokens, lanes)
    spread = lax.dot_general(
        grads, seg, (((1,), (1,)), ((), ())), precision=HIGH, preferred_element_type=F32
    )
    token_grad = spread * weights[...]
    emb_width = queries.shape[1]
    scale = emb_width ** (-0.5)
    half = doc_len // 2
    bases = halves(place, half)
    tile = lane_tile(tokens)
    for start in range(0, tokens, tile):
        span = slice(start, start + tile)
        query = queries[span]
        query_grad = jnp.zeros((emb_width, tile), F32)
        for p in range(docs):
            doc = emb[p * doc_len : (p + 1) * doc_len]
            scores = nt(doc, query) * scale
            grad = (token_grad[p : p + 1, span] * jnp.exp(scores - lses[p][:1, span])).astype(BF)
            part = nn(grad, query) * scale
            if start == 0:
                doc_s[p * doc_len : (p + 1) * doc_len] = part
            else:
                doc_s[p * doc_len : (p + 1) * doc_len] += part
            query_grad = query_grad + nn(doc.T, grad)
        query_o[span] = (query_grad * scale).T.astype(BF)
    for p in range(docs):
        keep_o[p * half : (p + 1) * half] = doc_s[pl.ds(p * doc_len + bases[0], half)].astype(BF)
        send_o[p * half : (p + 1) * half] = doc_s[pl.ds(p * doc_len + bases[1], half)].astype(BF)


def score_back(place, gathered, own, weights, hot, emb, queries, lses, doc_len, lane_total, query_total):
    docs = len(lses)
    width = emb.shape[1]
    part = sds((docs * doc_len // 2, width), BF)
    return call(
        functools.partial(score_back_body, docs, doc_len, lane_total, query_total),
        "score_back",
        (part, part, sds(queries.shape, BF), sds((8, 128), F32)),
        [SMEM] + [PASS] * 4 + [LOAD] + [PASS] * (1 + docs),
        3.0,
        [pltpu.VMEM((docs * doc_len, width), F32), pltpu.VMEM((8, 128), F32)],
    )(place, gathered, own, weights, hot, emb, queries, *lses)


def query_sum_body(parts, out):
    out[...] = jnp.sum(parts[...].astype(F32), axis=0).astype(BF)


def query_sum(parts, after):
    return call(
        query_sum_body, "query_sum", (sds(parts.shape[1:], BF),), [PASS], 1.5, after=after
    )(parts)[0]


def ffn_bwd_body(lengths, masked, pieces, early, *refs):
    refs = list(refs)
    count = len(lengths)

    def take(number):
        taken = refs[:number]
        del refs[:number]
        return taken

    (place,) = take(1)
    finals, normeds = take(count), take(count)
    doc_mine, doc_other = take(2)
    query_grads = take(4 if masked else 0)
    gain_final, wp, wg, wu, wd = take(5)
    early_normeds, early_fgrads = take(early), take(early)
    early_inner, early_sums = (take(3), take(2)) if early else ((), ())
    fgrads = take(count)
    keep_o, send_o, gain_o = take(3)
    if early:
        packs = take(4)
        emb_s, hidden, ggrad, ugrad, up_s, down_s = refs
    else:
        hidden, ggrad, ugrad, proj_o = refs
    width = finals[0].shape[1]
    units = hidden.shape[1]
    gain_sum = jnp.zeros((1, width), F32)
    proj = jnp.zeros((wp.shape[1], width), F32)
    at = 0
    for c, length in enumerate(lengths):
        half = length // 2
        bases = halves(place, half)
        if masked and c == count - 1:
            lane = query_grads[0].shape[0]
            for step, grad in enumerate(query_grads):
                emb_s[pl.ds(pl.multiple_of((place[0] ^ step) * lane, lane), lane)] = grad[...]
            egs = [emb_s[pl.ds(base, half)] for base in bases]
        else:
            egs = [grad[c * half : (c + 1) * half] for grad in (doc_mine, doc_other)]
        for n, out in enumerate((keep_o, send_o)):
            span = slice(n * half, (n + 1) * half)
            rows = slice(at + n * half, at + (n + 1) * half)
            output = finals[c][span]
            r = rinv(output)
            dn = nt(egs[n], wp[...])
            unit = output * r
            gain_sum = gain_sum + jnp.sum(dn * unit, axis=0, keepdims=True)
            proj = proj + nn(egs[n].T, (unit * gain_final[...]).astype(BF))
            fgrad = norm_back(output, r, gain_final[...], dn).astype(BF)
            fgrads[c][span] = fgrad
            if n == 1:
                fgrads[c].done()
            gate = nn(normeds[c][span], wg[...])
            up = nn(normeds[c][span], wu[...])
            act, t = gelu_parts(gate)
            hidden[rows] = (act * up).astype(BF)
            hgrad = nt(fgrad, wd[...])
            slope = 0.5 * (1.0 + t) + 0.5 * gate * (1.0 - t * t) * (
                GELU_A * (1.0 + 3.0 * GELU_B * gate * gate)
            )
            gg = (hgrad * up * slope).astype(BF)
            ug = (hgrad * act).astype(BF)
            ggrad[rows] = gg
            ugrad[rows] = ug
            out[at // 2 : at // 2 + half] = (nt(gg, wg[...]) + nt(ug, wu[...])).astype(BF)
        at += length
    send_o.done()
    keep_o.done()
    if not early:
        gain_o[...] = jnp.broadcast_to(gain_sum, gain_o.shape)
        proj_o[...] = proj
        return
    gain_o[...] = jnp.broadcast_to(gain_sum, gain_o.shape) + early_sums[0][...]
    proj = proj + early_sums[1][...]

    def total(lefts, own, earlier, span):
        result = 0.0
        at = 0
        for c, left in enumerate(lefts):
            if c == early:
                at = 0
            right = earlier if c < early else own
            rows = slice(at, at + left.shape[0])
            result = result + tn(left[:, span], right[rows])
            at += left.shape[0]
        return result.astype(BF)

    rows = width // pieces
    lefts = early_normeds + normeds
    blocks = ((up_s, 0, lefts, early_inner[1], ggrad), (up_s, 1, lefts, early_inner[2], ugrad))
    blocks += ((down_s, 0, early_fgrads + fgrads, early_inner[0], hidden),)
    for out, k, left, earlier, own in blocks:
        lanes = slice(k * units, (k + 1) * units)
        for start in range(0, width, 4 * rows):
            value = total(left, own, earlier, slice(start, start + 4 * rows))
            relative_store(out, value, place[2], pieces, rows, start // rows, lanes)
        if k == 1:
            split_out(up_s, *packs[:2])
            packs[1].done()
            packs[0].done()
    lanes = slice(units, down_s.shape[1])
    relative_store(down_s, proj.T.astype(BF), place[2], pieces, rows, 0, lanes)
    split_out(down_s, *packs[2:])


def ffn_bwd(
    lengths, pieces, place, finals, normeds, doc_grads, doc_at, query_grads, gain, wp, wg, wu, wd,
    early=(), after=(),
):
    masked = len(query_grads) > 0
    count = len(lengths)
    docs = count - 1 if masked else count
    width = finals[0].shape[1]
    emb = wp.shape[1]
    units = wg.shape[1]
    rows = sum(lengths)
    part = sds((rows // 2, width), BF)
    outs = tuple(kept((length, width), BF) for length in lengths)
    outs += (part, part, sds((8, width), F32))
    doc_rows = sum(lengths[:docs]) // 2
    grads = Load(doc_at, doc_rows, pinned=False)
    specs = [SMEM] + [LOAD] * (2 * count) + [grads] * 2 + [PASS] * len(query_grads)
    specs += [PASS] + [LOAD] * 4
    extra = []
    first = 1 + 2 * count
    gates = first + 2 + len(query_grads)
    order = [gates, first, first + 1, gates + 1, 1, 1 + count, gates + 2, gates + 3, gates + 4]
    if early:
        number = len(early[0])
        extra = [*early[0], *early[1], *early[2], *early[3]]
        specs += [LOAD] * (2 * number + 3) + [PASS] * 2
        base = gates + 5
        order += list(range(2, first)) + list(range(base, base + number))
        order += [base + 2 * number + k for k in (1, 2, 0)]
        up = sds((width // 2, 2 * units), BF)
        down = sds((width // 2, units + emb), BF)
        outs += (up, up, down, down)
        inner = pltpu.VMEM((rows, units), BF)
        scratch = [
            pltpu.VMEM((lengths[-1], emb), BF),
            inner,
            inner,
            inner,
            pltpu.VMEM((width, 2 * units), BF),
            pltpu.VMEM((width, units + emb), BF),
        ]
    else:
        outs += (kept((rows, units), BF),) * 3 + (sds((emb, width), F32),)
        scratch = []
    return call(
        functools.partial(
            ffn_bwd_body, lengths, masked, pieces, len(early[0]) if early else 0
        ),
        "ffn_bwd",
        outs,
        specs,
        14.0,
        scratch,
        order=order,
        after=after,
    )(place, *finals, *normeds, *doc_grads, *query_grads, gain, wp, wg, wu, wd, *extra)


def relative_store(out, value, base, pieces, rows, first, lanes):
    for n in range(value.shape[0] // rows):
        slot = reversed_bits(first + n, pieces) ^ base
        out[pl.ds(pl.multiple_of(slot * rows, rows), rows), lanes] = value[n * rows : (n + 1) * rows]


def reversed_bits(number, count):
    result = 0
    while count > 1:
        result = result * 2 + number % 2
        number //= 2
        count //= 2
    return result


def split_out(out, keep_o, send_o):
    half = out.shape[0] // 2
    keep_o[...] = out[:half]
    send_o[...] = out[half:]


def unpack_body(pieces, rows, count, cut, results, *refs):
    place = refs[0]
    parts = [part.ready() for part in refs[1 : 1 + count]]
    outs = list(refs[1 + count : 1 + count + results])
    refs[1 + count + results][...] = jnp.zeros((8, 128), F32)
    turned = refs[2 + count + results :]
    if turned:
        outs[0] = turned[0]
    for number in range(pieces):
        slot = reversed_bits(number, pieces) ^ place[2]
        for part, base in zip(parts, (0, pieces // 2)):

            @pl.when((slot >= base) & (slot < base + part.shape[0] // rows))
            def _(part=part, base=base):
                start = pl.multiple_of((slot - base) * rows, rows)
                value = part[pl.ds(start, rows)].astype(F32)
                cut(outs, number * rows, rows, value)

    if turned:
        refs[1 + count][...] = turned[0][...].T


def cut_lanes(outs, at, rows, value):
    lane = 0
    for out in outs:
        out[at : at + rows] = value[:, lane : lane + out.shape[1]]
        lane += out.shape[1]


def cut_rows(outs, at, rows, value):
    n, at = divmod(at, outs[0].shape[0])
    outs[n][at : at + rows] = value


def unpack(place, pieces, parts, cut, shapes, turned=None):
    rows = sum(part.shape[0] for part in parts) // pieces
    return call(
        functools.partial(unpack_body, pieces, rows, len(parts), cut, len(shapes)),
        "unpack",
        tuple(kept(shape, F32) for shape in shapes) + (sds((8, 128), F32),),
        [SMEM] + [PASS] * len(parts),
        2.0,
        [pltpu.VMEM(turned, F32)] if turned else [],
    )(place, *parts)


def diagonal_sums(block):
    length = block.shape[0]
    rows = length
    value = jnp.concatenate([block, jnp.zeros((rows, WIDE - length), F32)], axis=1)
    while rows > 8:
        rows //= 2
        value = value[:rows] + pltpu.roll(value[rows:], WIDE - rows, 1)
    total = value[0:1]
    for s in range(1, 8):
        total = total + pltpu.roll(jnp.broadcast_to(value[s : s + 1], (8, WIDE)), WIDE - s, 1)[:1]
    return total


def attn_bwd_chunk(place, length, masked, heads, ins, shared, outs, sums, base, ctx_s):
    x, mid, gm, go, g_at, fgrad, q, k, v, lse = ins
    bias, gain, wq, wk, wv, wo, keep_col = shared
    agrad_o, dq_o, dk_o, dv_o, keep_o, send_o = outs
    half = length // 2
    bases = halves(place, half)
    for n, g in enumerate((gm, go)):
        rows = pl.ds(bases[n], half)
        middle = mid[n * half : (n + 1) * half]
        r = rinv(middle)
        dn = g[g_at : g_at + half].astype(F32)
        sums["ffn"] = sums["ffn"] + jnp.sum(dn * (middle * r), axis=0, keepdims=True)
        grad = fgrad[n * half : (n + 1) * half].astype(F32) + norm_back(middle, r, gain[...], dn)
        agrad = grad.astype(BF)
        agrad_o[rows] = agrad
        ctx_s[rows] = nt(agrad, wo[...]).astype(BF)
    agrad_o.done()
    width = q.shape[1] // heads
    tile = min(length, 256)
    kt = k[...].T
    for h in range(heads):
        cols = slice(h * width, (h + 1) * width)
        kh = k[:, cols]
        vh = v[:, cols]
        dk = jnp.zeros((length, width), F32)
        dv = jnp.zeros((length, width), F32)
        pieces = []
        for start in range(0, length, tile):
            span = slice(start, start + tile)
            qh = q[span, cols]
            ch = ctx_s[span, cols]
            logits = nt(kh, qh) + bias[h, :length, span]
            if masked:
                logits = jnp.where(query_mask_of(keep_col, length), logits, MASKED)
            probs = jnp.exp(logits - lse[h : h + 1, span])
            pgrad = nt(vh, ch)
            delta = jnp.sum(probs * pgrad, axis=0, keepdims=True)
            lgrad = (probs * (pgrad - delta)).astype(BF)
            dv = dv + nn(probs.astype(BF), ch)
            dk = dk + nn(lgrad, qh)
            dq_o[span, cols] = nn(kt[cols], lgrad).T.astype(BF)
            pieces.append(lgrad)
        dk_o[:, cols] = dk.astype(BF)
        dv_o[:, cols] = dv.astype(BF)
        lgrad = jnp.concatenate(pieces, axis=1) if len(pieces) > 1 else pieces[0]
        sums["diag"][h] = sums["diag"][h] + diagonal_sums(lgrad.astype(F32))
    for result in (dq_o, dk_o, dv_o):
        result.done()
    part = nn(dq_o[...], wq[...]) + nn(dk_o[...], wk[...]) + nn(dv_o[...], wv[...])
    xf = x[...].astype(F32)
    sums["attn"] = sums["attn"] + jnp.sum(part * (xf * rinv(xf)), axis=0, keepdims=True)
    return part.astype(BF)


def attn_bwd_body(group, heads, pieces, weights, *refs):
    refs = list(refs)
    size = len(group)
    others = weights - size if weights else 0

    def take(number):
        taken = refs[:number]
        del refs[:number]
        return taken

    (place,) = take(1)
    x, mid, fgrad, q, k, v, lse = (take(size) for _ in range(7))
    gm, go, bias, gain, wq, wk, wv, wo, keep_col = take(9)
    earlier = [take(others) for _ in range(4)]
    normed, ctx = take(weights), take(weights)
    agrad, dq, dk, dv = (take(size) for _ in range(4))
    keep_o, send_o, diag_o, gain_o = take(4)
    packs = take(2) if weights else None
    ctx_s, part_s = take(2)
    width = x[0].shape[1]
    sums = {
        "ffn": jnp.zeros((1, width), F32),
        "attn": jnp.zeros((1, width), F32),
        "diag": [jnp.zeros((1, WIDE), F32)] * heads,
    }
    at = 0
    for c, (length, masked) in enumerate(group):
        half = length // 2
        part = attn_bwd_chunk(
            place,
            length,
            masked,
            heads,
            (x[c], mid[c], gm, go, at, fgrad[c], q[c], k[c], v[c], lse[c]),
            (bias, gain, wq, wk, wv, wo, keep_col),
            (agrad[c], dq[c], dk[c], dv[c], keep_o, send_o),
            sums,
            at,
            ctx_s,
        )
        part_s[:length] = part
        bases = halves(place, half)
        keep_o[at : at + half] = part_s[pl.ds(bases[0], half)]
        send_o[at : at + half] = part_s[pl.ds(bases[1], half)]
        at += half
    send_o.done()
    keep_o.done()
    diag_o[...] = jnp.zeros(diag_o.shape, F32)
    for h in range(heads):
        diag_o[h : h + 1] = sums["diag"][h]
    row = lax.broadcasted_iota(jnp.int32, gain_o.shape, 0)
    gain_o[...] = jnp.where(row == 0, sums["attn"], sums["ffn"])
    if weights:
        pack_s = refs[0]
        cols = q[0].shape[1]
        rows = pack_s.shape[0] // pieces
        every = [old + new for old, new in zip(earlier, (dq, dk, dv, agrad))]
        pairs = ((every[0], normed), (every[1], normed), (every[2], normed), (ctx, every[3]))
        for n, (left, right) in enumerate(pairs):
            total = sum(tn(a[...], b[...]) for a, b in zip(left, right)).astype(BF)
            relative_store(pack_s, total, place[2], pieces, rows, n * cols // rows, slice(0, width))
        split_out(pack_s, *packs)


def attn_bwd(
    group, place, xs, mids, fgrads, heads_kept, gs, bias, gain, wq, wk, wv, wo, keep_col,
    pieces=0, earlier=None, normed=(), ctx=(), after=(), start=0, rows=0, so_far=(None, None),
):
    heads = bias.shape[0]
    size = len(group)
    cols = wq.shape[0]
    width = wq.shape[1]
    weights = len(normed)
    others = weights - size if weights else 0
    longest = max(length for _, length, _ in group)
    part = sds((sum(length for _, length, _ in group) // 2, width), BF)
    outs = tuple(kept((length, width), BF) for _, length, _ in group)
    outs += tuple(kept((length, cols), BF) for _, length, _ in group) * 3
    outs += (part, part, sds((8, WIDE), F32), sds((8, width), F32))
    scratch = [pltpu.VMEM((longest, cols), BF), pltpu.VMEM((longest, width), BF)]
    if weights:
        outs += (sds((2 * cols, width), BF),) * 2
        scratch.append(pltpu.VMEM((4 * cols, width), BF))
    specs = [SMEM] + [Load(index * length, length) for index, length, _ in group]
    sums = Load(start, part.shape[0], pinned=False)
    specs += [LOAD] * (6 * size) + [sums] * 2 + [LOAD, PASS] + [LOAD] * 4 + [PASS]
    specs += [LOAD] * (4 * others + 2 * weights)
    operands = [place, *xs, *mids, *fgrads]
    operands += [kept_heads[i] for i in range(4) for kept_heads in heads_kept]
    operands += [*gs, bias, gain, wq, wk, wv, wo, keep_col]
    operands += [array for arrays in (earlier or ()) for array in arrays]
    operands += [*normed, *ctx]
    g = 1 + 7 * size
    order = [g + 3, 1 + size, g, g + 1, 1 + 2 * size, g + 7]
    order += [1 + 4 * size, 1 + 3 * size, 1 + 5 * size, 1 + 6 * size, g + 2, g + 4, g + 5, g + 6, 1]
    return call(
        functools.partial(
            attn_bwd_body, [(length, masked) for _, length, masked in group], heads, pieces, weights
        ),
        "attn_bwd",
        outs,
        specs,
        9.0 * size,
        scratch,
        after=after,
        order=order,
        into={
            4 * size + n: (sds((rows or part.shape[0], width), BF), start, so_far[n]) for n in range(2)
        },
    )(*operands)


def tail_body(group, *refs):
    refs = list(refs)
    size = len(group)

    def take(number):
        taken = refs[:number]
        del refs[:number]
        return taken

    (place, x_doc, x_query), agrad, grads = take(3), take(size), take(4)
    gain, doc_o, query_o = refs
    at = [0, 0]
    for c, (length, masked) in enumerate(group):
        half = length // 2
        bases = halves(place, half)
        pair = 0 if c < 2 else 1
        x, out, base = (x_query, query_o, 0) if masked else (x_doc, doc_o, c * length)
        for n in range(2):
            rows = pl.ds(base + bases[n], half)
            xf = x[rows].astype(F32)
            dn = grads[2 * pair + n][at[pair] : at[pair] + half].astype(F32)
            own = agrad[c][pl.ds(bases[n], half)].astype(F32)
            out[rows] = (own + norm_back(xf, rinv(xf), gain[...], dn)).astype(BF)
        at[pair] += half


def tail(group, place, doc_tokens, query_tokens, agrads, first, rest, gain, after):
    return call(
        functools.partial(tail_body, group),
        "tokens_grad",
        (kept(doc_tokens.shape, BF), kept(query_tokens.shape, BF)),
        [SMEM] + [LOAD] * (2 + len(group)) + [PASS] * 5,
        8.0,
        after=after,
    )(place, doc_tokens, query_tokens, *agrads, *first, *rest, gain)


def swap(block, axis, distance):
    count = lax.axis_size(axis)
    return lax.ppermute(block, axis, [(i, i ^ distance) for i in range(count)])


def added(a, b):
    return (a.astype(F32) + b.astype(F32)).astype(BF)


def once(value, earlier):
    if not earlier:
        return value
    return lax.optimization_barrier((value, *earlier))[0]


class DpSum:
    def __init__(self, keep, send):
        self.keep = keep
        self.send = send
        self.distance = 1
        self.count = lax.axis_size("dp")
        self.total = None

    def start(self, holds=()):
        if self.distance < self.count:
            self.arrived = swap(once(self.send, holds), "dp", self.distance)
        else:
            self.back //= 2
            self.arrived = swap(once(self.total, holds), "dp", self.back)

    def add(self, holds=()):
        if self.distance < self.count:
            self.total = added(self.keep, once(self.arrived, holds))
            self.distance *= 2
            self.back = self.count
            if self.distance < self.count:
                half = self.total.shape[0] // 2
                self.keep, self.send = self.total[:half], self.total[half:]
        else:
            self.total = jnp.concatenate([self.total, once(self.arrived, holds)], axis=0)
        return self.total


class DpWhole:
    def __init__(self, keep, send):
        self.total, self.arrived = lax.psum((keep, send), "dp")

    def start(self, holds=()):
        pass

    def add(self, holds=()):
        return self.total

def dp_gather(block):
    count = lax.axis_size("dp")
    spread = jnp.broadcast_to(block[None], (count,) + block.shape)
    return lax.all_to_all(spread, "dp", 0, 0, tiled=True)


def on_device(
    doc_tokens,
    query_tokens,
    w_query,
    w_key,
    w_value,
    w_out,
    w_gate,
    w_up,
    w_down,
    w_proj,
    gain_attn,
    gain_ffn,
    gain_final,
    bias_table,
    query_mask,
    retrieval_mask,
    positives,
):
    dp_count = lax.axis_size("dp")
    mp_count = lax.axis_size("mp")
    dp_index = lax.axis_index("dp")
    mp_index = lax.axis_index("mp")
    query_len = query_mask.shape[1]
    docs_here = doc_tokens.shape[0] // DOC_LEN
    queries_here = query_tokens.shape[0] // query_len
    query_total = dp_count * queries_here
    width = doc_tokens.shape[1]
    emb_width = w_proj.shape[1]
    units = w_gate.shape[1]
    lane_count = queries_here // mp_count
    lane_total = lane_count * dp_count
    lane_tokens = lane_total * query_len
    lane_pad = -(-lane_total // 128) * 128
    pieces = 8
    order_here = sum(((dp_index >> bit) & 1) << (2 - bit) for bit in range(3))
    if dp_count != pieces:
        order_here = jnp.zeros_like(dp_index)
    place = jnp.stack([mp_index, mp_index % 2, order_here]).astype(jnp.int32)
    w_query = w_query.T
    w_key = w_key.T
    w_value = w_value.T
    gain_attn = gain_attn.reshape(1, width)
    gain_ffn = gain_ffn.reshape(1, width)
    gain_final = gain_final.reshape(1, width)
    home_keep = lax.dynamic_slice_in_dim(query_mask, dp_index * queries_here, queries_here, 0)
    keep_col = home_keep.astype(F32).reshape(-1, 1)

    def lane_view(whole):
        grouped = whole.reshape((dp_count, queries_here) + whole.shape[1:])
        picked = lax.dynamic_slice_in_dim(grouped, mp_index * lane_count, lane_count, 1)
        return picked.reshape((lane_total,) + whole.shape[1:])

    lane_keep = lane_view(query_mask).astype(F32)
    lane_hits = lane_view(retrieval_mask).astype(F32)
    token_weights = lane_keep[:, :, None] * lane_hits / jnp.sum(lane_keep, axis=1)[:, None, None]
    token_weights = token_weights.reshape(lane_tokens, docs_here).T
    token_weights = jnp.pad(token_weights, ((0, 8 - docs_here), (0, 0)))
    doc_ids = dp_index * docs_here + jnp.arange(8, dtype=jnp.int32)
    doc_ids = jnp.where(jnp.arange(8) < docs_here, doc_ids, -1)
    lane_positive = jnp.pad(lane_view(positives), (0, lane_pad - lane_total), constant_values=-2)
    hot = (lane_positive[None, :] == doc_ids[:, None]).astype(F32)

    chunks = [(0, query_tokens.shape[0], True)] + [(p, DOC_LEN, False) for p in range(docs_here)]
    bias = make_bias(bias_table.T)
    sources = [query_tokens] + [doc_tokens] * docs_here
    dp_sum = DpSum if dp_count == pieces else DpWhole

    class MpSum:
        def __init__(self, keep, send):
            self.keep = keep
            self.arrived = swap(send, "mp", 1)

        def near(self, holds=()):
            self.sum = added(self.keep, once(self.arrived, holds))
            self.arrived = swap(self.sum, "mp", 2)
            return self.sum

        def far(self, holds=()):
            total = added(self.sum, once(self.arrived, holds))
            return (total, swap(total, "mp", 1))

    last = len(chunks) - 1
    attn, ffn, attn_sums, ffn_sums, attended = [], [], [], [], []
    for n, (c, t) in enumerate(zip(chunks, sources)):
        after = [a[6] for a in attn[-1:]] + [m.sum for m in attn_sums[-2:-1]]
        a = attn_fwd(
            c, place, t, gain_attn, w_query, w_key, w_value, w_out, bias, keep_col, after
        )
        attn.append(a)
        attn_sums.append(MpSum(a[6], a[7]))
        if n >= 1:
            attn_sums[n - 1].near([a[6]])
        if n >= 2:
            attended.append(attn_sums[n - 2].far([a[6]]))
    done, summed = attn[-1][6], attn_sums[-2].sum
    for n, (c, t) in enumerate(zip(chunks, sources)):
        f = ffn_fwd(
            c, place, t, *attended[n], gain_ffn, w_gate, w_up, w_down, [done, summed]
        )
        done = f[2]
        ffn.append(f)
        ffn_sums.append(MpSum(f[2], f[3]))
        summed = (attn_sums[last] if n == 0 else ffn_sums[n - 1]).near([done])
        if len(attended) <= last and n >= 1:
            attended.append(attn_sums[len(attended)].far([done]))
    ffn_sums[last].near()

    lane_block, output = query_embed(
        place,
        ffn[0][0],
        *ffn_sums[0].far([done]),
        gain_final,
        w_proj,
        lane_count * query_len,
        [ffn_sums[last].sum],
    )
    outputs = [output]
    queries = dp_gather(lane_block).reshape(lane_tokens, emb_width)
    emb = None
    lses = []
    done = queries
    sums = [ffn_sums[1].far(), ffn_sums[2].far()]
    for p in range(docs_here):
        if p >= 1 and len(sums) < docs_here:
            sums.append(ffn_sums[len(sums) + 1].far([done]))
        emb, lse, output = doc_embed(
            p,
            place,
            ffn[p + 1][0],
            *sums[p],
            gain_final,
            w_proj,
            queries,
            emb,
            docs_here,
            [sums[p + 1][0]] if p == 0 else [],
        )
        done = lse
        lses.append(lse)
        outputs.append(output)
    own = stats(lses, token_weights, hot, DOC_LEN)
    gathered = dp_gather(own)
    keep, send, query_part, scalars = score_back(
        place, gathered, own, token_weights, hot, emb, queries, lses, DOC_LEN, lane_total, query_total
    )
    doc_sum = MpSum(keep, send)
    query_part = query_part.reshape(dp_count, lane_count * query_len, emb_width)
    query_part = lax.all_to_all(query_part, "dp", 0, 0, tiled=True)
    doc_sum.near()
    doc_grads = doc_sum.far()
    query_here = query_sum(query_part, ())
    query_far = swap(query_here, "mp", 2)
    query_near = swap(query_here, "mp", 1)
    order = list(range(1, docs_here + 1)) + [0]
    count = len(order)
    lengths = [chunks[n][1] for n in order]
    groups = (order[:2], order[2:])
    weights = (gain_final, w_proj, w_gate, w_up, w_down)
    back_first = ffn_bwd(
        lengths[:2],
        pieces,
        place,
        [outputs[n] for n in groups[0]],
        [ffn[n][1] for n in groups[0]],
        doc_grads,
        0,
        [],
        *weights,
        after=[query_far, query_near],
    )
    first_done = [back_first[2]]
    mid_first = MpSum(back_first[2], back_first[3])
    mid_first.near()
    query_far = once(query_far, first_done)
    query_grads = [query_here, query_near, query_far, swap(query_far, "mp", 1)]
    back_rest = ffn_bwd(
        lengths[2:],
        pieces,
        place,
        [outputs[n] for n in groups[1]],
        [ffn[n][1] for n in groups[1]],
        doc_grads,
        DOC_LEN,
        query_grads,
        *weights,
        early=[
            [ffn[n][1] for n in groups[0]],
            back_first[:2],
            back_first[5:8],
            [back_first[4], back_first[8]],
        ],
        after=[mid_first.sum],
    )
    rest_done = [back_rest[2]]
    fgrads = (back_first[:2], back_rest[:2])
    mid_rest = MpSum(back_rest[2], back_rest[3])
    final_gain = back_rest[4]
    up = dp_sum(*back_rest[5:7])
    down = dp_sum(*back_rest[7:9])
    up.start()
    down.start()
    grads_first = mid_first.far(rest_done)
    mid_rest.near(grads_first[:1])

    def attn_chunk(i, grads, position, so_far=(None, None), **more):
        n = order[i]
        return attn_bwd(
            [chunks[n]],
            place,
            [sources[n]],
            [ffn[n][0]],
            [fgrads[i // 2][i % 2]],
            [attn[n][1:5]],
            grads,
            bias,
            gain_ffn,
            w_query,
            w_key,
            w_value,
            w_out,
            keep_col,
            start=position,
            rows=back_first[2].shape[0] if i < 2 else back_rest[2].shape[0],
            so_far=so_far,
            **more,
        )

    half = DOC_LEN // 2
    back0 = attn_chunk(0, grads_first, 0, after=[mid_rest.sum])
    step = [back0[6]]
    up.add(step)
    up.start()
    back1 = attn_chunk(1, grads_first, half, back0[4:6], after=[up.total, back0[6]])
    first_done = [back1[6]]
    up.add(first_done)
    up.start()
    down.add([up.total])
    down.start()
    grads_rest = mid_rest.far([down.total])
    in_first = MpSum(back1[4], back1[5])
    back2 = attn_chunk(2, grads_rest, 0, after=[up.total, down.total, back1[6]])
    step = [back2[6]]
    up.add(step)
    up.start()
    down.add([up.total])
    down.start()
    in_first.near([down.total])
    back3 = attn_chunk(
        3,
        grads_rest,
        half,
        back2[4:6],
        after=[up.total, down.total, in_first.sum, back2[6]],
        pieces=pieces,
        earlier=[[b[n] for b in (back0, back1, back2)] for n in (1, 2, 3, 0)],
        normed=[attn[n][0] for n in order],
        ctx=[attn[n][5] for n in order],
    )
    ends = [back3[6]]
    gain_rows = back0[7] + back1[7] + back2[7] + back3[7]
    diag = back0[6] + back1[6] + back2[6] + back3[6]
    small = jnp.concatenate([gain_rows[:2], final_gain[:1], jnp.zeros((5, width), F32)], axis=0)
    small = jnp.concatenate([small, diag], axis=1)
    heads_sum = dp_sum(*back3[8:10])
    heads_sum.start()
    small_x = swap(small, "dp", 1)
    in_rest = MpSum(back3[4], back3[5])
    up.add(ends)
    up.start()
    step = [down.add([up.total])]
    down.start()
    step = [heads_sum.add(step)]
    heads_sum.start()
    small = small + once(small_x, step)
    arrived = swap(small, "dp", 2)
    step = [up.add([small])]
    up.start()
    input_first = in_first.far(step)
    step = [down.add([input_first[0]])]
    down.start()
    step = [in_rest.near(step)]
    step = [heads_sum.add(step)]
    heads_sum.start()
    small = small + once(arrived, step)
    arrived = swap(small, "dp", 4)
    across = (width, units)

    def landed(pack, step):
        return (pack.total, once(pack.arrived, step) if dp_sum is DpSum else pack.arrived)

    step = [down.add([small])]
    down.start()
    up_grads = unpack(place, pieces, landed(up, step), cut_lanes, [across, across])
    step = [heads_sum.add([up_grads[2]])]
    heads_sum.start()
    small = small + once(arrived, step)
    step = [heads_sum.add([small])]
    heads_sum.start()
    distance = 8
    while distance < dp_count:
        small = small + swap(small, "dp", distance)
        distance *= 2
    over_mp = jnp.concatenate([small[:, :width], scalars], axis=1)
    over_mp = over_mp + swap(over_mp, "mp", 1)
    input_rest = in_rest.far([over_mp])
    down_grads = unpack(
        place,
        pieces,
        landed(down, [input_rest[0]]),
        cut_lanes,
        [(units, width), (width, emb_width)],
        across,
    )
    step = [heads_sum.add([down_grads[2]])]
    heads_sum.start()
    over_mp = over_mp + swap(once(over_mp, step), "mp", 2)
    tokens_grad, query_tokens_grad = tail(
        [chunks[n][1:] for n in order],
        place,
        doc_tokens,
        query_tokens,
        [b[0] for b in (back0, back1, back2, back3)],
        input_first,
        input_rest,
        gain_attn,
        step,
    )
    own_gain = over_mp[:, :width]
    scalars = over_mp[:, width:]
    diag = small[:, width:]
    cols = w_query.shape[0]
    attn_pack = landed(heads_sum, [])
    attn_grads = unpack(place, pieces, attn_pack, cut_rows, [(cols, width)] * 4)

    lane = jnp.arange(WIDE, dtype=jnp.int32)
    offset = jnp.where(lane < DOC_LEN, -lane, WIDE - lane)
    distance = jnp.abs(offset)
    far = 8 + sum(((distance >= edge).astype(jnp.int32) for edge in EDGES))
    index = jnp.where(distance < 8, distance, far) + 16 * (offset > 0).astype(jnp.int32)
    onehot = (jnp.arange(bias_table.shape[0], dtype=jnp.int32)[:, None] == index[None]).astype(F32)
    grad_bias = lax.dot_general(
        onehot, diag[: bias_table.shape[1]], (((1,), (1,)), ((), ())), precision=HIGH
    )
    return (
        scalars[0, 0],
        scalars[1, 0],
        emb,
        tokens_grad,
        query_tokens_grad,
        attn_grads[0].T,
        attn_grads[1].T,
        attn_grads[2].T,
        attn_grads[3],
        up_grads[0],
        up_grads[1],
        down_grads[0],
        down_grads[1],
        own_gain[0],
        small[1, :width],
        small[2, :width],
        grad_bias,
    )


def solution(mesh):
    placed = (
        P("dp", None),
        P("dp", None),
        P(None, "mp"),
        P(None, "mp"),
        P(None, "mp"),
        P("mp", None),
        P(None, "mp"),
        P(None, "mp"),
        P("mp", None),
        P(),
        P(),
        P(),
        P(),
        P(None, "mp"),
        P(),
        P(None, None, "dp"),
        P(),
    )
    return jax.shard_map(
        on_device,
        mesh=mesh,
        in_specs=placed,
        out_specs=(
            P(),
            P(),
            P("dp", None),
            P("dp", None),
            P("dp", None),
            P(None, "mp"),
            P(None, "mp"),
            P(None, "mp"),
            P("mp", None),
            P(None, "mp"),
            P(None, "mp"),
            P("mp", None),
            P(),
            P(),
            P(),
            P(),
            P(None, "mp"),
        ),
        check_vma=False,
    )
```

```python
import functools
import math

import jax
import jax.numpy as jnp
from jax import lax
from jax.experimental import pallas as pl
from jax.experimental.pallas import tpu as pltpu
from jax.sharding import PartitionSpec as P

DOC_LEN = 512
EPS = 1e-06
DOC_TEMP = 32.0
EDGES = (12, 16, 23, 32, 46, 64, 91)
HIGH = lax.Precision.HIGHEST
MASKED = -1000000000.0
BF = jnp.bfloat16
F32 = jnp.float32
WIDE = 2 * DOC_LEN
GELU_A = math.sqrt(2.0 / math.pi)
GELU_B = 0.044715


def nn(a, b):
    return jnp.dot(a, b, preferred_element_type=F32)


def nt(a, b):
    return lax.dot_general(a, b, (((1,), (1,)), ((), ())), preferred_element_type=F32)


def tn(a, b):
    return lax.dot_general(a, b, (((0,), (0,)), ((), ())), preferred_element_type=F32)


def rinv(v):
    return lax.rsqrt(jnp.mean(v * v, axis=-1, keepdims=True) + EPS)


def norm_back(v, r, gain, grad):
    scaled = grad * gain
    return r * scaled - v * (r * r * r * jnp.mean(scaled * v, axis=-1, keepdims=True))


def rowsum8(v):
    return jnp.broadcast_to(jnp.sum(v, axis=0, keepdims=True), (8, v.shape[1]))


def halves(place, half):
    mine = pl.multiple_of(place[1] * half, half)
    other = pl.multiple_of((1 - place[1]) * half, half)
    return (mine, other)


class Load:
    def __init__(self, start=0, rows=None, pinned=True):
        self.start = start
        self.rows = rows
        self.pinned = pinned

    def shape(self, operand):
        return operand.shape if self.rows is None else (self.rows,) + operand.shape[1:]

    def of(self, ref):
        return ref if self.rows is None else ref.at[pl.ds(self.start, self.rows)]


class Held:
    def __init__(self, ref, copy):
        self.ref = ref
        self.copy = copy
        self.begun = False

    @property
    def shape(self):
        return self.ref.shape

    @property
    def dtype(self):
        return self.ref.dtype


class Operand(Held):
    def ready(self):
        if not self.begun:
            self.begun = True
            self.copy.wait()
        return self.ref

    def __getitem__(self, at):
        return self.ready()[at]


class Result(Held):
    def __getitem__(self, at):
        return self.ref[at]

    def __setitem__(self, at, value):
        self.ref[at] = value

    def done(self):
        if not self.begun:
            self.begun = True
            self.copy.start()


class Rows:
    def __init__(self, first, second):
        self.parts = (first, second)
        self.shape = (2 * first.shape[0],) + first.shape[1:]

    def __getitem__(self, at):
        half = self.shape[0] // 2
        return self.parts[at.start // half][...]


def halved(length):
    return [Load(0, length // 2), Load(length // 2, length // 2)]


LOAD = Load()
PASS = Load(pinned=False)
SMEM = pl.BlockSpec(memory_space=pltpu.SMEM)
FAR = pl.BlockSpec(memory_space=pltpu.HBM)


def sds(shape, dtype):
    return jax.ShapeDtypeStruct(shape, dtype)


class Kept:
    def __init__(self, shape, dtype):
        self.shape = shape
        self.dtype = dtype


def kept(shape, dtype):
    return Kept(shape, dtype)


def call(body, name, outs, in_specs, micros, scratch=(), into=None, after=(), order=()):
    count = len(outs)
    stores = [LOAD] * count
    out_shape = list(outs)
    begun = []
    for k, (whole, start, so_far) in (into or {}).items():
        out_shape[k] = whole
        stores[k] = Load(start, outs[k].shape[0])
        if so_far is not None:
            begun.append((k, so_far))
    after = [so_far for _, so_far in begun] + list(after)

    def run(*operands):
        pinned = [
            pltpu.with_memory_space_constraint(operand, pltpu.HBM) if isinstance(spec, Load) and spec.pinned else operand
            for spec, operand in zip(in_specs, operands)
        ]
        loads = [n for n, spec in enumerate(in_specs) if isinstance(spec, Load)]
        total = len(loads)
        given = len(operands)
        buffers = [
            pltpu.VMEM(in_specs[n].shape(operands[n]), operands[n].dtype) for n in loads
        ] + [pltpu.VMEM(out.shape, out.dtype) for out in outs]

        def kernel(*refs):
            ins = list(refs[:given])
            results = refs[given + len(after) : given + len(after) + count]
            rest = refs[given + len(after) + count :]
            own, held, sems = rest[: len(scratch)], rest[len(scratch) : -1], rest[-1]
            for n in sorted(loads, key=lambda n: order.index(n) if n in order else given + n):
                k = loads.index(n)
                copy = pltpu.make_async_copy(in_specs[n].of(ins[n]), held[k], sems.at[k])
                copy.start()
                ins[n] = Operand(held[k], copy)
            made = []
            for k, result in enumerate(results):
                buffer = held[total + k]
                copy = pltpu.make_async_copy(buffer, stores[k].of(result), sems.at[total + k])
                made.append(Result(buffer, copy))
            body(*ins, *made, *own)
            for n in loads:
                ins[n].ready()
            for result in made:
                result.done()
            for result in made:
                result.copy.wait()

        return pl.pallas_call(
            kernel,
            name=name,
            out_shape=tuple(
                pltpu.HBM(out.shape, out.dtype) if isinstance(out, Kept) else out for out in out_shape
            ),
            in_specs=[FAR if isinstance(spec, Load) else spec for spec in in_specs]
            + [FAR] * len(after),
            out_specs=(FAR,) * count,
            scratch_shapes=list(scratch) + buffers + [pltpu.SemaphoreType.DMA((total + count,))],
            input_output_aliases={given + n: k for n, (k, _) in enumerate(begun)},
            compiler_params=pltpu.CompilerParams(vmem_limit_bytes=48 * 1024 * 1024),
            cost_estimate=pl.CostEstimate(
                flops=int(micros * 5e8), bytes_accessed=int(micros * 1e5), transcendentals=0
            ),
        )(*pinned, *after)

    return run


def bias_into(table, out):
    lane = lax.broadcasted_iota(jnp.int32, (8, WIDE), 1)
    offset = jnp.where(lane < DOC_LEN, -lane, WIDE - lane)
    distance = jnp.abs(offset)
    far = jnp.full_like(distance, 8)
    for edge in EDGES:
        far = far + (distance >= edge).astype(jnp.int32)
    index = jnp.where(distance < 8, distance, far) + jnp.where(offset > 0, 16, 0)
    for head in range(out.shape[0]):
        row = jnp.zeros((8, WIDE), F32)
        for bucket in range(table.shape[1]):
            row = jnp.where(index == bucket, table[head, bucket], row)
        spread = jnp.broadcast_to(row[:1], (DOC_LEN, WIDE))
        rolled = pltpu.roll(spread, 0, 1, stride=1, stride_axis=0)
        out[head] = rolled[:, :DOC_LEN]


def attn_fwd_body(length, masked, heads, *refs):
    place, x, gain, wq, wk, wv, wo, bias = refs[:8]
    pos = 8
    if masked:
        table, bias, refs = bias, refs[-2], refs[:-2] + refs[-1:]
        bias_into(table, bias)
        bias.done()
    keep_col = None
    if masked:
        keep_col = refs[8]
        pos = 9
    normed_o, q_o, k_o, v_o, lse_o, ctx_o, keep_o, send_o, part_s = refs[pos:]
    half = length // 2
    xf = x[...].astype(F32)
    normed = (xf * rinv(xf) * gain[...]).astype(BF)
    normed_o[...] = normed
    normed_o.done()
    q = nt(normed, wq[...]).astype(BF)
    k = nt(normed, wk[...]).astype(BF)
    v = nt(normed, wv[...]).astype(BF)
    q_o[...] = q
    k_o[...] = k
    v_o[...] = v
    for result in (q_o, k_o, v_o):
        result.done()
    width = q.shape[1] // heads
    vt = v.T
    tile = min(length, 256)
    lse_o[...] = jnp.zeros(lse_o.shape, F32)
    for h in range(heads):
        cols = slice(h * width, (h + 1) * width)
        for start in range(0, length, tile):
            span = slice(start, start + tile)
            logits = nt(k[:, cols], q[span, cols]) + bias[h, :length, span]
            if masked:
                logits = jnp.where(query_mask_of(keep_col, length), logits, MASKED)
            top = jnp.max(logits, axis=0, keepdims=True)
            shifted = jnp.exp(logits - top)
            total = jnp.sum(shifted, axis=0, keepdims=True)
            probs = (shifted * (1.0 / total)).astype(BF)
            ctx_t = nn(vt[cols], probs)
            ctx_o[span, cols] = ctx_t.T.astype(BF)
            lse_o[h : h + 1, span] = top + jnp.log(total)
    ctx_o.done()
    lse_o.done()
    part_s[...] = nn(ctx_o[...], wo[...]).astype(BF)
    mine, other = halves(place, half)
    keep_o[...] = part_s[pl.ds(mine, half)]
    send_o[...] = part_s[pl.ds(other, half)]


def query_mask_of(keep_col, length):
    key_row = lax.broadcasted_iota(jnp.int32, (length, length), 0)
    query_row = lax.broadcasted_iota(jnp.int32, (length, length), 1)
    return ((key_row // 32) == (query_row // 32)) & (keep_col[...] > 0)


def attn_fwd(chunk, place, tokens, gain, wq, wk, wv, wo, bias, keep_col, after):
    index, length, masked = chunk
    heads = bias.shape[0]
    cols = wq.shape[0]
    width = tokens.shape[1]
    specs = [SMEM, Load(index * length, length), PASS] + [LOAD] * 4 + [SMEM if masked else LOAD]
    operands = [place, tokens, gain, wq, wk, wv, wo, bias]
    if masked:
        specs.append(PASS)
        operands.append(keep_col)
    small = kept((length, cols), BF)
    part = sds((length // 2, width), BF)
    return call(
        functools.partial(attn_fwd_body, length, masked, heads),
        "attn_fwd",
        (kept((length, width), BF), small, small, small, kept((8, length), F32), small, part, part)
        + ((kept((heads, DOC_LEN, DOC_LEN), F32),) if masked else ()),
        specs,
        0.012 * length,
        [pltpu.VMEM((length, width), BF)],
        after=after,
    )(*operands)


def gelu_parts(gate):
    t = jnp.tanh(GELU_A * (gate + GELU_B * gate * gate * gate))
    return 0.5 * gate * (1.0 + t), t


def ffn_fwd_body(length, place, x, um, uo, gain, wg, wu, wd, middle_o, normed_o, keep_o, send_o):
    half = length // 2
    bases = halves(place, half)
    for n, (u, out) in enumerate(((um, keep_o), (uo, send_o))):
        middle = x[pl.ds(bases[n], half)].astype(F32) + u[...].astype(F32)
        middle_o[n * half : (n + 1) * half] = middle
        normed = (middle * rinv(middle) * gain[...]).astype(BF)
        normed_o[n * half : (n + 1) * half] = normed
        if n == 1:
            middle_o.done()
            normed_o.done()
        act, _ = gelu_parts(nn(normed, wg[...]))
        hidden = (act * nn(normed, wu[...])).astype(BF)
        out[...] = nn(hidden, wd[...]).astype(BF)


def ffn_fwd(chunk, place, tokens, um, uo, gain, wg, wu, wd, after):
    index, length, _ = chunk
    width = tokens.shape[1]
    part = sds((length // 2, width), BF)
    return call(
        functools.partial(ffn_fwd_body, length),
        "ffn_fwd",
        (kept((length, width), F32), kept((length, width), BF), part, part),
        [SMEM, Load(index * length, length)] + [PASS] * 3 + [LOAD] * 3,
        0.01 * length,
        after=after,
        order=(4, 2, 1, 5, 6, 7, 3),
    )(place, tokens, um, uo, gain, wg, wu, wd)


def embed_rows(length, place, middle, fs, gain, wp, emb_s, out_o):
    half = length // 2
    bases = halves(place, half)
    for n in range(2):
        span = slice(n * half, (n + 1) * half)
        out = middle[span] + fs[n][...].astype(F32)
        out_o[span] = out
        if n == 1:
            out_o.done()
        normed = (out * rinv(out) * gain[...]).astype(BF)
        emb_s[pl.ds(bases[n], half)] = nn(normed, wp[...]).astype(BF)


def query_embed_body(length, lane, place, middle, fm, fo, gain, wp, lane_o, out_o, emb_s):
    embed_rows(length, place, middle, (fm, fo), gain, wp, emb_s, out_o)
    lane_o[...] = emb_s[pl.ds(pl.multiple_of(place[0] * lane, lane), lane)]


def query_embed(place, middle, fm, fo, gain, wp, lane, after):
    length = middle.shape[0]
    emb = wp.shape[1]
    return call(
        functools.partial(query_embed_body, length, lane),
        "query_embed",
        (sds((lane, emb), BF), kept(middle.shape, F32)),
        [SMEM, LOAD] + [PASS] * 3 + [LOAD],
        0.004 * length,
        [pltpu.VMEM((length, emb), BF)],
        after=after,
    )(place, middle, fm, fo, gain, wp)


def lane_tile(tokens):
    return min(tokens, 512)


def doc_embed_body(length, place, upper, lower, fm, fo, gain, wp, queries, emb_o, lse_o, out_o):
    middle = Rows(upper, lower)
    embed_rows(length, place, middle, (fm, fo), gain, wp, emb_o, out_o)
    emb_o.done()
    scale = wp.shape[1] ** (-0.5)
    tile = lane_tile(queries.shape[0])
    for start in range(0, queries.shape[0], tile):
        span = slice(start, start + tile)
        scores = nt(emb_o[...], queries[span]) * scale
        top = jnp.max(scores, axis=0, keepdims=True)
        total = jnp.sum(jnp.exp(scores - top), axis=0, keepdims=True)
        lse_o[:, span] = jnp.broadcast_to(top + jnp.log(total), (8, tile))


def doc_embed(index, place, middle, fm, fo, gain, wp, queries, so_far, docs, after):
    length = middle.shape[0]
    emb = wp.shape[1]
    return call(
        functools.partial(doc_embed_body, length),
        "doc_embed",
        (kept((length, emb), BF), sds((8, queries.shape[0]), F32), kept(middle.shape, F32)),
        [SMEM, *halved(length)] + [PASS] * 3 + [LOAD, PASS],
        0.005 * length,
        into={0: (kept((docs * length, emb), BF), index * length, so_far)},
        order=(5, 3, 1, 6, 4, 2, 7),
        after=after,
    )(place, middle, middle, fm, fo, gain, wp, queries)


def segment(tokens, lanes):
    token = lax.broadcasted_iota(jnp.int32, (tokens, lanes), 0) // 32
    return (token == lax.broadcasted_iota(jnp.int32, (tokens, lanes), 1)).astype(F32)


def stats_body(docs, doc_len, *refs):
    lses = refs[:docs]
    weights, hot, out = refs[docs:]
    lanes = hot.shape[1]
    tokens = weights.shape[1]
    seg = segment(tokens, lanes)
    w = weights[...]
    rows = lax.broadcasted_iota(jnp.int32, (8, tokens), 0)
    scores = jnp.zeros((8, tokens), F32)
    for p in range(docs):
        scores = jnp.where(rows == p, lses[p][...], scores)
    scores = w * (scores - jnp.where(rows < docs, math.log(doc_len), 0.0))
    table = DOC_TEMP * jnp.dot(scores, seg, precision=HIGH, preferred_element_type=F32)
    share = jnp.dot(w, seg, precision=HIGH, preferred_element_type=F32)
    lane_rows = lax.broadcasted_iota(jnp.int32, (8, lanes), 0)
    positive = jnp.sum(table * hot[...], axis=0, keepdims=True)
    share = jnp.sum(share * hot[...], axis=0, keepdims=True)
    result = jnp.where(lane_rows < docs, table, 0.0)
    result = jnp.where(lane_rows == docs, positive, result)
    out[...] = jnp.where(lane_rows == docs + 1, share, result)


def stats(lses, weights, hot, doc_len):
    return call(
        functools.partial(stats_body, len(lses), doc_len),
        "doc_stats",
        (sds(hot.shape, F32),),
        [PASS] * (len(lses) + 2),
        0.5,
    )(*lses, weights, hot)[0]


def score_back_body(docs, doc_len, lane_total, query_total, *refs):
    place, gathered, own, weights, hot, emb, queries = refs[:7]
    lses = refs[7 : 7 + docs]
    keep_o, send_o, query_o, scalars_o, doc_s, query_s = refs[7 + docs :]
    lanes = hot.shape[1]
    tokens = weights.shape[1]
    everything = gathered[...]
    rows = lax.broadcasted_iota(jnp.int32, everything.shape, 1)
    scores = jnp.where(rows < docs, everything, -jnp.inf)
    top = jnp.max(jnp.max(scores, axis=0), axis=0, keepdims=True)
    total = jnp.sum(jnp.sum(jnp.exp(scores - top[None]), axis=0), axis=0, keepdims=True)
    log_norm = top + jnp.log(total)
    summed = jnp.sum(everything, axis=0)
    valid = lax.broadcasted_iota(jnp.int32, (1, lanes), 1) < lane_total
    loss = jnp.where(valid, log_norm - summed[docs : docs + 1], 0.0)
    share = jnp.where(valid, summed[docs + 1 : docs + 2], 0.0)
    out_rows = lax.broadcasted_iota(jnp.int32, (8, 128), 0)
    loss = jnp.sum(loss, axis=1, keepdims=True) / query_total
    share = jnp.sum(share, axis=1, keepdims=True) / query_total
    scalars_o[...] = jnp.where(out_rows == 0, loss, share)
    own_rows = lax.broadcasted_iota(jnp.int32, own.shape, 0)
    grads = DOC_TEMP * (jnp.exp(own[...] - log_norm) - hot[...]) / query_total
    grads = jnp.where(own_rows < docs, grads, 0.0)
    seg = segment(tokens, lanes)
    spread = lax.dot_general(
        grads, seg, (((1,), (1,)), ((), ())), precision=HIGH, preferred_element_type=F32
    )
    token_grad = spread * weights[...]
    emb_width = queries.shape[1]
    scale = emb_width ** (-0.5)
    half = doc_len // 2
    bases = halves(place, half)
    tile = lane_tile(tokens)
    for start in range(0, tokens, tile):
        span = slice(start, start + tile)
        query = queries[span]
        query_grad = jnp.zeros((emb_width, tile), F32)
        for p in range(docs):
            doc = emb[p * doc_len : (p + 1) * doc_len]
            scores = nt(doc, query) * scale
            grad = (token_grad[p : p + 1, span] * jnp.exp(scores - lses[p][:1, span])).astype(BF)
            part = nn(grad, query) * scale
            if start == 0:
                doc_s[p * doc_len : (p + 1) * doc_len] = part
            else:
                doc_s[p * doc_len : (p + 1) * doc_len] += part
            query_grad = query_grad + nn(doc.T, grad)
        query_o[span] = (query_grad * scale).T.astype(BF)
    for p in range(docs):
        keep_o[p * half : (p + 1) * half] = doc_s[pl.ds(p * doc_len + bases[0], half)].astype(BF)
        send_o[p * half : (p + 1) * half] = doc_s[pl.ds(p * doc_len + bases[1], half)].astype(BF)


def score_back(place, gathered, own, weights, hot, emb, queries, lses, doc_len, lane_total, query_total):
    docs = len(lses)
    width = emb.shape[1]
    part = sds((docs * doc_len // 2, width), BF)
    return call(
        functools.partial(score_back_body, docs, doc_len, lane_total, query_total),
        "score_back",
        (part, part, sds(queries.shape, BF), sds((8, 128), F32)),
        [SMEM] + [PASS] * 4 + [LOAD] + [PASS] * (1 + docs),
        3.0,
        [pltpu.VMEM((docs * doc_len, width), F32), pltpu.VMEM((8, 128), F32)],
    )(place, gathered, own, weights, hot, emb, queries, *lses)


def query_sum_body(parts, out):
    out[...] = jnp.sum(parts[...].astype(F32), axis=0).astype(BF)


def query_sum(parts, after):
    return call(
        query_sum_body, "query_sum", (sds(parts.shape[1:], BF),), [PASS], 1.5, after=after
    )(parts)[0]


def ffn_bwd_body(lengths, masked, pieces, early, *refs):
    refs = list(refs)
    count = len(lengths)

    def take(number):
        taken = refs[:number]
        del refs[:number]
        return taken

    (place,) = take(1)
    finals, normeds = [Rows(*take(2)) for _ in range(count)], take(count)
    doc_mine, doc_other = take(2)
    query_grads = take(4 if masked else 0)
    gain_final, wp, wg, wu, wd = take(5)
    early_normeds, early_fgrads = take(early), take(early)
    early_inner, early_sums = (take(3), take(2)) if early else ((), ())
    fgrads = take(count)
    keep_o, send_o, gain_o = take(3)
    if early:
        packs = take(4)
        emb_s, hidden, ggrad, ugrad, up_s, down_s = refs
    else:
        hidden, ggrad, ugrad, proj_o = refs
    width = finals[0].shape[1]
    units = hidden.shape[1]
    gain_sum = jnp.zeros((1, width), F32)
    proj = jnp.zeros((wp.shape[1], width), F32)
    at = 0
    for c, length in enumerate(lengths):
        half = length // 2
        bases = halves(place, half)
        if masked and c == count - 1:
            lane = query_grads[0].shape[0]
            for step, grad in enumerate(query_grads):
                emb_s[pl.ds(pl.multiple_of((place[0] ^ step) * lane, lane), lane)] = grad[...]
            egs = [emb_s[pl.ds(base, half)] for base in bases]
        else:
            egs = [grad[c * half : (c + 1) * half] for grad in (doc_mine, doc_other)]
        for n, out in enumerate((keep_o, send_o)):
            span = slice(n * half, (n + 1) * half)
            rows = slice(at + n * half, at + (n + 1) * half)
            output = finals[c][span]
            r = rinv(output)
            dn = nt(egs[n], wp[...])
            unit = output * r
            gain_sum = gain_sum + jnp.sum(dn * unit, axis=0, keepdims=True)
            proj = proj + nn(egs[n].T, (unit * gain_final[...]).astype(BF))
            fgrad = norm_back(output, r, gain_final[...], dn).astype(BF)
            fgrads[c][span] = fgrad
            if n == 1:
                fgrads[c].done()
            gate = nn(normeds[c][span], wg[...])
            up = nn(normeds[c][span], wu[...])
            act, t = gelu_parts(gate)
            hidden[rows] = (act * up).astype(BF)
            hgrad = nt(fgrad, wd[...])
            slope = 0.5 * (1.0 + t) + 0.5 * gate * (1.0 - t * t) * (
                GELU_A * (1.0 + 3.0 * GELU_B * gate * gate)
            )
            gg = (hgrad * up * slope).astype(BF)
            ug = (hgrad * act).astype(BF)
            ggrad[rows] = gg
            ugrad[rows] = ug
            out[at // 2 : at // 2 + half] = (nt(gg, wg[...]) + nt(ug, wu[...])).astype(BF)
        at += length
    send_o.done()
    keep_o.done()
    if not early:
        gain_o[...] = jnp.broadcast_to(gain_sum, gain_o.shape)
        proj_o[...] = proj
        return
    gain_o[...] = jnp.broadcast_to(gain_sum, gain_o.shape) + early_sums[0][...]
    proj = proj + early_sums[1][...]

    def total(lefts, own, earlier, span):
        result = 0.0
        at = 0
        for c, left in enumerate(lefts):
            if c == early:
                at = 0
            right = earlier if c < early else own
            rows = slice(at, at + left.shape[0])
            result = result + tn(left[:, span], right[rows])
            at += left.shape[0]
        return result.astype(BF)

    rows = width // pieces
    lefts = early_normeds + normeds
    blocks = ((up_s, 0, lefts, early_inner[1], ggrad), (up_s, 1, lefts, early_inner[2], ugrad))
    blocks += ((down_s, 0, early_fgrads + fgrads, early_inner[0], hidden),)
    for out, k, left, earlier, own in blocks:
        lanes = slice(k * units, (k + 1) * units)
        for start in range(0, width, 4 * rows):
            value = total(left, own, earlier, slice(start, start + 4 * rows))
            relative_store(out, value, place[2], pieces, rows, start // rows, lanes)
        if k == 1:
            split_out(up_s, *packs[:2])
            packs[1].done()
            packs[0].done()
    lanes = slice(units, down_s.shape[1])
    relative_store(down_s, proj.T.astype(BF), place[2], pieces, rows, 0, lanes)
    split_out(down_s, *packs[2:])


def ffn_bwd(
    lengths, pieces, place, finals, normeds, doc_grads, doc_at, query_grads, gain, wp, wg, wu, wd,
    early=(), after=(),
):
    masked = len(query_grads) > 0
    count = len(lengths)
    docs = count - 1 if masked else count
    width = finals[0].shape[1]
    emb = wp.shape[1]
    units = wg.shape[1]
    rows = sum(lengths)
    part = sds((rows // 2, width), BF)
    outs = tuple(kept((length, width), BF) for length in lengths)
    outs += (part, part, sds((8, width), F32))
    doc_rows = sum(lengths[:docs]) // 2
    grads = Load(doc_at, doc_rows, pinned=False)
    specs = [SMEM] + [spec for length in lengths for spec in halved(length)] + [LOAD] * count
    specs += [grads] * 2 + [PASS] * len(query_grads)
    specs += [PASS] + [LOAD] * 4
    extra = []
    first = 1 + 3 * count
    gates = first + 2 + len(query_grads)
    order = [gates, first, first + 1, gates + 1, 1, 1 + 2 * count, gates + 2, gates + 3]
    order += [gates + 4, 2]
    if early:
        number = len(early[0])
        extra = [*early[0], *early[1], *early[2], *early[3]]
        specs += [LOAD] * (2 * number + 3) + [PASS] * 2
        base = gates + 5
        order += list(range(3, first)) + list(range(base, base + number))
        order += [base + 2 * number + k for k in (1, 2, 0)]
        up = sds((width // 2, 2 * units), BF)
        down = sds((width // 2, units + emb), BF)
        outs += (up, up, down, down)
        inner = pltpu.VMEM((rows, units), BF)
        scratch = [
            pltpu.VMEM((lengths[-1], emb), BF),
            inner,
            inner,
            inner,
            pltpu.VMEM((width, 2 * units), BF),
            pltpu.VMEM((width, units + emb), BF),
        ]
    else:
        outs += (kept((rows, units), BF),) * 3 + (sds((emb, width), F32),)
        scratch = []
    return call(
        functools.partial(
            ffn_bwd_body, lengths, masked, pieces, len(early[0]) if early else 0
        ),
        "ffn_bwd",
        outs,
        specs,
        14.0,
        scratch,
        order=order,
        after=after,
    )(
        place,
        *[array for array in finals for _ in range(2)],
        *normeds,
        *doc_grads,
        *query_grads,
        gain,
        wp,
        wg,
        wu,
        wd,
        *extra,
    )


def relative_store(out, value, base, pieces, rows, first, lanes):
    for n in range(value.shape[0] // rows):
        slot = reversed_bits(first + n, pieces) ^ base
        out[pl.ds(pl.multiple_of(slot * rows, rows), rows), lanes] = value[n * rows : (n + 1) * rows]


def reversed_bits(number, count):
    result = 0
    while count > 1:
        result = result * 2 + number % 2
        number //= 2
        count //= 2
    return result


def split_out(out, keep_o, send_o):
    half = out.shape[0] // 2
    keep_o[...] = out[:half]
    send_o[...] = out[half:]


def unpack_body(pieces, rows, count, cut, results, *refs):
    place = refs[0]
    parts = [part.ready() for part in refs[1 : 1 + count]]
    outs = list(refs[1 + count : 1 + count + results])
    refs[1 + count + results][...] = jnp.zeros((8, 128), F32)
    turned = refs[2 + count + results :]
    if turned:
        outs[0] = turned[0]
    for number in range(pieces):
        slot = reversed_bits(number, pieces) ^ place[2]
        for part, base in zip(parts, (0, pieces // 2)):

            @pl.when((slot >= base) & (slot < base + part.shape[0] // rows))
            def _(part=part, base=base):
                start = pl.multiple_of((slot - base) * rows, rows)
                value = part[pl.ds(start, rows)].astype(F32)
                cut(outs, number * rows, rows, value)

    if turned:
        refs[1 + count][...] = turned[0][...].T


def cut_lanes(outs, at, rows, value):
    lane = 0
    for out in outs:
        out[at : at + rows] = value[:, lane : lane + out.shape[1]]
        lane += out.shape[1]


def cut_rows(outs, at, rows, value):
    n, at = divmod(at, outs[0].shape[0])
    outs[n][at : at + rows] = value


def unpack(place, pieces, parts, cut, shapes, turned=None):
    rows = sum(part.shape[0] for part in parts) // pieces
    return call(
        functools.partial(unpack_body, pieces, rows, len(parts), cut, len(shapes)),
        "unpack",
        tuple(kept(shape, F32) for shape in shapes) + (sds((8, 128), F32),),
        [SMEM] + [PASS] * len(parts),
        2.0,
        [pltpu.VMEM(turned, F32)] if turned else [],
    )(place, *parts)


def diagonal_sums(block):
    length = block.shape[0]
    rows = length
    value = jnp.concatenate([block, jnp.zeros((rows, WIDE - length), F32)], axis=1)
    while rows > 8:
        rows //= 2
        value = value[:rows] + pltpu.roll(value[rows:], WIDE - rows, 1)
    total = value[0:1]
    for s in range(1, 8):
        total = total + pltpu.roll(jnp.broadcast_to(value[s : s + 1], (8, WIDE)), WIDE - s, 1)[:1]
    return total


def attn_bwd_chunk(place, length, masked, heads, ins, shared, outs, sums, base, ctx_s):
    x, mid, gm, go, g_at, fgrad, q, k, v, lse = ins
    bias, gain, wq, wk, wv, wo, keep_col = shared
    agrad_o, dq_o, dk_o, dv_o, keep_o, send_o = outs
    half = length // 2
    bases = halves(place, half)
    for n, g in enumerate((gm, go)):
        rows = pl.ds(bases[n], half)
        middle = mid[n * half : (n + 1) * half]
        r = rinv(middle)
        dn = g[g_at : g_at + half].astype(F32)
        sums["ffn"] = sums["ffn"] + jnp.sum(dn * (middle * r), axis=0, keepdims=True)
        grad = fgrad[n * half : (n + 1) * half].astype(F32) + norm_back(middle, r, gain[...], dn)
        agrad = grad.astype(BF)
        agrad_o[rows] = agrad
        ctx_s[rows] = nt(agrad, wo[...]).astype(BF)
    agrad_o.done()
    width = q.shape[1] // heads
    tile = min(length, 256)
    kt = k[...].T
    for h in range(heads):
        cols = slice(h * width, (h + 1) * width)
        kh = k[:, cols]
        vh = v[:, cols]
        dk = jnp.zeros((length, width), F32)
        dv = jnp.zeros((length, width), F32)
        pieces = []
        for start in range(0, length, tile):
            span = slice(start, start + tile)
            qh = q[span, cols]
            ch = ctx_s[span, cols]
            logits = nt(kh, qh) + bias[h, :length, span]
            if masked:
                logits = jnp.where(query_mask_of(keep_col, length), logits, MASKED)
            probs = jnp.exp(logits - lse[h : h + 1, span])
            pgrad = nt(vh, ch)
            delta = jnp.sum(probs * pgrad, axis=0, keepdims=True)
            lgrad = (probs * (pgrad - delta)).astype(BF)
            dv = dv + nn(probs.astype(BF), ch)
            dk = dk + nn(lgrad, qh)
            dq_o[span, cols] = nn(kt[cols], lgrad).T.astype(BF)
            pieces.append(lgrad)
        dk_o[:, cols] = dk.astype(BF)
        dv_o[:, cols] = dv.astype(BF)
        lgrad = jnp.concatenate(pieces, axis=1) if len(pieces) > 1 else pieces[0]
        sums["diag"][h] = sums["diag"][h] + diagonal_sums(lgrad.astype(F32))
    for result in (dq_o, dk_o, dv_o):
        result.done()
    part = nn(dq_o[...], wq[...]) + nn(dk_o[...], wk[...]) + nn(dv_o[...], wv[...])
    xf = x[...].astype(F32)
    sums["attn"] = sums["attn"] + jnp.sum(part * (xf * rinv(xf)), axis=0, keepdims=True)
    return part.astype(BF)


def attn_bwd_body(group, heads, pieces, weights, *refs):
    refs = list(refs)
    size = len(group)
    others = weights - size if weights else 0

    def take(number):
        taken = refs[:number]
        del refs[:number]
        return taken

    (place,) = take(1)
    x = take(size)
    mid, fgrad = ([Rows(*take(2)) for _ in range(size)] for _ in range(2))
    q, k, v, lse = (take(size) for _ in range(4))
    gm, go, bias, gain, wq, wk, wv, wo, keep_col = take(9)
    earlier = [take(others) for _ in range(4)]
    normed, ctx = take(weights), take(weights)
    agrad, dq, dk, dv = (take(size) for _ in range(4))
    keep_o, send_o, diag_o, gain_o = take(4)
    packs = take(2) if weights else None
    ctx_s, part_s = take(2)
    width = x[0].shape[1]
    sums = {
        "ffn": jnp.zeros((1, width), F32),
        "attn": jnp.zeros((1, width), F32),
        "diag": [jnp.zeros((1, WIDE), F32)] * heads,
    }
    at = 0
    for c, (length, masked) in enumerate(group):
        half = length // 2
        part = attn_bwd_chunk(
            place,
            length,
            masked,
            heads,
            (x[c], mid[c], gm, go, at, fgrad[c], q[c], k[c], v[c], lse[c]),
            (bias, gain, wq, wk, wv, wo, keep_col),
            (agrad[c], dq[c], dk[c], dv[c], keep_o, send_o),
            sums,
            at,
            ctx_s,
        )
        part_s[:length] = part
        bases = halves(place, half)
        keep_o[at : at + half] = part_s[pl.ds(bases[0], half)]
        send_o[at : at + half] = part_s[pl.ds(bases[1], half)]
        at += half
    send_o.done()
    keep_o.done()
    diag_o[...] = jnp.zeros(diag_o.shape, F32)
    for h in range(heads):
        diag_o[h : h + 1] = sums["diag"][h]
    row = lax.broadcasted_iota(jnp.int32, gain_o.shape, 0)
    gain_o[...] = jnp.where(row == 0, sums["attn"], sums["ffn"])
    if weights:
        pack_s = refs[0]
        cols = q[0].shape[1]
        rows = pack_s.shape[0] // pieces
        every = [old + new for old, new in zip(earlier, (dq, dk, dv, agrad))]
        pairs = ((every[0], normed), (every[1], normed), (every[2], normed), (ctx, every[3]))
        for n, (left, right) in enumerate(pairs):
            total = sum(tn(a[...], b[...]) for a, b in zip(left, right)).astype(BF)
            relative_store(pack_s, total, place[2], pieces, rows, n * cols // rows, slice(0, width))
        split_out(pack_s, *packs)


def attn_bwd(
    group, place, xs, mids, fgrads, heads_kept, gs, bias, gain, wq, wk, wv, wo, keep_col,
    pieces=0, earlier=None, normed=(), ctx=(), after=(), start=0, rows=0, so_far=(None, None),
):
    heads = bias.shape[0]
    size = len(group)
    cols = wq.shape[0]
    width = wq.shape[1]
    weights = len(normed)
    others = weights - size if weights else 0
    longest = max(length for _, length, _ in group)
    part = sds((sum(length for _, length, _ in group) // 2, width), BF)
    outs = tuple(kept((length, width), BF) for _, length, _ in group)
    outs += tuple(kept((length, cols), BF) for _, length, _ in group) * 3
    outs += (part, part, sds((8, WIDE), F32), sds((8, width), F32))
    scratch = [pltpu.VMEM((longest, cols), BF), pltpu.VMEM((longest, width), BF)]
    if weights:
        outs += (sds((2 * cols, width), BF),) * 2
        scratch.append(pltpu.VMEM((4 * cols, width), BF))
    specs = [SMEM] + [Load(index * length, length) for index, length, _ in group]
    sums = Load(start, part.shape[0], pinned=False)
    specs += [spec for _ in range(2) for _, length, _ in group for spec in halved(length)]
    specs += [LOAD] * (4 * size) + [sums] * 2 + [LOAD, PASS] + [LOAD] * 4 + [PASS]
    specs += [LOAD] * (4 * others + 2 * weights)
    operands = [place, *xs] + [array for array in (*mids, *fgrads) for _ in range(2)]
    operands += [kept_heads[i] for i in range(4) for kept_heads in heads_kept]
    operands += [*gs, bias, gain, wq, wk, wv, wo, keep_col]
    operands += [array for arrays in (earlier or ()) for array in arrays]
    operands += [*normed, *ctx]
    g = 1 + 9 * size
    h = 1 + 5 * size
    order = [g + 3, 1 + size, g, 1 + 3 * size, g + 7, 2 + size, g + 1, 2 + 3 * size]
    order += [h + size, h, h + 2 * size, h + 3 * size, g + 2, g + 4, g + 5, g + 6, 1]
    return call(
        functools.partial(
            attn_bwd_body, [(length, masked) for _, length, masked in group], heads, pieces, weights
        ),
        "attn_bwd",
        outs,
        specs,
        9.0 * size,
        scratch,
        after=after,
        order=order,
        into={
            4 * size + n: (sds((rows or part.shape[0], width), BF), start, so_far[n]) for n in range(2)
        },
    )(*operands)


def tail_body(group, *refs):
    refs = list(refs)
    size = len(group)

    def take(number):
        taken = refs[:number]
        del refs[:number]
        return taken

    (place, x_doc, x_query), agrad, grads = take(3), take(size), take(4)
    gain, doc_o, query_o = refs
    at = [0, 0]
    for c, (length, masked) in enumerate(group):
        half = length // 2
        bases = halves(place, half)
        pair = 0 if c < 2 else 1
        x, out, base = (x_query, query_o, 0) if masked else (x_doc, doc_o, c * length)
        for n in range(2):
            rows = pl.ds(base + bases[n], half)
            xf = x[rows].astype(F32)
            dn = grads[2 * pair + n][at[pair] : at[pair] + half].astype(F32)
            own = agrad[c][pl.ds(bases[n], half)].astype(F32)
            out[rows] = (own + norm_back(xf, rinv(xf), gain[...], dn)).astype(BF)
        at[pair] += half


def tail(group, place, doc_tokens, query_tokens, agrads, first, rest, gain, after):
    return call(
        functools.partial(tail_body, group),
        "tokens_grad",
        (kept(doc_tokens.shape, BF), kept(query_tokens.shape, BF)),
        [SMEM] + [LOAD] * (2 + len(group)) + [PASS] * 5,
        8.0,
        after=after,
    )(place, doc_tokens, query_tokens, *agrads, *first, *rest, gain)


def swap(block, axis, distance):
    count = lax.axis_size(axis)
    return lax.ppermute(block, axis, [(i, i ^ distance) for i in range(count)])


def added(a, b):
    return (a.astype(F32) + b.astype(F32)).astype(BF)


def once(value, earlier):
    if not earlier:
        return value
    return lax.optimization_barrier((value, *earlier))[0]


class DpSum:
    def __init__(self, keep, send):
        self.keep = keep
        self.send = send
        self.distance = 1
        self.count = lax.axis_size("dp")
        self.total = None

    def start(self, holds=()):
        if self.distance < self.count:
            self.arrived = swap(once(self.send, holds), "dp", self.distance)
        else:
            self.back //= 2
            self.arrived = swap(once(self.total, holds), "dp", self.back)

    def add(self, holds=()):
        if self.distance < self.count:
            self.total = added(self.keep, once(self.arrived, holds))
            self.distance *= 2
            self.back = self.count
            if self.distance < self.count:
                half = self.total.shape[0] // 2
                self.keep, self.send = self.total[:half], self.total[half:]
        else:
            self.total = jnp.concatenate([self.total, once(self.arrived, holds)], axis=0)
        return self.total


class DpWhole:
    def __init__(self, keep, send):
        self.total, self.arrived = lax.psum((keep, send), "dp")

    def start(self, holds=()):
        pass

    def add(self, holds=()):
        return self.total

def dp_gather(block):
    count = lax.axis_size("dp")
    spread = jnp.broadcast_to(block[None], (count,) + block.shape)
    return lax.all_to_all(spread, "dp", 0, 0, tiled=True)


def on_device(
    doc_tokens,
    query_tokens,
    w_query,
    w_key,
    w_value,
    w_out,
    w_gate,
    w_up,
    w_down,
    w_proj,
    gain_attn,
    gain_ffn,
    gain_final,
    bias_table,
    query_mask,
    retrieval_mask,
    positives,
):
    dp_count = lax.axis_size("dp")
    mp_count = lax.axis_size("mp")
    dp_index = lax.axis_index("dp")
    mp_index = lax.axis_index("mp")
    query_len = query_mask.shape[1]
    docs_here = doc_tokens.shape[0] // DOC_LEN
    queries_here = query_tokens.shape[0] // query_len
    query_total = dp_count * queries_here
    width = doc_tokens.shape[1]
    emb_width = w_proj.shape[1]
    units = w_gate.shape[1]
    lane_count = queries_here // mp_count
    lane_total = lane_count * dp_count
    lane_tokens = lane_total * query_len
    lane_pad = -(-lane_total // 128) * 128
    pieces = 8
    order_here = sum(((dp_index >> bit) & 1) << (2 - bit) for bit in range(3))
    if dp_count != pieces:
        order_here = jnp.zeros_like(dp_index)
    place = jnp.stack([mp_index, mp_index % 2, order_here]).astype(jnp.int32)
    w_query = w_query.T
    w_key = w_key.T
    w_value = w_value.T
    gain_attn = gain_attn.reshape(1, width)
    gain_ffn = gain_ffn.reshape(1, width)
    gain_final = gain_final.reshape(1, width)
    home_keep = lax.dynamic_slice_in_dim(query_mask, dp_index * queries_here, queries_here, 0)
    keep_col = home_keep.astype(F32).reshape(-1, 1)

    def lane_view(whole):
        grouped = whole.reshape((dp_count, queries_here) + whole.shape[1:])
        picked = lax.dynamic_slice_in_dim(grouped, mp_index * lane_count, lane_count, 1)
        return picked.reshape((lane_total,) + whole.shape[1:])

    lane_keep = lane_view(query_mask).astype(F32)
    lane_hits = lane_view(retrieval_mask).astype(F32)
    token_weights = lane_keep[:, :, None] * lane_hits / jnp.sum(lane_keep, axis=1)[:, None, None]
    token_weights = token_weights.reshape(lane_tokens, docs_here).T
    token_weights = jnp.pad(token_weights, ((0, 8 - docs_here), (0, 0)))
    doc_ids = dp_index * docs_here + jnp.arange(8, dtype=jnp.int32)
    doc_ids = jnp.where(jnp.arange(8) < docs_here, doc_ids, -1)
    lane_positive = jnp.pad(lane_view(positives), (0, lane_pad - lane_total), constant_values=-2)
    hot = (lane_positive[None, :] == doc_ids[:, None]).astype(F32)

    chunks = [(0, query_tokens.shape[0], True)] + [(p, DOC_LEN, False) for p in range(docs_here)]
    bias = bias_table.T
    sources = [query_tokens] + [doc_tokens] * docs_here
    dp_sum = DpSum if dp_count == pieces else DpWhole

    class MpSum:
        def __init__(self, keep, send):
            self.keep = keep
            self.arrived = swap(send, "mp", 1)

        def near(self, holds=()):
            self.sum = added(self.keep, once(self.arrived, holds))
            self.arrived = swap(self.sum, "mp", 2)
            return self.sum

        def far(self, holds=()):
            total = added(self.sum, once(self.arrived, holds))
            return (total, swap(total, "mp", 1))

    last = len(chunks) - 1
    attn, ffn, attn_sums, ffn_sums, attended = [], [], [], [], []
    for n, (c, t) in enumerate(zip(chunks, sources)):
        after = [a[6] for a in attn[-1:]] + [m.sum for m in attn_sums[-2:-1]]
        a = attn_fwd(
            c, place, t, gain_attn, w_query, w_key, w_value, w_out, bias, keep_col, after
        )
        if n == 0:
            bias = a[8]
        attn.append(a)
        attn_sums.append(MpSum(a[6], a[7]))
        if n >= 1:
            attn_sums[n - 1].near([a[6]])
        if n >= 2:
            attended.append(attn_sums[n - 2].far([a[6]]))
    done, summed = attn[-1][6], attn_sums[-2].sum
    for n, (c, t) in enumerate(zip(chunks, sources)):
        f = ffn_fwd(
            c, place, t, *attended[n], gain_ffn, w_gate, w_up, w_down, [done, summed]
        )
        done = f[2]
        ffn.append(f)
        ffn_sums.append(MpSum(f[2], f[3]))
        summed = (attn_sums[last] if n == 0 else ffn_sums[n - 1]).near([done])
        if len(attended) <= last and n >= 1:
            attended.append(attn_sums[len(attended)].far([done]))
    ffn_sums[last].near()

    lane_block, output = query_embed(
        place,
        ffn[0][0],
        *ffn_sums[0].far([done]),
        gain_final,
        w_proj,
        lane_count * query_len,
        [ffn_sums[last].sum],
    )
    outputs = [output]
    queries = dp_gather(lane_block).reshape(lane_tokens, emb_width)
    emb = None
    lses = []
    done = queries
    sums = [ffn_sums[1].far(), ffn_sums[2].far()]
    for p in range(docs_here):
        if p >= 1 and len(sums) < docs_here:
            sums.append(ffn_sums[len(sums) + 1].far([done]))
        emb, lse, output = doc_embed(
            p,
            place,
            ffn[p + 1][0],
            *sums[p],
            gain_final,
            w_proj,
            queries,
            emb,
            docs_here,
            [sums[p + 1][0]] if p == 0 else [],
        )
        done = lse
        lses.append(lse)
        outputs.append(output)
    own = stats(lses, token_weights, hot, DOC_LEN)
    gathered = dp_gather(own)
    keep, send, query_part, scalars = score_back(
        place, gathered, own, token_weights, hot, emb, queries, lses, DOC_LEN, lane_total, query_total
    )
    doc_sum = MpSum(keep, send)
    query_part = query_part.reshape(dp_count, lane_count * query_len, emb_width)
    query_part = lax.all_to_all(query_part, "dp", 0, 0, tiled=True)
    doc_sum.near()
    doc_grads = doc_sum.far()
    query_here = query_sum(query_part, ())
    query_far = swap(query_here, "mp", 2)
    query_near = swap(query_here, "mp", 1)
    order = list(range(1, docs_here + 1)) + [0]
    count = len(order)
    lengths = [chunks[n][1] for n in order]
    groups = (order[:2], order[2:])
    weights = (gain_final, w_proj, w_gate, w_up, w_down)
    back_first = ffn_bwd(
        lengths[:2],
        pieces,
        place,
        [outputs[n] for n in groups[0]],
        [ffn[n][1] for n in groups[0]],
        doc_grads,
        0,
        [],
        *weights,
        after=[query_far, query_near],
    )
    first_done = [back_first[2]]
    mid_first = MpSum(back_first[2], back_first[3])
    mid_first.near()
    query_far = once(query_far, first_done)
    query_grads = [query_here, query_near, query_far, swap(query_far, "mp", 1)]
    back_rest = ffn_bwd(
        lengths[2:],
        pieces,
        place,
        [outputs[n] for n in groups[1]],
        [ffn[n][1] for n in groups[1]],
        doc_grads,
        DOC_LEN,
        query_grads,
        *weights,
        early=[
            [ffn[n][1] for n in groups[0]],
            back_first[:2],
            back_first[5:8],
            [back_first[4], back_first[8]],
        ],
        after=[mid_first.sum],
    )
    rest_done = [back_rest[2]]
    fgrads = (back_first[:2], back_rest[:2])
    mid_rest = MpSum(back_rest[2], back_rest[3])
    final_gain = back_rest[4]
    up = dp_sum(*back_rest[5:7])
    down = dp_sum(*back_rest[7:9])
    up.start()
    down.start()
    grads_first = mid_first.far(rest_done)
    mid_rest.near(grads_first[:1])

    def attn_chunk(i, grads, position, so_far=(None, None), **more):
        n = order[i]
        return attn_bwd(
            [chunks[n]],
            place,
            [sources[n]],
            [ffn[n][0]],
            [fgrads[i // 2][i % 2]],
            [attn[n][1:5]],
            grads,
            bias,
            gain_ffn,
            w_query,
            w_key,
            w_value,
            w_out,
            keep_col,
            start=position,
            rows=back_first[2].shape[0] if i < 2 else back_rest[2].shape[0],
            so_far=so_far,
            **more,
        )

    half = DOC_LEN // 2
    back0 = attn_chunk(0, grads_first, 0, after=[mid_rest.sum])
    step = [back0[6]]
    up.add(step)
    up.start()
    back1 = attn_chunk(1, grads_first, half, back0[4:6], after=[up.total, back0[6]])
    first_done = [back1[6]]
    up.add(first_done)
    up.start()
    down.add([up.total])
    down.start()
    grads_rest = mid_rest.far([down.total])
    in_first = MpSum(back1[4], back1[5])
    back2 = attn_chunk(2, grads_rest, 0, after=[up.total, down.total, back1[6]])
    step = [back2[6]]
    up.add(step)
    up.start()
    down.add([up.total])
    down.start()
    in_first.near([down.total])
    back3 = attn_chunk(
        3,
        grads_rest,
        half,
        back2[4:6],
        after=[up.total, down.total, in_first.sum, back2[6]],
        pieces=pieces,
        earlier=[[b[n] for b in (back0, back1, back2)] for n in (1, 2, 3, 0)],
        normed=[attn[n][0] for n in order],
        ctx=[attn[n][5] for n in order],
    )
    ends = [back3[6]]
    gain_rows = back0[7] + back1[7] + back2[7] + back3[7]
    diag = back0[6] + back1[6] + back2[6] + back3[6]
    small = jnp.concatenate([gain_rows[:2], final_gain[:1], jnp.zeros((5, width), F32)], axis=0)
    small = jnp.concatenate([small, diag], axis=1)
    heads_sum = dp_sum(*back3[8:10])
    heads_sum.start()
    small_x = swap(small, "dp", 1)
    in_rest = MpSum(back3[4], back3[5])
    up.add(ends)
    up.start()
    step = [down.add([up.total])]
    down.start()
    step = [heads_sum.add(step)]
    heads_sum.start()
    small = small + once(small_x, step)
    arrived = swap(small, "dp", 2)
    step = [up.add([small])]
    up.start()
    input_first = in_first.far(step)
    step = [down.add([input_first[0]])]
    down.start()
    step = [in_rest.near(step)]
    step = [heads_sum.add(step)]
    heads_sum.start()
    small = small + once(arrived, step)
    arrived = swap(small, "dp", 4)
    across = (width, units)

    def landed(pack, step):
        return (pack.total, once(pack.arrived, step) if dp_sum is DpSum else pack.arrived)

    step = [down.add([small])]
    down.start()
    up_grads = unpack(place, pieces, landed(up, step), cut_lanes, [across, across])
    step = [heads_sum.add([up_grads[2]])]
    heads_sum.start()
    small = small + once(arrived, step)
    step = [heads_sum.add([small])]
    heads_sum.start()
    distance = 8
    while distance < dp_count:
        small = small + swap(small, "dp", distance)
        distance *= 2
    over_mp = jnp.concatenate([small[:, :width], scalars], axis=1)
    over_mp = over_mp + swap(over_mp, "mp", 1)
    input_rest = in_rest.far([over_mp])
    down_grads = unpack(
        place,
        pieces,
        landed(down, [input_rest[0]]),
        cut_lanes,
        [(units, width), (width, emb_width)],
        across,
    )
    step = [heads_sum.add([down_grads[2]])]
    heads_sum.start()
    over_mp = over_mp + swap(once(over_mp, step), "mp", 2)
    tokens_grad, query_tokens_grad = tail(
        [chunks[n][1:] for n in order],
        place,
        doc_tokens,
        query_tokens,
        [b[0] for b in (back0, back1, back2, back3)],
        input_first,
        input_rest,
        gain_attn,
        step,
    )
    own_gain = over_mp[:, :width]
    scalars = over_mp[:, width:]
    diag = small[:, width:]
    cols = w_query.shape[0]
    attn_pack = landed(heads_sum, [])
    attn_grads = unpack(place, pieces, attn_pack, cut_rows, [(cols, width)] * 4)

    lane = jnp.arange(WIDE, dtype=jnp.int32)
    offset = jnp.where(lane < DOC_LEN, -lane, WIDE - lane)
    distance = jnp.abs(offset)
    far = 8 + sum(((distance >= edge).astype(jnp.int32) for edge in EDGES))
    index = jnp.where(distance < 8, distance, far) + 16 * (offset > 0).astype(jnp.int32)
    onehot = (jnp.arange(bias_table.shape[0], dtype=jnp.int32)[:, None] == index[None]).astype(F32)
    grad_bias = lax.dot_general(
        onehot, diag[: bias_table.shape[1]], (((1,), (1,)), ((), ())), precision=HIGH
    )
    return (
        scalars[0, 0],
        scalars[1, 0],
        emb,
        tokens_grad,
        query_tokens_grad,
        attn_grads[0].T,
        attn_grads[1].T,
        attn_grads[2].T,
        attn_grads[3],
        up_grads[0],
        up_grads[1],
        down_grads[0],
        down_grads[1],
        own_gain[0],
        small[1, :width],
        small[2, :width],
        grad_bias,
    )


def solution(mesh):
    placed = (
        P("dp", None),
        P("dp", None),
        P(None, "mp"),
        P(None, "mp"),
        P(None, "mp"),
        P("mp", None),
        P(None, "mp"),
        P(None, "mp"),
        P("mp", None),
        P(),
        P(),
        P(),
        P(),
        P(None, "mp"),
        P(),
        P(None, None, "dp"),
        P(),
    )
    return jax.shard_map(
        on_device,
        mesh=mesh,
        in_specs=placed,
        out_specs=(
            P(),
            P(),
            P("dp", None),
            P("dp", None),
            P("dp", None),
            P(None, "mp"),
            P(None, "mp"),
            P(None, "mp"),
            P("mp", None),
            P(None, "mp"),
            P(None, "mp"),
            P("mp", None),
            P(),
            P(),
            P(),
            P(),
            P(None, "mp"),
        ),
        check_vma=False,
    )
```

```python
import functools
import math

import jax
import jax.numpy as jnp
from jax import lax
from jax.experimental import pallas as pl
from jax.experimental.pallas import tpu as pltpu
from jax.sharding import PartitionSpec as P

DOC_LEN = 512
EPS = 1e-06
DOC_TEMP = 32.0
EDGES = (12, 16, 23, 32, 46, 64, 91)
HIGH = lax.Precision.HIGHEST
MASKED = -1000000000.0
BF = jnp.bfloat16
F32 = jnp.float32
WIDE = 2 * DOC_LEN
GELU_A = math.sqrt(2.0 / math.pi)
GELU_B = 0.044715


def nn(a, b):
    return jnp.dot(a, b, preferred_element_type=F32)


def nt(a, b):
    return lax.dot_general(a, b, (((1,), (1,)), ((), ())), preferred_element_type=F32)


def tn(a, b):
    return lax.dot_general(a, b, (((0,), (0,)), ((), ())), preferred_element_type=F32)


def rinv(v):
    return lax.rsqrt(jnp.mean(v * v, axis=-1, keepdims=True) + EPS)


def norm_back(v, r, gain, grad):
    scaled = grad * gain
    return r * scaled - v * (r * r * r * jnp.mean(scaled * v, axis=-1, keepdims=True))


def rowsum8(v):
    return jnp.broadcast_to(jnp.sum(v, axis=0, keepdims=True), (8, v.shape[1]))


def halves(place, half):
    mine = pl.multiple_of(place[1] * half, half)
    other = pl.multiple_of((1 - place[1]) * half, half)
    return (mine, other)


class Load:
    def __init__(self, start=0, rows=None, pinned=True):
        self.start = start
        self.rows = rows
        self.pinned = pinned

    def shape(self, operand):
        return operand.shape if self.rows is None else (self.rows,) + operand.shape[1:]

    def of(self, ref):
        return ref if self.rows is None else ref.at[pl.ds(self.start, self.rows)]


class Held:
    def __init__(self, ref, copy):
        self.ref = ref
        self.copy = copy
        self.begun = False

    @property
    def shape(self):
        return self.ref.shape

    @property
    def dtype(self):
        return self.ref.dtype


class Operand(Held):
    def ready(self):
        if not self.begun:
            self.begun = True
            self.copy.wait()
        return self.ref

    def __getitem__(self, at):
        return self.ready()[at]


class Result(Held):
    def __getitem__(self, at):
        return self.ref[at]

    def __setitem__(self, at, value):
        self.ref[at] = value

    def done(self):
        if not self.begun:
            self.begun = True
            self.copy.start()


class Rows:
    def __init__(self, first, second):
        self.parts = (first, second)
        self.shape = (2 * first.shape[0],) + first.shape[1:]

    def __getitem__(self, at):
        half = self.shape[0] // 2
        return self.parts[at.start // half][...]


def halved(length):
    return [Load(0, length // 2), Load(length // 2, length // 2)]


LOAD = Load()
PASS = Load(pinned=False)
SMEM = pl.BlockSpec(memory_space=pltpu.SMEM)
FAR = pl.BlockSpec(memory_space=pltpu.HBM)


def sds(shape, dtype):
    return jax.ShapeDtypeStruct(shape, dtype)


class Kept:
    def __init__(self, shape, dtype):
        self.shape = shape
        self.dtype = dtype


def kept(shape, dtype):
    return Kept(shape, dtype)


def call(body, name, outs, in_specs, micros, scratch=(), into=None, after=(), order=()):
    count = len(outs)
    stores = [LOAD] * count
    out_shape = list(outs)
    begun = []
    for k, (whole, start, so_far) in (into or {}).items():
        out_shape[k] = whole
        stores[k] = Load(start, outs[k].shape[0])
        if so_far is not None:
            begun.append((k, so_far))
    after = [so_far for _, so_far in begun] + list(after)

    def run(*operands):
        pinned = [
            pltpu.with_memory_space_constraint(operand, pltpu.HBM) if isinstance(spec, Load) and spec.pinned else operand
            for spec, operand in zip(in_specs, operands)
        ]
        loads = [n for n, spec in enumerate(in_specs) if isinstance(spec, Load)]
        total = len(loads)
        given = len(operands)
        buffers = [
            pltpu.VMEM(in_specs[n].shape(operands[n]), operands[n].dtype) for n in loads
        ] + [pltpu.VMEM(out.shape, out.dtype) for out in outs]

        def kernel(*refs):
            ins = list(refs[:given])
            results = refs[given + len(after) : given + len(after) + count]
            rest = refs[given + len(after) + count :]
            own, held, sems = rest[: len(scratch)], rest[len(scratch) : -1], rest[-1]
            for n in sorted(loads, key=lambda n: order.index(n) if n in order else given + n):
                k = loads.index(n)
                copy = pltpu.make_async_copy(in_specs[n].of(ins[n]), held[k], sems.at[k])
                copy.start()
                ins[n] = Operand(held[k], copy)
            made = []
            for k, result in enumerate(results):
                buffer = held[total + k]
                copy = pltpu.make_async_copy(buffer, stores[k].of(result), sems.at[total + k])
                made.append(Result(buffer, copy))
            body(*ins, *made, *own)
            for n in loads:
                ins[n].ready()
            for result in made:
                result.done()
            for result in made:
                result.copy.wait()

        return pl.pallas_call(
            kernel,
            name=name,
            out_shape=tuple(
                pltpu.HBM(out.shape, out.dtype) if isinstance(out, Kept) else out for out in out_shape
            ),
            in_specs=[FAR if isinstance(spec, Load) else spec for spec in in_specs]
            + [FAR] * len(after),
            out_specs=(FAR,) * count,
            scratch_shapes=list(scratch) + buffers + [pltpu.SemaphoreType.DMA((total + count,))],
            input_output_aliases={given + n: k for n, (k, _) in enumerate(begun)},
            compiler_params=pltpu.CompilerParams(vmem_limit_bytes=48 * 1024 * 1024),
            cost_estimate=pl.CostEstimate(
                flops=int(micros * 6e8), bytes_accessed=int(micros * 1e5), transcendentals=0
            ),
        )(*pinned, *after)

    return run


def bias_into(table, out):
    lane = lax.broadcasted_iota(jnp.int32, (8, WIDE), 1)
    offset = jnp.where(lane < DOC_LEN, -lane, WIDE - lane)
    distance = jnp.abs(offset)
    far = jnp.full_like(distance, 8)
    for edge in EDGES:
        far = far + (distance >= edge).astype(jnp.int32)
    index = jnp.where(distance < 8, distance, far) + jnp.where(offset > 0, 16, 0)
    for head in range(out.shape[0]):
        row = jnp.zeros((8, WIDE), F32)
        for bucket in range(table.shape[1]):
            row = jnp.where(index == bucket, table[head, bucket], row)
        spread = jnp.broadcast_to(row[:1], (DOC_LEN, WIDE))
        rolled = pltpu.roll(spread, 0, 1, stride=1, stride_axis=0)
        out[head] = rolled[:, :DOC_LEN]


def attn_fwd_body(length, masked, heads, *refs):
    place, x, gain, wq, wk, wv, wo, bias = refs[:8]
    pos = 8
    if masked:
        table, bias, refs = bias, refs[-2], refs[:-2] + refs[-1:]
        bias_into(table, bias)
        bias.done()
    keep_col = None
    if masked:
        keep_col = refs[8]
        pos = 9
    normed_o, q_o, k_o, v_o, lse_o, ctx_o, keep_o, send_o, part_s = refs[pos:]
    half = length // 2
    xf = x[...].astype(F32)
    normed = (xf * rinv(xf) * gain[...]).astype(BF)
    normed_o[...] = normed
    normed_o.done()
    q = nt(normed, wq[...]).astype(BF)
    k = nt(normed, wk[...]).astype(BF)
    v = nt(normed, wv[...]).astype(BF)
    q_o[...] = q
    k_o[...] = k
    v_o[...] = v
    for result in (q_o, k_o, v_o):
        result.done()
    width = q.shape[1] // heads
    vt = v.T
    tile = min(length, 256)
    lse_o[...] = jnp.zeros(lse_o.shape, F32)
    for h in range(heads):
        cols = slice(h * width, (h + 1) * width)
        for start in range(0, length, tile):
            span = slice(start, start + tile)
            logits = nt(k[:, cols], q[span, cols]) + bias[h, :length, span]
            if masked:
                logits = jnp.where(query_mask_of(keep_col, length), logits, MASKED)
            top = jnp.max(logits, axis=0, keepdims=True)
            shifted = jnp.exp(logits - top)
            total = jnp.sum(shifted, axis=0, keepdims=True)
            probs = (shifted * (1.0 / total)).astype(BF)
            ctx_t = nn(vt[cols], probs)
            ctx_o[span, cols] = ctx_t.T.astype(BF)
            lse_o[h : h + 1, span] = top + jnp.log(total)
    ctx_o.done()
    lse_o.done()
    part_s[...] = nn(ctx_o[...], wo[...]).astype(BF)
    mine, other = halves(place, half)
    keep_o[...] = part_s[pl.ds(mine, half)]
    send_o[...] = part_s[pl.ds(other, half)]


def query_mask_of(keep_col, length):
    key_row = lax.broadcasted_iota(jnp.int32, (length, length), 0)
    query_row = lax.broadcasted_iota(jnp.int32, (length, length), 1)
    return ((key_row // 32) == (query_row // 32)) & (keep_col[...] > 0)


def attn_fwd(chunk, place, tokens, gain, wq, wk, wv, wo, bias, keep_col, after):
    index, length, masked = chunk
    heads = bias.shape[0]
    cols = wq.shape[0]
    width = tokens.shape[1]
    specs = [SMEM, Load(index * length, length), PASS] + [LOAD] * 4 + [SMEM if masked else LOAD]
    operands = [place, tokens, gain, wq, wk, wv, wo, bias]
    if masked:
        specs.append(PASS)
        operands.append(keep_col)
    small = kept((length, cols), BF)
    part = sds((length // 2, width), BF)
    return call(
        functools.partial(attn_fwd_body, length, masked, heads),
        "attn_fwd",
        (kept((length, width), BF), small, small, small, kept((8, length), F32), small, part, part)
        + ((kept((heads, DOC_LEN, DOC_LEN), F32),) if masked else ()),
        specs,
        0.012 * length,
        [pltpu.VMEM((length, width), BF)],
        after=after,
    )(*operands)


def gelu_parts(gate):
    t = jnp.tanh(GELU_A * (gate + GELU_B * gate * gate * gate))
    return 0.5 * gate * (1.0 + t), t


def ffn_fwd_body(length, place, x, um, uo, gain, wg, wu, wd, middle_o, normed_o, keep_o, send_o):
    half = length // 2
    bases = halves(place, half)
    for n, (u, out) in enumerate(((um, keep_o), (uo, send_o))):
        middle = x[pl.ds(bases[n], half)].astype(F32) + u[...].astype(F32)
        middle_o[n * half : (n + 1) * half] = middle
        normed = (middle * rinv(middle) * gain[...]).astype(BF)
        normed_o[n * half : (n + 1) * half] = normed
        if n == 1:
            middle_o.done()
            normed_o.done()
        act, _ = gelu_parts(nn(normed, wg[...]))
        hidden = (act * nn(normed, wu[...])).astype(BF)
        out[...] = nn(hidden, wd[...]).astype(BF)


def ffn_fwd(chunk, place, tokens, um, uo, gain, wg, wu, wd, after):
    index, length, _ = chunk
    width = tokens.shape[1]
    part = sds((length // 2, width), BF)
    return call(
        functools.partial(ffn_fwd_body, length),
        "ffn_fwd",
        (kept((length, width), F32), kept((length, width), BF), part, part),
        [SMEM, Load(index * length, length)] + [PASS] * 3 + [LOAD] * 3,
        0.01 * length,
        after=after,
        order=(4, 2, 1, 5, 6, 7, 3),
    )(place, tokens, um, uo, gain, wg, wu, wd)


def embed_rows(length, place, middle, fs, gain, wp, emb_s, out_o):
    half = length // 2
    bases = halves(place, half)
    for n in range(2):
        span = slice(n * half, (n + 1) * half)
        out = middle[span] + fs[n][...].astype(F32)
        out_o[span] = out
        if n == 1:
            out_o.done()
        normed = (out * rinv(out) * gain[...]).astype(BF)
        emb_s[pl.ds(bases[n], half)] = nn(normed, wp[...]).astype(BF)


def query_embed_body(length, lane, place, middle, fm, fo, gain, wp, lane_o, out_o, emb_s):
    embed_rows(length, place, middle, (fm, fo), gain, wp, emb_s, out_o)
    lane_o[...] = emb_s[pl.ds(pl.multiple_of(place[0] * lane, lane), lane)]


def query_embed(place, middle, fm, fo, gain, wp, lane, after):
    length = middle.shape[0]
    emb = wp.shape[1]
    return call(
        functools.partial(query_embed_body, length, lane),
        "query_embed",
        (sds((lane, emb), BF), kept(middle.shape, F32)),
        [SMEM, LOAD] + [PASS] * 3 + [LOAD],
        0.004 * length,
        [pltpu.VMEM((length, emb), BF)],
        after=after,
    )(place, middle, fm, fo, gain, wp)


def lane_tile(tokens):
    return min(tokens, 512)


def doc_embed_body(length, place, upper, lower, fm, fo, gain, wp, queries, emb_o, lse_o, out_o):
    middle = Rows(upper, lower)
    embed_rows(length, place, middle, (fm, fo), gain, wp, emb_o, out_o)
    emb_o.done()
    scale = wp.shape[1] ** (-0.5)
    tile = lane_tile(queries.shape[0])
    for start in range(0, queries.shape[0], tile):
        span = slice(start, start + tile)
        scores = nt(emb_o[...], queries[span]) * scale
        top = jnp.max(scores, axis=0, keepdims=True)
        total = jnp.sum(jnp.exp(scores - top), axis=0, keepdims=True)
        lse_o[:, span] = jnp.broadcast_to(top + jnp.log(total), (8, tile))


def doc_embed(index, place, middle, fm, fo, gain, wp, queries, so_far, docs, after):
    length = middle.shape[0]
    emb = wp.shape[1]
    return call(
        functools.partial(doc_embed_body, length),
        "doc_embed",
        (kept((length, emb), BF), sds((8, queries.shape[0]), F32), kept(middle.shape, F32)),
        [SMEM, *halved(length)] + [PASS] * 3 + [LOAD, PASS],
        0.005 * length,
        into={0: (kept((docs * length, emb), BF), index * length, so_far)},
        order=(5, 3, 1, 6, 4, 2, 7),
        after=after,
    )(place, middle, middle, fm, fo, gain, wp, queries)


def segment(tokens, lanes):
    token = lax.broadcasted_iota(jnp.int32, (tokens, lanes), 0) // 32
    return (token == lax.broadcasted_iota(jnp.int32, (tokens, lanes), 1)).astype(F32)


def stats_body(docs, doc_len, *refs):
    lses = refs[:docs]
    weights, hot, out = refs[docs:]
    lanes = hot.shape[1]
    tokens = weights.shape[1]
    seg = segment(tokens, lanes)
    w = weights[...]
    rows = lax.broadcasted_iota(jnp.int32, (8, tokens), 0)
    scores = jnp.zeros((8, tokens), F32)
    for p in range(docs):
        scores = jnp.where(rows == p, lses[p][...], scores)
    scores = w * (scores - jnp.where(rows < docs, math.log(doc_len), 0.0))
    table = DOC_TEMP * jnp.dot(scores, seg, precision=HIGH, preferred_element_type=F32)
    share = jnp.dot(w, seg, precision=HIGH, preferred_element_type=F32)
    lane_rows = lax.broadcasted_iota(jnp.int32, (8, lanes), 0)
    positive = jnp.sum(table * hot[...], axis=0, keepdims=True)
    share = jnp.sum(share * hot[...], axis=0, keepdims=True)
    result = jnp.where(lane_rows < docs, table, 0.0)
    result = jnp.where(lane_rows == docs, positive, result)
    out[...] = jnp.where(lane_rows == docs + 1, share, result)


def stats(lses, weights, hot, doc_len):
    return call(
        functools.partial(stats_body, len(lses), doc_len),
        "doc_stats",
        (sds(hot.shape, F32),),
        [PASS] * (len(lses) + 2),
        0.5,
    )(*lses, weights, hot)[0]


def score_back_body(docs, doc_len, lane_total, query_total, *refs):
    place, gathered, own, weights, hot, emb, queries = refs[:7]
    lses = refs[7 : 7 + docs]
    keep_o, send_o, query_o, scalars_o, doc_s, query_s = refs[7 + docs :]
    lanes = hot.shape[1]
    tokens = weights.shape[1]
    everything = gathered[...]
    rows = lax.broadcasted_iota(jnp.int32, everything.shape, 1)
    scores = jnp.where(rows < docs, everything, -jnp.inf)
    top = jnp.max(jnp.max(scores, axis=0), axis=0, keepdims=True)
    total = jnp.sum(jnp.sum(jnp.exp(scores - top[None]), axis=0), axis=0, keepdims=True)
    log_norm = top + jnp.log(total)
    summed = jnp.sum(everything, axis=0)
    valid = lax.broadcasted_iota(jnp.int32, (1, lanes), 1) < lane_total
    loss = jnp.where(valid, log_norm - summed[docs : docs + 1], 0.0)
    share = jnp.where(valid, summed[docs + 1 : docs + 2], 0.0)
    out_rows = lax.broadcasted_iota(jnp.int32, (8, 128), 0)
    loss = jnp.sum(loss, axis=1, keepdims=True) / query_total
    share = jnp.sum(share, axis=1, keepdims=True) / query_total
    scalars_o[...] = jnp.where(out_rows == 0, loss, share)
    own_rows = lax.broadcasted_iota(jnp.int32, own.shape, 0)
    grads = DOC_TEMP * (jnp.exp(own[...] - log_norm) - hot[...]) / query_total
    grads = jnp.where(own_rows < docs, grads, 0.0)
    seg = segment(tokens, lanes)
    spread = lax.dot_general(
        grads, seg, (((1,), (1,)), ((), ())), precision=HIGH, preferred_element_type=F32
    )
    token_grad = spread * weights[...]
    emb_width = queries.shape[1]
    scale = emb_width ** (-0.5)
    half = doc_len // 2
    bases = halves(place, half)
    tile = lane_tile(tokens)
    for start in range(0, tokens, tile):
        span = slice(start, start + tile)
        query = queries[span]
        query_grad = jnp.zeros((emb_width, tile), F32)
        for p in range(docs):
            doc = emb[p * doc_len : (p + 1) * doc_len]
            scores = nt(doc, query) * scale
            grad = (token_grad[p : p + 1, span] * jnp.exp(scores - lses[p][:1, span])).astype(BF)
            part = nn(grad, query) * scale
            if start == 0:
                doc_s[p * doc_len : (p + 1) * doc_len] = part
            else:
                doc_s[p * doc_len : (p + 1) * doc_len] += part
            query_grad = query_grad + nn(doc.T, grad)
        query_o[span] = (query_grad * scale).T.astype(BF)
    for p in range(docs):
        keep_o[p * half : (p + 1) * half] = doc_s[pl.ds(p * doc_len + bases[0], half)].astype(BF)
        send_o[p * half : (p + 1) * half] = doc_s[pl.ds(p * doc_len + bases[1], half)].astype(BF)


def score_back(place, gathered, own, weights, hot, emb, queries, lses, doc_len, lane_total, query_total):
    docs = len(lses)
    width = emb.shape[1]
    part = sds((docs * doc_len // 2, width), BF)
    return call(
        functools.partial(score_back_body, docs, doc_len, lane_total, query_total),
        "score_back",
        (part, part, sds(queries.shape, BF), sds((8, 128), F32)),
        [SMEM] + [PASS] * 4 + [LOAD] + [PASS] * (1 + docs),
        3.0,
        [pltpu.VMEM((docs * doc_len, width), F32), pltpu.VMEM((8, 128), F32)],
    )(place, gathered, own, weights, hot, emb, queries, *lses)


def query_sum_body(parts, out):
    out[...] = jnp.sum(parts[...].astype(F32), axis=0).astype(BF)


def query_sum(parts, after):
    return call(
        query_sum_body, "query_sum", (sds(parts.shape[1:], BF),), [PASS], 1.5, after=after
    )(parts)[0]


def ffn_bwd_body(lengths, masked, pieces, early, *refs):
    refs = list(refs)
    count = len(lengths)

    def take(number):
        taken = refs[:number]
        del refs[:number]
        return taken

    (place,) = take(1)
    finals, normeds = [Rows(*take(2)) for _ in range(count)], take(count)
    doc_mine, doc_other = take(2)
    query_grads = take(4 if masked else 0)
    gain_final, wp, wg, wu, wd = take(5)
    early_normeds, early_fgrads = take(early), take(early)
    early_inner, early_sums = (take(3), take(2)) if early else ((), ())
    fgrads = take(count)
    keep_o, send_o, gain_o = take(3)
    if early:
        packs = take(4)
        emb_s, hidden, ggrad, ugrad, up_s, down_s = refs
    else:
        hidden, ggrad, ugrad, proj_o = refs
    width = finals[0].shape[1]
    units = hidden.shape[1]
    gain_sum = jnp.zeros((1, width), F32)
    proj = jnp.zeros((wp.shape[1], width), F32)
    at = 0
    for c, length in enumerate(lengths):
        half = length // 2
        bases = halves(place, half)
        if masked and c == count - 1:
            lane = query_grads[0].shape[0]
            for step, grad in enumerate(query_grads):
                emb_s[pl.ds(pl.multiple_of((place[0] ^ step) * lane, lane), lane)] = grad[...]
            egs = [emb_s[pl.ds(base, half)] for base in bases]
        else:
            egs = [grad[c * half : (c + 1) * half] for grad in (doc_mine, doc_other)]
        for n, out in enumerate((keep_o, send_o)):
            span = slice(n * half, (n + 1) * half)
            rows = slice(at + n * half, at + (n + 1) * half)
            output = finals[c][span]
            r = rinv(output)
            dn = nt(egs[n], wp[...])
            unit = output * r
            gain_sum = gain_sum + jnp.sum(dn * unit, axis=0, keepdims=True)
            proj = proj + nn(egs[n].T, (unit * gain_final[...]).astype(BF))
            fgrad = norm_back(output, r, gain_final[...], dn).astype(BF)
            fgrads[c][span] = fgrad
            if n == 1:
                fgrads[c].done()
            gate = nn(normeds[c][span], wg[...])
            up = nn(normeds[c][span], wu[...])
            act, t = gelu_parts(gate)
            hidden[rows] = (act * up).astype(BF)
            hgrad = nt(fgrad, wd[...])
            slope = 0.5 * (1.0 + t) + 0.5 * gate * (1.0 - t * t) * (
                GELU_A * (1.0 + 3.0 * GELU_B * gate * gate)
            )
            gg = (hgrad * up * slope).astype(BF)
            ug = (hgrad * act).astype(BF)
            ggrad[rows] = gg
            ugrad[rows] = ug
            out[at // 2 : at // 2 + half] = (nt(gg, wg[...]) + nt(ug, wu[...])).astype(BF)
        at += length
    send_o.done()
    keep_o.done()
    if not early:
        gain_o[...] = jnp.broadcast_to(gain_sum, gain_o.shape)
        proj_o[...] = proj
        return
    gain_o[...] = jnp.broadcast_to(gain_sum, gain_o.shape) + early_sums[0][...]
    proj = proj + early_sums[1][...]

    def total(lefts, own, earlier, span):
        result = 0.0
        at = 0
        for c, left in enumerate(lefts):
            if c == early:
                at = 0
            right = earlier if c < early else own
            rows = slice(at, at + left.shape[0])
            result = result + tn(left[:, span], right[rows])
            at += left.shape[0]
        return result.astype(BF)

    rows = width // pieces
    lefts = early_normeds + normeds
    blocks = ((up_s, 0, lefts, early_inner[1], ggrad), (up_s, 1, lefts, early_inner[2], ugrad))
    blocks += ((down_s, 0, early_fgrads + fgrads, early_inner[0], hidden),)
    for out, k, left, earlier, own in blocks:
        lanes = slice(k * units, (k + 1) * units)
        for start in range(0, width, 4 * rows):
            value = total(left, own, earlier, slice(start, start + 4 * rows))
            relative_store(out, value, place[2], pieces, rows, start // rows, lanes)
        if k == 1:
            split_out(up_s, *packs[:2])
            packs[1].done()
            packs[0].done()
    lanes = slice(units, down_s.shape[1])
    relative_store(down_s, proj.T.astype(BF), place[2], pieces, rows, 0, lanes)
    split_out(down_s, *packs[2:])


def ffn_bwd(
    lengths, pieces, place, finals, normeds, doc_grads, doc_at, query_grads, gain, wp, wg, wu, wd,
    early=(), after=(),
):
    masked = len(query_grads) > 0
    count = len(lengths)
    docs = count - 1 if masked else count
    width = finals[0].shape[1]
    emb = wp.shape[1]
    units = wg.shape[1]
    rows = sum(lengths)
    part = sds((rows // 2, width), BF)
    outs = tuple(kept((length, width), BF) for length in lengths)
    outs += (part, part, sds((8, width), F32))
    doc_rows = sum(lengths[:docs]) // 2
    grads = Load(doc_at, doc_rows, pinned=False)
    specs = [SMEM] + [spec for length in lengths for spec in halved(length)] + [LOAD] * count
    specs += [grads] * 2 + [PASS] * len(query_grads)
    specs += [PASS] + [LOAD] * 4
    extra = []
    first = 1 + 3 * count
    gates = first + 2 + len(query_grads)
    order = [gates, first, first + 1, gates + 1, 1, 1 + 2 * count, gates + 2, gates + 3]
    order += [gates + 4, 2]
    if early:
        number = len(early[0])
        extra = [*early[0], *early[1], *early[2], *early[3]]
        specs += [LOAD] * (2 * number + 3) + [PASS] * 2
        base = gates + 5
        order += list(range(3, first)) + list(range(base, base + number))
        order += [base + 2 * number + k for k in (1, 2, 0)]
        up = sds((width // 2, 2 * units), BF)
        down = sds((width // 2, units + emb), BF)
        outs += (up, up, down, down)
        inner = pltpu.VMEM((rows, units), BF)
        scratch = [
            pltpu.VMEM((lengths[-1], emb), BF),
            inner,
            inner,
            inner,
            pltpu.VMEM((width, 2 * units), BF),
            pltpu.VMEM((width, units + emb), BF),
        ]
    else:
        outs += (kept((rows, units), BF),) * 3 + (sds((emb, width), F32),)
        scratch = []
    return call(
        functools.partial(
            ffn_bwd_body, lengths, masked, pieces, len(early[0]) if early else 0
        ),
        "ffn_bwd",
        outs,
        specs,
        14.0,
        scratch,
        order=order,
        after=after,
    )(
        place,
        *[array for array in finals for _ in range(2)],
        *normeds,
        *doc_grads,
        *query_grads,
        gain,
        wp,
        wg,
        wu,
        wd,
        *extra,
    )


def relative_store(out, value, base, pieces, rows, first, lanes):
    for n in range(value.shape[0] // rows):
        slot = reversed_bits(first + n, pieces) ^ base
        out[pl.ds(pl.multiple_of(slot * rows, rows), rows), lanes] = value[n * rows : (n + 1) * rows]


def reversed_bits(number, count):
    result = 0
    while count > 1:
        result = result * 2 + number % 2
        number //= 2
        count //= 2
    return result


def split_out(out, keep_o, send_o):
    half = out.shape[0] // 2
    keep_o[...] = out[:half]
    send_o[...] = out[half:]


def unpack_body(pieces, rows, count, cut, results, *refs):
    place = refs[0]
    parts = [part.ready() for part in refs[1 : 1 + count]]
    outs = list(refs[1 + count : 1 + count + results])
    refs[1 + count + results][...] = jnp.zeros((8, 128), F32)
    turned = refs[2 + count + results :]
    if turned:
        outs[0] = turned[0]
    for number in range(pieces):
        slot = reversed_bits(number, pieces) ^ place[2]
        for part, base in zip(parts, (0, pieces // 2)):

            @pl.when((slot >= base) & (slot < base + part.shape[0] // rows))
            def _(part=part, base=base):
                start = pl.multiple_of((slot - base) * rows, rows)
                value = part[pl.ds(start, rows)].astype(F32)
                cut(outs, number * rows, rows, value)

    if turned:
        refs[1 + count][...] = turned[0][...].T


def cut_lanes(outs, at, rows, value):
    lane = 0
    for out in outs:
        out[at : at + rows] = value[:, lane : lane + out.shape[1]]
        lane += out.shape[1]


def cut_rows(outs, at, rows, value):
    n, at = divmod(at, outs[0].shape[0])
    outs[n][at : at + rows] = value


def unpack(place, pieces, parts, cut, shapes, turned=None):
    rows = sum(part.shape[0] for part in parts) // pieces
    return call(
        functools.partial(unpack_body, pieces, rows, len(parts), cut, len(shapes)),
        "unpack",
        tuple(kept(shape, F32) for shape in shapes) + (sds((8, 128), F32),),
        [SMEM] + [PASS] * len(parts),
        2.0,
        [pltpu.VMEM(turned, F32)] if turned else [],
    )(place, *parts)


def diagonal_sums(block):
    length = block.shape[0]
    rows = length
    value = jnp.concatenate([block, jnp.zeros((rows, WIDE - length), F32)], axis=1)
    while rows > 8:
        rows //= 2
        value = value[:rows] + pltpu.roll(value[rows:], WIDE - rows, 1)
    total = value[0:1]
    for s in range(1, 8):
        total = total + pltpu.roll(jnp.broadcast_to(value[s : s + 1], (8, WIDE)), WIDE - s, 1)[:1]
    return total


def attn_bwd_chunk(place, length, masked, heads, ins, shared, outs, sums, base, ctx_s):
    x, mid, gm, go, g_at, fgrad, q, k, v, lse = ins
    bias, gain, wq, wk, wv, wo, keep_col = shared
    agrad_o, dq_o, dk_o, dv_o, keep_o, send_o = outs
    half = length // 2
    bases = halves(place, half)
    for n, g in enumerate((gm, go)):
        rows = pl.ds(bases[n], half)
        middle = mid[n * half : (n + 1) * half]
        r = rinv(middle)
        dn = g[g_at : g_at + half].astype(F32)
        sums["ffn"] = sums["ffn"] + jnp.sum(dn * (middle * r), axis=0, keepdims=True)
        grad = fgrad[n * half : (n + 1) * half].astype(F32) + norm_back(middle, r, gain[...], dn)
        agrad = grad.astype(BF)
        agrad_o[rows] = agrad
        ctx_s[rows] = nt(agrad, wo[...]).astype(BF)
    agrad_o.done()
    width = q.shape[1] // heads
    tile = min(length, 256)
    kt = k[...].T
    for h in range(heads):
        cols = slice(h * width, (h + 1) * width)
        kh = k[:, cols]
        vh = v[:, cols]
        dk = jnp.zeros((length, width), F32)
        dv = jnp.zeros((length, width), F32)
        pieces = []
        for start in range(0, length, tile):
            span = slice(start, start + tile)
            qh = q[span, cols]
            ch = ctx_s[span, cols]
            logits = nt(kh, qh) + bias[h, :length, span]
            if masked:
                logits = jnp.where(query_mask_of(keep_col, length), logits, MASKED)
            probs = jnp.exp(logits - lse[h : h + 1, span])
            pgrad = nt(vh, ch)
            delta = jnp.sum(probs * pgrad, axis=0, keepdims=True)
            lgrad = (probs * (pgrad - delta)).astype(BF)
            dv = dv + nn(probs.astype(BF), ch)
            dk = dk + nn(lgrad, qh)
            dq_o[span, cols] = nn(kt[cols], lgrad).T.astype(BF)
            pieces.append(lgrad)
        dk_o[:, cols] = dk.astype(BF)
        dv_o[:, cols] = dv.astype(BF)
        lgrad = jnp.concatenate(pieces, axis=1) if len(pieces) > 1 else pieces[0]
        sums["diag"][h] = sums["diag"][h] + diagonal_sums(lgrad.astype(F32))
    for result in (dq_o, dk_o, dv_o):
        result.done()
    part = nn(dq_o[...], wq[...]) + nn(dk_o[...], wk[...]) + nn(dv_o[...], wv[...])
    xf = x[...].astype(F32)
    sums["attn"] = sums["attn"] + jnp.sum(part * (xf * rinv(xf)), axis=0, keepdims=True)
    return part.astype(BF)


def attn_bwd_body(group, heads, pieces, weights, *refs):
    refs = list(refs)
    size = len(group)
    others = weights - size if weights else 0

    def take(number):
        taken = refs[:number]
        del refs[:number]
        return taken

    (place,) = take(1)
    x = take(size)
    mid, fgrad = ([Rows(*take(2)) for _ in range(size)] for _ in range(2))
    q, k, v, lse = (take(size) for _ in range(4))
    gm, go, bias, gain, wq, wk, wv, wo, keep_col = take(9)
    earlier = [take(others) for _ in range(4)]
    normed, ctx = take(weights), take(weights)
    agrad, dq, dk, dv = (take(size) for _ in range(4))
    keep_o, send_o, diag_o, gain_o = take(4)
    packs = take(2) if weights else None
    ctx_s, part_s = take(2)
    width = x[0].shape[1]
    sums = {
        "ffn": jnp.zeros((1, width), F32),
        "attn": jnp.zeros((1, width), F32),
        "diag": [jnp.zeros((1, WIDE), F32)] * heads,
    }
    at = 0
    for c, (length, masked) in enumerate(group):
        half = length // 2
        part = attn_bwd_chunk(
            place,
            length,
            masked,
            heads,
            (x[c], mid[c], gm, go, at, fgrad[c], q[c], k[c], v[c], lse[c]),
            (bias, gain, wq, wk, wv, wo, keep_col),
            (agrad[c], dq[c], dk[c], dv[c], keep_o, send_o),
            sums,
            at,
            ctx_s,
        )
        part_s[:length] = part
        bases = halves(place, half)
        keep_o[at : at + half] = part_s[pl.ds(bases[0], half)]
        send_o[at : at + half] = part_s[pl.ds(bases[1], half)]
        at += half
    send_o.done()
    keep_o.done()
    diag_o[...] = jnp.zeros(diag_o.shape, F32)
    for h in range(heads):
        diag_o[h : h + 1] = sums["diag"][h]
    row = lax.broadcasted_iota(jnp.int32, gain_o.shape, 0)
    gain_o[...] = jnp.where(row == 0, sums["attn"], sums["ffn"])
    if weights:
        pack_s = refs[0]
        cols = q[0].shape[1]
        rows = pack_s.shape[0] // pieces
        every = [old + new for old, new in zip(earlier, (dq, dk, dv, agrad))]
        pairs = ((every[0], normed), (every[1], normed), (every[2], normed), (ctx, every[3]))
        for n, (left, right) in enumerate(pairs):
            total = sum(tn(a[...], b[...]) for a, b in zip(left, right)).astype(BF)
            relative_store(pack_s, total, place[2], pieces, rows, n * cols // rows, slice(0, width))
        split_out(pack_s, *packs)


def attn_bwd(
    group, place, xs, mids, fgrads, heads_kept, gs, bias, gain, wq, wk, wv, wo, keep_col,
    pieces=0, earlier=None, normed=(), ctx=(), after=(), start=0, rows=0, so_far=(None, None),
):
    heads = bias.shape[0]
    size = len(group)
    cols = wq.shape[0]
    width = wq.shape[1]
    weights = len(normed)
    others = weights - size if weights else 0
    longest = max(length for _, length, _ in group)
    part = sds((sum(length for _, length, _ in group) // 2, width), BF)
    outs = tuple(kept((length, width), BF) for _, length, _ in group)
    outs += tuple(kept((length, cols), BF) for _, length, _ in group) * 3
    outs += (part, part, sds((8, WIDE), F32), sds((8, width), F32))
    scratch = [pltpu.VMEM((longest, cols), BF), pltpu.VMEM((longest, width), BF)]
    if weights:
        outs += (sds((2 * cols, width), BF),) * 2
        scratch.append(pltpu.VMEM((4 * cols, width), BF))
    specs = [SMEM] + [Load(index * length, length) for index, length, _ in group]
    sums = Load(start, part.shape[0], pinned=False)
    specs += [spec for _ in range(2) for _, length, _ in group for spec in halved(length)]
    specs += [LOAD] * (4 * size) + [sums] * 2 + [LOAD, PASS] + [LOAD] * 4 + [PASS]
    specs += [LOAD] * (4 * others + 2 * weights)
    operands = [place, *xs] + [array for array in (*mids, *fgrads) for _ in range(2)]
    operands += [kept_heads[i] for i in range(4) for kept_heads in heads_kept]
    operands += [*gs, bias, gain, wq, wk, wv, wo, keep_col]
    operands += [array for arrays in (earlier or ()) for array in arrays]
    operands += [*normed, *ctx]
    g = 1 + 9 * size
    h = 1 + 5 * size
    order = [g + 3, 1 + size, g, 1 + 3 * size, g + 7, 2 + size, g + 1, 2 + 3 * size]
    order += [h + size, h, h + 2 * size, h + 3 * size, g + 2, g + 4, g + 5, g + 6, 1]
    return call(
        functools.partial(
            attn_bwd_body, [(length, masked) for _, length, masked in group], heads, pieces, weights
        ),
        "attn_bwd",
        outs,
        specs,
        9.0 * size,
        scratch,
        after=after,
        order=order,
        into={
            4 * size + n: (sds((rows or part.shape[0], width), BF), start, so_far[n]) for n in range(2)
        },
    )(*operands)


def tail_body(group, *refs):
    refs = list(refs)
    size = len(group)

    def take(number):
        taken = refs[:number]
        del refs[:number]
        return taken

    (place, x_doc, x_query), agrad, grads = take(3), take(size), take(4)
    gain, doc_o, query_o = refs
    at = [0, 0]
    for c, (length, masked) in enumerate(group):
        half = length // 2
        bases = halves(place, half)
        pair = 0 if c < 2 else 1
        x, out, base = (x_query, query_o, 0) if masked else (x_doc, doc_o, c * length)
        for n in range(2):
            rows = pl.ds(base + bases[n], half)
            xf = x[rows].astype(F32)
            dn = grads[2 * pair + n][at[pair] : at[pair] + half].astype(F32)
            own = agrad[c][pl.ds(bases[n], half)].astype(F32)
            out[rows] = (own + norm_back(xf, rinv(xf), gain[...], dn)).astype(BF)
        at[pair] += half


def tail(group, place, doc_tokens, query_tokens, agrads, first, rest, gain, after):
    return call(
        functools.partial(tail_body, group),
        "tokens_grad",
        (kept(doc_tokens.shape, BF), kept(query_tokens.shape, BF)),
        [SMEM] + [LOAD] * (2 + len(group)) + [PASS] * 5,
        8.0,
        after=after,
    )(place, doc_tokens, query_tokens, *agrads, *first, *rest, gain)


def swap(block, axis, distance):
    count = lax.axis_size(axis)
    return lax.ppermute(block, axis, [(i, i ^ distance) for i in range(count)])


def added(a, b):
    return (a.astype(F32) + b.astype(F32)).astype(BF)


def once(value, earlier):
    if not earlier:
        return value
    return lax.optimization_barrier((value, *earlier))[0]


class DpSum:
    def __init__(self, keep, send):
        self.keep = keep
        self.send = send
        self.distance = 1
        self.count = lax.axis_size("dp")
        self.total = None

    def start(self, holds=()):
        if self.distance < self.count:
            self.arrived = swap(once(self.send, holds), "dp", self.distance)
        else:
            self.back //= 2
            self.arrived = swap(once(self.total, holds), "dp", self.back)

    def add(self, holds=()):
        if self.distance < self.count:
            self.total = added(self.keep, once(self.arrived, holds))
            self.distance *= 2
            self.back = self.count
            if self.distance < self.count:
                half = self.total.shape[0] // 2
                self.keep, self.send = self.total[:half], self.total[half:]
        else:
            self.total = jnp.concatenate([self.total, once(self.arrived, holds)], axis=0)
        return self.total


class DpWhole:
    def __init__(self, keep, send):
        self.total, self.arrived = lax.psum((keep, send), "dp")

    def start(self, holds=()):
        pass

    def add(self, holds=()):
        return self.total

def dp_gather(block):
    count = lax.axis_size("dp")
    spread = jnp.broadcast_to(block[None], (count,) + block.shape)
    return lax.all_to_all(spread, "dp", 0, 0, tiled=True)


def on_device(
    doc_tokens,
    query_tokens,
    w_query,
    w_key,
    w_value,
    w_out,
    w_gate,
    w_up,
    w_down,
    w_proj,
    gain_attn,
    gain_ffn,
    gain_final,
    bias_table,
    query_mask,
    retrieval_mask,
    positives,
):
    dp_count = lax.axis_size("dp")
    mp_count = lax.axis_size("mp")
    dp_index = lax.axis_index("dp")
    mp_index = lax.axis_index("mp")
    query_len = query_mask.shape[1]
    docs_here = doc_tokens.shape[0] // DOC_LEN
    queries_here = query_tokens.shape[0] // query_len
    query_total = dp_count * queries_here
    width = doc_tokens.shape[1]
    emb_width = w_proj.shape[1]
    units = w_gate.shape[1]
    lane_count = queries_here // mp_count
    lane_total = lane_count * dp_count
    lane_tokens = lane_total * query_len
    lane_pad = -(-lane_total // 128) * 128
    pieces = 8
    order_here = sum(((dp_index >> bit) & 1) << (2 - bit) for bit in range(3))
    if dp_count != pieces:
        order_here = jnp.zeros_like(dp_index)
    place = jnp.stack([mp_index, mp_index % 2, order_here]).astype(jnp.int32)
    w_query = w_query.T
    w_key = w_key.T
    w_value = w_value.T
    gain_attn = gain_attn.reshape(1, width)
    gain_ffn = gain_ffn.reshape(1, width)
    gain_final = gain_final.reshape(1, width)
    home_keep = lax.dynamic_slice_in_dim(query_mask, dp_index * queries_here, queries_here, 0)
    keep_col = home_keep.astype(F32).reshape(-1, 1)

    def lane_view(whole):
        grouped = whole.reshape((dp_count, queries_here) + whole.shape[1:])
        picked = lax.dynamic_slice_in_dim(grouped, mp_index * lane_count, lane_count, 1)
        return picked.reshape((lane_total,) + whole.shape[1:])

    lane_keep = lane_view(query_mask).astype(F32)
    lane_hits = lane_view(retrieval_mask).astype(F32)
    token_weights = lane_keep[:, :, None] * lane_hits / jnp.sum(lane_keep, axis=1)[:, None, None]
    token_weights = token_weights.reshape(lane_tokens, docs_here).T
    token_weights = jnp.pad(token_weights, ((0, 8 - docs_here), (0, 0)))
    doc_ids = dp_index * docs_here + jnp.arange(8, dtype=jnp.int32)
    doc_ids = jnp.where(jnp.arange(8) < docs_here, doc_ids, -1)
    lane_positive = jnp.pad(lane_view(positives), (0, lane_pad - lane_total), constant_values=-2)
    hot = (lane_positive[None, :] == doc_ids[:, None]).astype(F32)

    chunks = [(0, query_tokens.shape[0], True)] + [(p, DOC_LEN, False) for p in range(docs_here)]
    bias = bias_table.T
    sources = [query_tokens] + [doc_tokens] * docs_here
    dp_sum = DpSum if dp_count == pieces else DpWhole

    class MpSum:
        def __init__(self, keep, send):
            self.keep = keep
            self.arrived = swap(send, "mp", 1)

        def near(self, holds=()):
            self.sum = added(self.keep, once(self.arrived, holds))
            self.arrived = swap(self.sum, "mp", 2)
            return self.sum

        def far(self, holds=()):
            total = added(self.sum, once(self.arrived, holds))
            return (total, swap(total, "mp", 1))

    last = len(chunks) - 1
    attn, ffn, attn_sums, ffn_sums, attended = [], [], [], [], []
    for n, (c, t) in enumerate(zip(chunks, sources)):
        after = [a[6] for a in attn[-1:]] + [m.sum for m in attn_sums[-2:-1]]
        a = attn_fwd(
            c, place, t, gain_attn, w_query, w_key, w_value, w_out, bias, keep_col, after
        )
        if n == 0:
            bias = a[8]
        attn.append(a)
        attn_sums.append(MpSum(a[6], a[7]))
        if n >= 1:
            attn_sums[n - 1].near([a[6]])
        if n >= 2:
            attended.append(attn_sums[n - 2].far([a[6]]))
    done, summed = attn[-1][6], attn_sums[-2].sum
    for n, (c, t) in enumerate(zip(chunks, sources)):
        f = ffn_fwd(
            c, place, t, *attended[n], gain_ffn, w_gate, w_up, w_down, [done, summed]
        )
        done = f[2]
        ffn.append(f)
        ffn_sums.append(MpSum(f[2], f[3]))
        summed = (attn_sums[last] if n == 0 else ffn_sums[n - 1]).near([done])
        if len(attended) <= last and n >= 1:
            attended.append(attn_sums[len(attended)].far([done]))
    ffn_sums[last].near()

    lane_block, output = query_embed(
        place,
        ffn[0][0],
        *ffn_sums[0].far([done]),
        gain_final,
        w_proj,
        lane_count * query_len,
        [ffn_sums[last].sum],
    )
    outputs = [output]
    queries = dp_gather(lane_block).reshape(lane_tokens, emb_width)
    emb = None
    lses = []
    done = queries
    sums = [ffn_sums[1].far(), ffn_sums[2].far()]
    for p in range(docs_here):
        if p >= 1 and len(sums) < docs_here:
            sums.append(ffn_sums[len(sums) + 1].far([done]))
        emb, lse, output = doc_embed(
            p,
            place,
            ffn[p + 1][0],
            *sums[p],
            gain_final,
            w_proj,
            queries,
            emb,
            docs_here,
            [sums[p + 1][0]] if p == 0 else [],
        )
        done = lse
        lses.append(lse)
        outputs.append(output)
    own = stats(lses, token_weights, hot, DOC_LEN)
    gathered = dp_gather(own)
    keep, send, query_part, scalars = score_back(
        place, gathered, own, token_weights, hot, emb, queries, lses, DOC_LEN, lane_total, query_total
    )
    doc_sum = MpSum(keep, send)
    query_part = query_part.reshape(dp_count, lane_count * query_len, emb_width)
    query_part = lax.all_to_all(query_part, "dp", 0, 0, tiled=True)
    doc_sum.near()
    doc_grads = doc_sum.far()
    query_here = query_sum(query_part, ())
    query_far = swap(query_here, "mp", 2)
    query_near = swap(query_here, "mp", 1)
    order = list(range(1, docs_here + 1)) + [0]
    count = len(order)
    lengths = [chunks[n][1] for n in order]
    groups = (order[:2], order[2:])
    weights = (gain_final, w_proj, w_gate, w_up, w_down)
    back_first = ffn_bwd(
        lengths[:2],
        pieces,
        place,
        [outputs[n] for n in groups[0]],
        [ffn[n][1] for n in groups[0]],
        doc_grads,
        0,
        [],
        *weights,
        after=[query_far, query_near],
    )
    first_done = [back_first[2]]
    mid_first = MpSum(back_first[2], back_first[3])
    mid_first.near()
    query_far = once(query_far, first_done)
    query_grads = [query_here, query_near, query_far, swap(query_far, "mp", 1)]
    back_rest = ffn_bwd(
        lengths[2:],
        pieces,
        place,
        [outputs[n] for n in groups[1]],
        [ffn[n][1] for n in groups[1]],
        doc_grads,
        DOC_LEN,
        query_grads,
        *weights,
        early=[
            [ffn[n][1] for n in groups[0]],
            back_first[:2],
            back_first[5:8],
            [back_first[4], back_first[8]],
        ],
        after=[mid_first.sum],
    )
    rest_done = [back_rest[2]]
    fgrads = (back_first[:2], back_rest[:2])
    mid_rest = MpSum(back_rest[2], back_rest[3])
    final_gain = back_rest[4]
    up = dp_sum(*back_rest[5:7])
    down = dp_sum(*back_rest[7:9])
    up.start()
    down.start()
    grads_first = mid_first.far(rest_done)
    mid_rest.near(grads_first[:1])

    def attn_chunk(i, grads, position, so_far=(None, None), **more):
        n = order[i]
        return attn_bwd(
            [chunks[n]],
            place,
            [sources[n]],
            [ffn[n][0]],
            [fgrads[i // 2][i % 2]],
            [attn[n][1:5]],
            grads,
            bias,
            gain_ffn,
            w_query,
            w_key,
            w_value,
            w_out,
            keep_col,
            start=position,
            rows=back_first[2].shape[0] if i < 2 else back_rest[2].shape[0],
            so_far=so_far,
            **more,
        )

    half = DOC_LEN // 2
    back0 = attn_chunk(0, grads_first, 0, after=[mid_rest.sum])
    step = [back0[6]]
    up.add(step)
    up.start()
    back1 = attn_chunk(1, grads_first, half, back0[4:6], after=[up.total, back0[6]])
    first_done = [back1[6]]
    up.add(first_done)
    up.start()
    down.add([up.total])
    down.start()
    grads_rest = mid_rest.far([down.total])
    in_first = MpSum(back1[4], back1[5])
    back2 = attn_chunk(2, grads_rest, 0, after=[up.total, down.total, back1[6]])
    step = [back2[6]]
    up.add(step)
    up.start()
    down.add([up.total])
    down.start()
    in_first.near([down.total])
    back3 = attn_chunk(
        3,
        grads_rest,
        half,
        back2[4:6],
        after=[up.total, down.total, in_first.sum, back2[6]],
        pieces=pieces,
        earlier=[[b[n] for b in (back0, back1, back2)] for n in (1, 2, 3, 0)],
        normed=[attn[n][0] for n in order],
        ctx=[attn[n][5] for n in order],
    )
    ends = [back3[6]]
    gain_rows = back0[7] + back1[7] + back2[7] + back3[7]
    diag = back0[6] + back1[6] + back2[6] + back3[6]
    small = jnp.concatenate([gain_rows[:2], final_gain[:1], jnp.zeros((5, width), F32)], axis=0)
    small = jnp.concatenate([small, diag], axis=1)
    heads_sum = dp_sum(*back3[8:10])
    heads_sum.start()
    small_x = swap(small, "dp", 1)
    in_rest = MpSum(back3[4], back3[5])
    up.add(ends)
    up.start()
    step = [down.add([up.total])]
    down.start()
    step = [heads_sum.add(step)]
    heads_sum.start()
    small = small + once(small_x, step)
    arrived = swap(small, "dp", 2)
    step = [up.add([small])]
    up.start()
    input_first = in_first.far(step)
    step = [down.add([input_first[0]])]
    down.start()
    step = [in_rest.near(step)]
    step = [heads_sum.add(step)]
    heads_sum.start()
    small = small + once(arrived, step)
    arrived = swap(small, "dp", 4)
    across = (width, units)

    def landed(pack, step):
        return (pack.total, once(pack.arrived, step) if dp_sum is DpSum else pack.arrived)

    step = [down.add([small])]
    down.start()
    up_grads = unpack(place, pieces, landed(up, step), cut_lanes, [across, across])
    step = [heads_sum.add([up_grads[2]])]
    heads_sum.start()
    small = small + once(arrived, step)
    step = [heads_sum.add([small])]
    heads_sum.start()
    distance = 8
    while distance < dp_count:
        small = small + swap(small, "dp", distance)
        distance *= 2
    over_mp = jnp.concatenate([small[:, :width], scalars], axis=1)
    over_mp = over_mp + swap(over_mp, "mp", 1)
    input_rest = in_rest.far([over_mp])
    down_grads = unpack(
        place,
        pieces,
        landed(down, [input_rest[0]]),
        cut_lanes,
        [(units, width), (width, emb_width)],
        across,
    )
    step = [heads_sum.add([down_grads[2]])]
    heads_sum.start()
    over_mp = over_mp + swap(once(over_mp, step), "mp", 2)
    tokens_grad, query_tokens_grad = tail(
        [chunks[n][1:] for n in order],
        place,
        doc_tokens,
        query_tokens,
        [b[0] for b in (back0, back1, back2, back3)],
        input_first,
        input_rest,
        gain_attn,
        step,
    )
    own_gain = over_mp[:, :width]
    scalars = over_mp[:, width:]
    diag = small[:, width:]
    cols = w_query.shape[0]
    attn_pack = landed(heads_sum, [])
    attn_grads = unpack(place, pieces, attn_pack, cut_rows, [(cols, width)] * 4)

    lane = jnp.arange(WIDE, dtype=jnp.int32)
    offset = jnp.where(lane < DOC_LEN, -lane, WIDE - lane)
    distance = jnp.abs(offset)
    far = 8 + sum(((distance >= edge).astype(jnp.int32) for edge in EDGES))
    index = jnp.where(distance < 8, distance, far) + 16 * (offset > 0).astype(jnp.int32)
    onehot = (jnp.arange(bias_table.shape[0], dtype=jnp.int32)[:, None] == index[None]).astype(F32)
    grad_bias = lax.dot_general(
        onehot, diag[: bias_table.shape[1]], (((1,), (1,)), ((), ())), precision=HIGH
    )
    return (
        scalars[0, 0],
        scalars[1, 0],
        emb,
        tokens_grad,
        query_tokens_grad,
        attn_grads[0].T,
        attn_grads[1].T,
        attn_grads[2].T,
        attn_grads[3],
        up_grads[0],
        up_grads[1],
        down_grads[0],
        down_grads[1],
        own_gain[0],
        small[1, :width],
        small[2, :width],
        grad_bias,
    )


def solution(mesh):
    placed = (
        P("dp", None),
        P("dp", None),
        P(None, "mp"),
        P(None, "mp"),
        P(None, "mp"),
        P("mp", None),
        P(None, "mp"),
        P(None, "mp"),
        P("mp", None),
        P(),
        P(),
        P(),
        P(),
        P(None, "mp"),
        P(),
        P(None, None, "dp"),
        P(),
    )
    return jax.shard_map(
        on_device,
        mesh=mesh,
        in_specs=placed,
        out_specs=(
            P(),
            P(),
            P("dp", None),
            P("dp", None),
            P("dp", None),
            P(None, "mp"),
            P(None, "mp"),
            P(None, "mp"),
            P("mp", None),
            P(None, "mp"),
            P(None, "mp"),
            P("mp", None),
            P(),
            P(),
            P(),
            P(),
            P(None, "mp"),
        ),
        check_vma=False,
    )
```
